32 devices in a mesh: wide: 8 (over y, x, core), tensor: 4 (over z).
Axes of the slice: x: 2, y: 2, z: 4, core: 2. Of those that a mesh axis runs over, the one named last changes fastest.
Arguments:
- pixels: bfloat16 [1, 16, 128, 1024], P(None, 'wide', None, 'tensor'), may hold values from -25 to 25
- text_states: bfloat16 [1, 128, 4096], replicated, may hold values from -6 to 6
- text_length: int32 [1], replicated, may hold values from 17 to 128
- timestep: int32 [1], replicated, may hold values from 0 to 999
- conv_weights: bfloat16 [2, 9, 1024, 1024], P(None, None, 'wide', 'tensor'), may hold values from -0.0625 to 0.0625
- film_time: bfloat16 [1024, 2, 1024], P('wide', None, 'tensor'), may hold values from -0.1875 to 0.1875
- film_text: bfloat16 [4096, 2, 1024], P('wide', None, 'tensor'), may hold values from -0.375 to 0.375
- group_gain: float32 [2, 1024], P(None, 'tensor'), may hold values from 0.25 to 1.75
- group_bias: float32 [2, 1024], P(None, 'tensor'), may hold values from -3 to 3
- layer_gain: float32 [1024], P('tensor'), may hold values from 0.25 to 1.75
- layer_bias: float32 [1024], P('tensor'), may hold values from -3 to 3
- attn_in: bfloat16 [4, 1024, 1024], P(None, 'wide', 'tensor'), may hold values from -0.25 to 0.25
- text_kv: bfloat16 [2, 4096, 1024], P(None, 'wide', 'tensor'), may hold values from -0.125 to 0.125
- out_self: bfloat16 [1024, 1024], P('tensor', 'wide'), may hold values from -3 to 3
- out_cross: bfloat16 [1024, 1024], P('tensor', 'wide'), may hold values from -0.25 to 0.25
- cotangent: float32 [1, 16, 128, 1024], P(None, 'wide', None, 'tensor'), may hold values from -6 to 6
Outputs:
- result: float32 [1, 16, 128, 1024], P(None, 'wide', None, 'tensor')
- pixels_grad: float32 [1, 16, 128, 1024], P(None, 'wide', None, 'tensor')
- conv_grad: float32 [2, 9, 1024, 1024], P(None, None, 'wide', 'tensor')
- film_time_grad: float32 [1024, 2, 1024], P('wide', None, 'tensor')
- film_text_grad: float32 [4096, 2, 1024], P('wide', None, 'tensor')
- group_gain_grad: float32 [2, 1024], P(None, 'tensor')
- group_bias_grad: float32 [2, 1024], P(None, 'tensor')
- layer_gain_grad: float32 [1024], P('tensor')
- layer_bias_grad: float32 [1024], P('tensor')
- attn_in_grad: float32 [4, 1024, 1024], P(None, 'wide', 'tensor')
- text_kv_grad: float32 [2, 4096, 1024], P(None, 'wide', 'tensor')
- out_self_grad: float32 [1024, 1024], P('tensor', 'wide')
- out_cross_grad: float32 [1024, 1024], P('tensor', 'wide')
The draws below stay inside these ranges and needn't reach their ends.
All inputs are finite; a program needn't handle non-finite values.
Results may differ from the reference program's by a relative error of at most 0.02.
Values may be sent and summed in bfloat16 or wider, within the bound.
No kernel may reach another device: no remote copies, remote signals or barrier semaphores. Data moves between devices by JAX's collectives and lax.ppermute only.
A program may use at most 192 MiB of HBM per device.

```python
import math
import jax
import jax.numpy as jnp
from jax import lax

C = 1024
GROUPS = 32
HEADS = 8
HEAD_DIM = 128
TEXT = 128
TEXT_D = 4096
TEMB = 1024
STEPS = 1000
WIDTH = 128
MAPS = 1
HEIGHT = 16


def draw_pixels(key, part):
    key = jax.random.fold_in(key, 11)
    noise_key, offset_key = jax.random.split(key, 2)
    full_shape = (MAPS, HEIGHT, WIDTH, C)
    rising = 1.0 + 2.0 * jnp.arange(HEIGHT, dtype=jnp.float32) / max(HEIGHT - 1, 1)
    offsets = jax.random.uniform(offset_key, (MAPS, 1, 1, C), jnp.float32, -1.0, 1.0)
    noise_values = jax.random.truncated_normal(noise_key, -4.0, 4.0, full_shape, jnp.float32)
    return (noise_values * rising[None, :, None, None] + offsets).astype(jnp.bfloat16)


def shard_levels(key, dims, cuts, low, largest):
    factor_of, own = 1.0, jax.random.fold_in(key, 6)
    for dim, shards_of in cuts:
        steps = jnp.exp(jax.random.uniform(jax.random.fold_in(own, dim), (shards_of,), jnp.float32, low / len(cuts), largest / len(cuts)))
        factor_of = factor_of * jnp.repeat(steps, dims[dim] // shards_of).reshape([-1 if axis == dim else 1 for axis in range(len(dims))])
    return factor_of


def bell_draw(stream_key, extent, width, limit, cuts=(), held_as=jnp.bfloat16):
    values = jax.random.normal(stream_key, extent, jnp.float32) * width
    if len(cuts) > 0:
        values = shard_levels(stream_key, extent, cuts, -0.22, 0.18) * values
    return jnp.clip(values, min=-limit, max=limit).astype(held_as)


def setup_inputs(seed: int = 0) -> dict:
    key_list = jax.random.split(jax.random.key(seed), 17)
    return {
        "pixels": draw_pixels(jax.random.fold_in(key_list[16], 71), 0),
        "text_states": bell_draw(key_list[1], (MAPS, TEXT, TEXT_D), 1.0, 6.0),
        "text_length": jax.random.randint(key_list[2], (MAPS,), TEXT // 8 + 1, TEXT + 1).astype(jnp.int32),
        "timestep": jax.random.randint(key_list[3], (MAPS,), 0, STEPS).astype(jnp.int32),
        "conv_weights": bell_draw(key_list[4], (2, 9, C, C), (9 * C) ** -0.5, 0.0625, ((2, 8), (3, 4))),
        "film_time": bell_draw(key_list[5], (TEMB, 2, C), TEMB ** -0.5, 0.1875, ((0, 8), (2, 4))),
        "film_text": bell_draw(key_list[6], (TEXT_D, 2, C), (TEXT_D // 16) ** -0.5, 0.375, ((0, 8), (2, 4))),
        "group_gain": jnp.clip(1.0 + 0.15 * jax.random.normal(key_list[7], (2, C), jnp.float32), 0.25, 1.75),
        "group_bias": bell_draw(key_list[8], (2, C), 0.5, 3.0, ((1, 4),), jnp.float32),
        "layer_gain": jnp.clip(1.0 + 0.15 * jax.random.normal(key_list[9], (C,), jnp.float32), 0.25, 1.75),
        "layer_bias": bell_draw(key_list[10], (C,), 0.5, 3.0, ((0, 4),), jnp.float32),
        "attn_in": bell_draw(key_list[11], (4, C, C), (C // 2) ** -0.5, 0.25, ((1, 8), (2, 4))),
        "text_kv": bell_draw(key_list[12], (2, TEXT_D, C), (TEXT_D // 2) ** -0.5, 0.125, ((1, 8), (2, 4))),
        "out_self": bell_draw(key_list[13], (C, C), (max(1, C // 256)) ** -0.5, 3.0, ((0, 4), (1, 8))),
        "out_cross": bell_draw(key_list[14], (C, C), (C // 2) ** -0.5, 0.25, ((0, 4), (1, 8))),
        "cotangent": bell_draw(key_list[15], (MAPS, HEIGHT, WIDTH, C), 1.0, 6.0, ((1, 8), (3, 4)), jnp.float32),
    }


@jax.custom_vjp
def low(v):
    return lax.optimization_barrier(v.astype(jnp.bfloat16)).astype(jnp.float32)

@jax.custom_vjp
def low_back(v):
    return v

def low_keep(v):
    return (low(v), None)

def low_pass(kept, grad):
    return (grad,)

def back_keep(v):
    return (v, None)

def back_low(kept, grad):
    return (low(grad),)
low.defvjp(low_keep, low_pass)
low_back.defvjp(back_keep, back_low)
highest = lax.Precision.HIGHEST
root_half = 1.0 / math.sqrt(2.0)

def sinusoid(steps):
    half_width = TEMB // 2
    frequency = jnp.exp(-math.log(10000.0) * jnp.arange(half_width, dtype=jnp.float32) / half_width)
    angles = steps.astype(jnp.float32)[:, None] * frequency[None, :]
    return jnp.concatenate([jnp.cos(angles), jnp.sin(angles)], axis=1)

def pool_text(text_values, text_length):
    present = (jnp.arange(TEXT)[None, :] < text_length[:, None]).astype(jnp.float32)
    summed = jnp.einsum('mtd,mt->md', text_values, present, precision=highest)
    return summed / text_length.astype(jnp.float32)[:, None]

def group_norm(values, gain, bias):
    grouped = values.reshape(values.shape[0], -1, GROUPS, C // GROUPS)
    center = lax.optimization_barrier(jnp.mean(grouped, axis=(1, 3), keepdims=True))
    square = lax.optimization_barrier(jnp.mean(grouped * grouped, axis=(1, 3), keepdims=True))
    scaled = (grouped - center) * lax.rsqrt(square - center * center + 1e-05)
    return scaled.reshape(values.shape) * gain + bias

def layer_norm(values, gain, bias):
    center = lax.optimization_barrier(jnp.mean(values, axis=-1, keepdims=True))
    square = lax.optimization_barrier(jnp.mean(values * values, axis=-1, keepdims=True))
    return (values - center) * lax.rsqrt(square - center * center + 1e-05) * gain + bias

def convolve(values, kernel):
    padded = jnp.pad(values, ((0, 0), (1, 1), (1, 1), (0, 0)))
    rows_count = values.shape[1]
    cols_count = values.shape[2]
    summed = jnp.zeros(values.shape[:3] + (kernel.shape[2],), values.dtype)
    for position in range(9):
        window = padded[:, position // 3:position // 3 + rows_count, position % 3:position % 3 + cols_count, :]
        summed = summed + jnp.einsum('mhwc,cd->mhwd', window, kernel[position], precision=highest)
    return summed

def self_attention(query, keys, values):
    query_count = query.shape[0]
    block_rows = math.gcd(query_count, 512)

    def one_block(query_block):
        scores = low_back(jnp.einsum('qhd,khd->hqk', query_block, keys, precision=highest) * HEAD_DIM ** (-0.5))
        weights = low(jax.nn.softmax(scores, axis=-1))
        return jnp.einsum('hqk,khd->qhd', weights, values, precision=highest)
    blocks = query.reshape(query_count // block_rows, block_rows, HEADS, HEAD_DIM)
    outputs = lax.map(jax.checkpoint(one_block), blocks)
    return outputs.reshape(query.shape)

def cross_attention(query, keys, values, text_length):
    scores = low_back(jnp.einsum('mqhd,mkhd->mhqk', query, keys, precision=highest) * HEAD_DIM ** (-0.5))
    present = jnp.arange(TEXT)[None, None, None, :] < text_length[:, None, None, None]
    weights = low(jax.nn.softmax(jnp.where(present, scores, -1e+30), axis=-1))
    return jnp.einsum('mhqk,mkhd->mqhd', weights, values, precision=highest)

def forward(pixels, conv_weights, film_time, film_text, group_gain, group_bias, layer_gain, layer_bias, attn_in, text_kv, out_self, out_cross, text_values, text_length, timestep):
    map_count = pixels.shape[0]
    features = low(sinusoid(timestep))
    pooled = low(pool_text(text_values, text_length))
    film = jnp.einsum('mk,ksc->msc', features, film_time, precision=highest) + jnp.einsum('mk,ksc->msc', pooled, film_text, precision=highest)
    film_scale = film[:, 0][:, None, None, :]
    film_shift = film[:, 1][:, None, None, :]
    first = low(jax.nn.silu(group_norm(pixels, group_gain[0], group_bias[0])))
    inner = low_back(jax.checkpoint(convolve)(first, conv_weights[0]))
    second = low(jax.nn.silu(group_norm(inner * (1.0 + film_scale) + film_shift, group_gain[1], group_bias[1])))
    branch = low_back(jax.checkpoint(convolve)(second, conv_weights[1]))
    middle = (pixels + branch) * root_half
    normed = low(layer_norm(middle, layer_gain, layer_bias)).reshape(map_count, -1, C)
    projected = low(low_back(jnp.einsum('mnc,pcd->pmnd', normed, attn_in, precision=highest)))
    text_proj = low(jnp.einsum('mtx,pxd->pmtd', text_values, text_kv, precision=highest))
    split_shape = (map_count, -1, HEADS, HEAD_DIM)
    query = projected[0].reshape(split_shape)
    keys = projected[1].reshape(split_shape)
    values = projected[2].reshape(split_shape)
    cross_query = projected[3].reshape(split_shape)
    cross_keys = text_proj[0].reshape(split_shape)
    cross_values = text_proj[1].reshape(split_shape)
    attended = jnp.stack([self_attention(query[position], keys[position], values[position]) for position in range(map_count)])
    crossed = cross_attention(cross_query, cross_keys, cross_values, text_length)
    attended = low(low_back(attended.reshape(map_count, -1, C)))
    crossed = low(low_back(crossed.reshape(map_count, -1, C)))
    mixed = jnp.einsum('mnh,hc->mnc', attended, out_self, precision=highest) + jnp.einsum('mnh,hc->mnc', crossed, out_cross, precision=highest)
    return middle + low_back(mixed).reshape(middle.shape)

def reference(pixels, text_states, text_length, timestep, conv_weights, film_time, film_text, group_gain, group_bias, layer_gain, layer_bias, attn_in, text_kv, out_self, out_cross, cotangent):
    inputs = [array.astype(jnp.float32) for array in (pixels, conv_weights, film_time, film_text, group_gain, group_bias, layer_gain, layer_bias, attn_in, text_kv, out_self, out_cross)]
    text_values = text_states.astype(jnp.float32)

    def bound(*arrays):
        return forward(*arrays, text_values, text_length, timestep)
    result, pullback = jax.vjp(bound, *inputs)
    grads = pullback(cotangent.astype(jnp.float32))
    return (result, grads[0], grads[1], grads[2], grads[3], grads[4], grads[5], grads[6], grads[7], grads[8], grads[9], grads[10], grads[11])
```

```python
import math

import jax
import jax.numpy as jnp
from jax import lax
from jax.sharding import PartitionSpec as P

C = 1024
GROUPS = 32
HEAD_DIM = 128
TEXT = 128
TEMB = 1024


root_half = 1.0 / math.sqrt(2.0)
highest = lax.Precision.HIGHEST


def extended(cells, sides, width):
    for axis, dim in sides:
        count = lax.axis_size(axis)
        ends = count - 1
        head = lax.slice_in_dim(cells, 0, width, axis=dim)
        tail = lax.slice_in_dim(cells, cells.shape[dim] - width, cells.shape[dim], axis=dim)
        cells = jnp.concatenate(
            [
                lax.ppermute(tail, axis, [(i, (i + 1) % count) for i in range(ends)]),
                cells,
                lax.ppermute(head, axis, [((i + 1) % count, i) for i in range(ends)]),
            ],
            axis=dim,
        )
    return cells


def sinusoid(steps):
    half_width = TEMB // 2
    frequency = jnp.exp(-math.log(10000.0) * jnp.arange(half_width, dtype=jnp.float32) / half_width)
    angles = steps.astype(jnp.float32)[:, None] * frequency[None, :]
    return jnp.concatenate([jnp.cos(angles), jnp.sin(angles)], axis=1)


def silu_slope(values):
    logistic = jax.nn.sigmoid(values)
    return logistic * (1.0 + values * (1.0 - logistic))


def flipped(values, axis, mask):
    count = lax.axis_size(axis)
    return lax.ppermute(values, axis, [(i, i ^ mask) for i in range(count)])


def total(values, axis):
    mask = 1
    while mask < lax.axis_size(axis):
        values = values + flipped(values, axis, mask)
        mask *= 2
    return values


def wide_total(first, second):
    both = total(jnp.stack([first, second]), "wide")
    return both[0], both[1]


def token_total(first, second):
    both = total(jnp.stack([first, second]), "tensor")
    return both[0], both[1]


def rows_of(values):
    return extended(values, (("wide", 1),), 1)


def full_channels(values):
    return lax.all_gather(values, "tensor", axis=3, tiled=True)


def own_part(values):
    return lax.psum_scatter(
        values.astype(jnp.bfloat16), "tensor", scatter_dimension=3, tiled=True
    ).astype(jnp.float32)


def spread(values):
    framed = rows_of(full_channels(values))
    return jnp.pad(framed, ((0, 0), (0, 0), (1, 1), (0, 0)))


def group_mean(values, count):
    map_count = values.shape[0]
    per_group = C // GROUPS
    summed = jnp.sum(values.reshape(map_count, -1, per_group), axis=2) / count
    return jnp.repeat(summed, per_group, axis=1)[:, None, None, :]


def group_forward(values, count):
    sums, squares = wide_total(jnp.sum(values, axis=(1, 2)), jnp.sum(values * values, axis=(1, 2)))
    center = group_mean(sums, count)
    inverse = lax.rsqrt(group_mean(squares, count) - center * center + 1e-05)
    return ((values - center) * inverse, center, inverse)


def group_backward(grad_normed, scaled, gain, inverse, count, extra_first, extra_second):
    map_count = scaled.shape[0]
    first = jnp.sum(grad_normed * scaled, axis=(1, 2))
    second = jnp.sum(grad_normed, axis=(1, 2))
    first_all, second_all = wide_total(
        jnp.concatenate([first, extra_first], axis=0),
        jnp.concatenate([second, extra_second], axis=0),
    )
    gain_grad = jnp.sum(first_all[:map_count], axis=0)
    bias_grad = jnp.sum(second_all[:map_count], axis=0)
    dot_mean = group_mean(gain * first_all[:map_count], count)
    plain_mean = group_mean(gain * second_all[:map_count], count)
    grad_values = inverse * (grad_normed * gain - plain_mean - scaled * dot_mean)
    return (grad_values, gain_grad, bias_grad, first_all[map_count:], second_all[map_count:])


def convolve(framed, kernel):
    row_count = framed.shape[1] - 2
    col_count = framed.shape[2] - 2
    summed = None
    for position in range(9):
        window = framed[
            :, position // 3 : position // 3 + row_count, position % 3 : position % 3 + col_count, :
        ]
        contribution = jnp.einsum(
            "mrwc,cd->mrwd", window, kernel[position], preferred_element_type=jnp.float32
        )
        summed = contribution if position == 0 else summed + contribution
    return summed


def kernel_grad(own_framed, own_grad):
    own = own_framed[:, 1:-1, 1:-1, :]
    swapped = lax.all_to_all(own, "wide", split_axis=3, concat_axis=1, tiled=True)
    framed = jnp.pad(swapped, ((0, 0), (1, 1), (1, 1), (0, 0)))
    grad_low = lax.all_gather(own_grad, "wide", axis=1, tiled=True)
    row_count = grad_low.shape[1]
    col_count = grad_low.shape[2]
    return jnp.stack(
        [
            jnp.einsum(
                "mrwc,mrwd->cd",
                framed[
                    :,
                    position // 3 : position // 3 + row_count,
                    position % 3 : position % 3 + col_count,
                    :,
                ],
                grad_low,
                preferred_element_type=jnp.float32,
            )
            for position in range(9)
        ]
    )


def input_grad(grad_low, kernel):
    row_count = grad_low.shape[1]
    col_count = grad_low.shape[2]
    framed = jnp.pad(rows_of(grad_low), ((0, 0), (0, 0), (1, 1), (0, 0)))
    summed = None
    for position in range(9):
        top_row = 2 - position // 3
        left_col = 2 - position % 3
        window = framed[:, top_row : top_row + row_count, left_col : left_col + col_count, :]
        contribution = jnp.einsum(
            "mrwd,cd->mrwc", window, kernel[position], preferred_element_type=jnp.float32
        )
        summed = contribution if position == 0 else summed + contribution
    return summed


def key_blocks(array, block_rows):
    map_count = array.shape[0]
    length = array.shape[1]
    shaped = array.reshape((map_count, length // block_rows, block_rows) + array.shape[2:])
    return jnp.moveaxis(shaped, 1, 0)


def attend_forward(query, keys, values):
    score_scale = HEAD_DIM ** (-0.5)
    map_count, query_count, head_count = (query.shape[0], query.shape[1], query.shape[2])
    start_state = (
        jnp.full((map_count, query_count, head_count), -1e30, jnp.float32),
        jnp.zeros((map_count, query_count, head_count), jnp.float32),
        jnp.zeros(query.shape, jnp.float32),
    )
    pieces = (
        lax.all_gather(keys, "wide", axis=1, tiled=True),
        lax.all_gather(values, "wide", axis=1, tiled=True),
    )
    block_rows = math.gcd(pieces[0].shape[1], 1024)

    def attend_one_block(inner_state, blocks):
        running_max, weight_sum, weighted = inner_state
        key_block, value_block = blocks
        scores = (
            jnp.einsum("mqhd,mkhd->mqhk", query, key_block, preferred_element_type=jnp.float32)
            * score_scale
        )
        raised = jnp.maximum(running_max, jnp.max(scores, axis=-1))
        rescale = jnp.exp(running_max - raised)
        weights = jnp.exp(scores - raised[..., None])
        weight_sum = weight_sum * rescale + jnp.sum(weights, axis=-1)
        weighted = weighted * rescale[..., None] + jnp.einsum(
            "mqhk,mkhd->mqhd",
            weights.astype(jnp.bfloat16),
            value_block,
            preferred_element_type=jnp.float32,
        )
        return ((raised, weight_sum, weighted), None)

    outcome, unused = lax.scan(
        attend_one_block,
        start_state,
        (key_blocks(pieces[0], block_rows), key_blocks(pieces[1], block_rows)),
    )
    running_max, weight_sum, weighted = outcome
    return (weighted / weight_sum[..., None], running_max + jnp.log(weight_sum))


def query_grads(query, grad_out, log_sums, deltas, keys, values):
    score_scale = HEAD_DIM ** (-0.5)
    pieces = (
        lax.all_gather(keys, "wide", axis=1, tiled=True),
        lax.all_gather(values, "wide", axis=1, tiled=True),
    )
    block_rows = math.gcd(pieces[0].shape[1], 1024)

    def query_one_block(grad_sum, blocks):
        key_block, value_block = blocks
        scores = (
            jnp.einsum("mqhd,mkhd->mqhk", query, key_block, preferred_element_type=jnp.float32)
            * score_scale
        )
        probs = jnp.exp(scores - log_sums[..., None])
        grad_probs = jnp.einsum(
            "mqhd,mkhd->mqhk", grad_out, value_block, preferred_element_type=jnp.float32
        )
        grad_scores = (probs * (grad_probs - deltas[..., None])).astype(jnp.bfloat16)
        grad_sum = (
            grad_sum
            + jnp.einsum(
                "mqhk,mkhd->mqhd", grad_scores, key_block, preferred_element_type=jnp.float32
            )
            * score_scale
        )
        return (grad_sum, None)

    outcome, unused = lax.scan(
        query_one_block,
        jnp.zeros(query.shape, jnp.float32),
        (key_blocks(pieces[0], block_rows), key_blocks(pieces[1], block_rows)),
    )
    return outcome


def key_grads(keys, values, query_wide, grad_wide, log_sums, deltas):
    score_scale = HEAD_DIM ** (-0.5)
    start_state = (jnp.zeros(keys.shape, jnp.float32), jnp.zeros(keys.shape, jnp.float32))
    pieces = (
        lax.all_gather(query_wide, "wide", axis=1, tiled=True),
        lax.all_gather(grad_wide, "wide", axis=1, tiled=True),
        lax.all_gather(log_sums, "wide", axis=1, tiled=True),
        lax.all_gather(deltas, "wide", axis=1, tiled=True),
    )
    block_rows = math.gcd(pieces[0].shape[1], 1024)

    def key_one_block(sums, blocks):
        grad_keys, grad_values = sums
        query_block, grad_block, log_block, delta_block = blocks
        query_low = query_block.astype(jnp.bfloat16)
        grad_low = grad_block.astype(jnp.bfloat16)
        scores = (
            jnp.einsum("mqhd,mkhd->mqhk", query_low, keys, preferred_element_type=jnp.float32)
            * score_scale
        )
        probs = jnp.exp(scores - log_block[..., None])
        grad_values = grad_values + jnp.einsum(
            "mqhk,mqhd->mkhd",
            probs.astype(jnp.bfloat16),
            grad_low,
            preferred_element_type=jnp.float32,
        )
        grad_probs = jnp.einsum(
            "mqhd,mkhd->mqhk", grad_low, values, preferred_element_type=jnp.float32
        )
        grad_scores = (probs * (grad_probs - delta_block[..., None])).astype(jnp.bfloat16)
        grad_keys = (
            grad_keys
            + jnp.einsum(
                "mqhk,mqhd->mkhd", grad_scores, query_low, preferred_element_type=jnp.float32
            )
            * score_scale
        )
        return ((grad_keys, grad_values), None)

    blocks = (
        key_blocks(pieces[0], block_rows),
        key_blocks(pieces[1], block_rows),
        key_blocks(pieces[2], block_rows),
        key_blocks(pieces[3], block_rows),
    )
    outcome, unused = lax.scan(key_one_block, start_state, blocks)
    return outcome


def shards(
    pixels,
    text_states,
    text_length,
    timestep,
    conv_weights,
    film_time,
    film_text,
    group_gain,
    group_bias,
    layer_gain,
    layer_bias,
    attn_in,
    text_kv,
    out_self,
    out_cross,
    cotangent,
):
    map_count, row_count, col_count, width_own = pixels.shape
    head_count = width_own // HEAD_DIM
    token_count = row_count * col_count
    pixel_count = row_count * lax.axis_size("wide") * col_count * (C // GROUPS)
    score_scale = HEAD_DIM ** (-0.5)
    gathered = (
        (
            lax.all_gather(conv_weights[0], "wide", axis=1, tiled=True),
            lax.all_gather(conv_weights[1], "wide", axis=1, tiled=True),
        ),
        lax.all_gather(attn_in, "wide", axis=1, tiled=True),
        lax.all_gather(out_self, "wide", axis=1, tiled=True),
        lax.all_gather(out_cross, "wide", axis=1, tiled=True),
    )
    kernels, in_maps, self_out, cross_out = gathered
    features = sinusoid(timestep).astype(jnp.bfloat16)
    present = jnp.arange(TEXT)[None, :] < text_length[:, None]
    pooled = jnp.einsum(
        "mtx,mt->mx", text_states, present.astype(jnp.bfloat16), preferred_element_type=jnp.float32
    )
    pooled = (pooled / text_length.astype(jnp.float32)[:, None]).astype(jnp.bfloat16)
    wide_index = lax.axis_index("wide")
    time_rows = film_time.shape[0]
    text_rows = film_text.shape[0]
    own_features = lax.dynamic_slice_in_dim(features, wide_index * time_rows, time_rows, 1)
    own_pooled = lax.dynamic_slice_in_dim(pooled, wide_index * text_rows, text_rows, 1)
    own_text = lax.dynamic_slice_in_dim(text_states, wide_index * text_rows, text_rows, 2)
    film_term = jnp.einsum(
        "mk,ksc->msc", own_features, film_time, preferred_element_type=jnp.float32
    ) + jnp.einsum("mk,ksc->msc", own_pooled, film_text, preferred_element_type=jnp.float32)
    text_term = jnp.einsum("mtx,pxd->pmtd", own_text, text_kv, preferred_element_type=jnp.float32)
    film = total(film_term, "wide")
    text_proj = lax.psum(text_term.astype(jnp.bfloat16), "wide")
    film_scale = film[:, 0][:, None, None, :]
    film_shift = film[:, 1][:, None, None, :]
    source = pixels.astype(jnp.float32)
    first_scaled, first_center, first_inverse = group_forward(source, pixel_count)
    first_normed = first_scaled * group_gain[0] + group_bias[0]
    first_framed = spread(jax.nn.silu(first_normed).astype(jnp.bfloat16))
    inner = convolve(first_framed, kernels[0])
    lifted = inner * (1.0 + film_scale) + film_shift
    second_scaled, second_center, second_inverse = group_forward(lifted, pixel_count)
    second_normed = second_scaled * group_gain[1] + group_bias[1]
    second_framed = spread(jax.nn.silu(second_normed).astype(jnp.bfloat16))
    middle = (source + convolve(second_framed, kernels[1])) * root_half
    token_sum, token_square = token_total(jnp.sum(middle, axis=3), jnp.sum(middle * middle, axis=3))
    token_center = token_sum / C
    token_inverse = lax.rsqrt(token_square / C - token_center * token_center + 1e-05)[..., None]
    token_scaled = (middle - token_center[..., None]) * token_inverse
    normed = full_channels((token_scaled * layer_gain + layer_bias).astype(jnp.bfloat16)).reshape(
        map_count, token_count, C
    )
    projected = jnp.einsum(
        "mnc,pcd->pmnd", normed, in_maps, preferred_element_type=jnp.float32
    ).astype(jnp.bfloat16)
    heads_shape = (map_count, token_count, head_count, HEAD_DIM)
    text_shape = (map_count, TEXT, head_count, HEAD_DIM)
    query = projected[0].reshape(heads_shape)
    keys = projected[1].reshape(heads_shape)
    values = projected[2].reshape(heads_shape)
    cross_query = projected[3].reshape(heads_shape)
    cross_keys = text_proj[0].reshape(text_shape)
    cross_values = text_proj[1].reshape(text_shape)
    attended, log_sums = attend_forward(query, keys, values)
    attended_low = attended.astype(jnp.bfloat16).reshape(map_count, token_count, width_own)
    cross_scores = (
        jnp.einsum("mqhd,mkhd->mqhk", cross_query, cross_keys, preferred_element_type=jnp.float32)
        * score_scale
    )
    cross_probs = jax.nn.softmax(jnp.where(present[:, None, None, :], cross_scores, -1e30), axis=-1)
    crossed = jnp.einsum(
        "mqhk,mkhd->mqhd",
        cross_probs.astype(jnp.bfloat16),
        cross_values,
        preferred_element_type=jnp.float32,
    )
    crossed_low = crossed.astype(jnp.bfloat16).reshape(map_count, token_count, width_own)
    mixed = jnp.einsum(
        "mnh,hc->mnc", attended_low, self_out, preferred_element_type=jnp.float32
    ) + jnp.einsum("mnh,hc->mnc", crossed_low, cross_out, preferred_element_type=jnp.float32)
    result = middle + own_part(mixed.reshape(map_count, row_count, col_count, C))
    grad_full = full_channels(cotangent.astype(jnp.bfloat16)).reshape(map_count, token_count, C)
    out_self_part = jnp.einsum(
        "mnh,mnc->hc", attended_low, grad_full, preferred_element_type=jnp.float32
    )
    out_cross_part = jnp.einsum(
        "mnh,mnc->hc", crossed_low, grad_full, preferred_element_type=jnp.float32
    )
    grad_attended = (
        jnp.einsum("mnc,hc->mnh", grad_full, self_out, preferred_element_type=jnp.float32)
        .astype(jnp.bfloat16)
        .reshape(heads_shape)
    )
    grad_crossed = (
        jnp.einsum("mnc,hc->mnh", grad_full, cross_out, preferred_element_type=jnp.float32)
        .astype(jnp.bfloat16)
        .reshape(heads_shape)
    )
    deltas = jnp.sum(grad_attended.astype(jnp.float32) * attended, axis=-1)
    grad_query = query_grads(query, grad_attended, log_sums, deltas, keys, values).astype(
        jnp.bfloat16
    )
    grad_keys, grad_values = key_grads(
        keys, values, query.astype(jnp.float32), grad_attended.astype(jnp.float32), log_sums, deltas
    )
    grad_cross_probs = jnp.einsum(
        "mqhd,mkhd->mqhk", grad_crossed, cross_values, preferred_element_type=jnp.float32
    )
    grad_cross_scores = cross_probs * (
        grad_cross_probs - jnp.sum(cross_probs * grad_cross_probs, axis=-1, keepdims=True)
    )
    grad_cross_low = grad_cross_scores.astype(jnp.bfloat16)
    grad_cross_query = (
        jnp.einsum(
            "mqhk,mkhd->mqhd", grad_cross_low, cross_keys, preferred_element_type=jnp.float32
        )
        * score_scale
    ).astype(jnp.bfloat16)
    grad_cross_keys = (
        jnp.einsum(
            "mqhk,mqhd->mkhd", grad_cross_low, cross_query, preferred_element_type=jnp.float32
        )
        * score_scale
    )
    grad_cross_values = jnp.einsum(
        "mqhk,mqhd->mkhd",
        cross_probs.astype(jnp.bfloat16),
        grad_crossed,
        preferred_element_type=jnp.float32,
    )
    text_grads = jnp.stack([grad_cross_keys, grad_cross_values]).reshape(
        2, map_count, TEXT, width_own
    )
    grad_projected = jnp.stack(
        [
            grad_query,
            grad_keys.astype(jnp.bfloat16),
            grad_values.astype(jnp.bfloat16),
            grad_cross_query,
        ]
    ).reshape(4, map_count, token_count, width_own)
    in_part = jnp.einsum(
        "mnc,pmnd->pcd", normed, grad_projected, preferred_element_type=jnp.float32
    )
    grad_normed = own_part(
        jnp.einsum(
            "pmnd,pcd->mnc", grad_projected, in_maps, preferred_element_type=jnp.float32
        ).reshape(map_count, row_count, col_count, C)
    )
    layer_gain_part = jnp.sum(grad_normed * token_scaled, axis=(0, 1, 2))
    layer_bias_part = jnp.sum(grad_normed, axis=(0, 1, 2))
    grad_scaled = grad_normed * layer_gain
    plain_sum, dot_sum = token_total(
        jnp.sum(grad_scaled, axis=3), jnp.sum(grad_scaled * token_scaled, axis=3)
    )
    grad_middle = (
        token_inverse
        * (grad_scaled - plain_sum[..., None] / C - token_scaled * dot_sum[..., None] / C)
        + cotangent
    )
    grad_two = (grad_middle * root_half).astype(jnp.bfloat16)
    second_kernel_grad = kernel_grad(second_framed, grad_two)
    grad_second = own_part(input_grad(grad_two, kernels[1]))
    grad_lifted, gain_two, bias_two, layer_gain_sum, layer_bias_sum = group_backward(
        grad_second * silu_slope(second_normed),
        second_scaled,
        group_gain[1],
        second_inverse,
        pixel_count,
        layer_gain_part[None],
        layer_bias_part[None],
    )
    grad_film = jnp.stack(
        [jnp.sum(grad_lifted * inner, axis=(1, 2)), jnp.sum(grad_lifted, axis=(1, 2))], axis=1
    )
    film_all = total(grad_film, "wide")
    text_all = lax.psum(text_grads.astype(jnp.bfloat16), "wide").astype(jnp.float32)
    time_grad = jnp.einsum(
        "mk,msc->ksc", own_features.astype(jnp.float32), film_all, precision=highest
    )
    text_grad = jnp.einsum(
        "mx,msc->xsc", own_pooled.astype(jnp.float32), film_all, precision=highest
    )
    kv_grad = jnp.einsum("mtx,pmtd->pxd", own_text.astype(jnp.float32), text_all, precision=highest)
    grad_one = (grad_lifted * (1.0 + film_scale)).astype(jnp.bfloat16)
    first_kernel_grad = kernel_grad(first_framed, grad_one)
    grad_first = own_part(input_grad(grad_one, kernels[0]))
    empty_rows = jnp.zeros((0, width_own), jnp.float32)
    grad_source, gain_one, bias_one, unused_first, unused_second = group_backward(
        grad_first * silu_slope(first_normed),
        first_scaled,
        group_gain[0],
        first_inverse,
        pixel_count,
        empty_rows,
        empty_rows,
    )
    pixels_grad = grad_source + grad_middle * root_half
    parts = (
        lax.psum_scatter(
            in_part.astype(jnp.bfloat16), "wide", scatter_dimension=1, tiled=True
        ).astype(jnp.float32),
        lax.psum_scatter(
            jnp.concatenate([out_self_part, out_cross_part]).astype(jnp.bfloat16),
            "wide",
            scatter_dimension=1,
            tiled=True,
        ).astype(jnp.float32),
    )
    return (
        result,
        pixels_grad,
        jnp.stack([first_kernel_grad, second_kernel_grad]),
        time_grad,
        text_grad,
        jnp.stack([gain_one, gain_two]),
        jnp.stack([bias_one, bias_two]),
        layer_gain_sum[0],
        layer_bias_sum[0],
        parts[0],
        kv_grad,
        parts[1][:width_own],
        parts[1][width_own:],
    )


def solution(mesh):
    placed = (
        P(None, "wide", None, "tensor"),
        P(),
        P(),
        P(),
        P(None, None, "wide", "tensor"),
        P("wide", None, "tensor"),
        P("wide", None, "tensor"),
        P(None, "tensor"),
        P(None, "tensor"),
        P("tensor"),
        P("tensor"),
        P(None, "wide", "tensor"),
        P(None, "wide", "tensor"),
        P("tensor", "wide"),
        P("tensor", "wide"),
        P(None, "wide", None, "tensor"),
    )
    return jax.shard_map(
        shards,
        mesh=mesh,
        in_specs=placed,
        out_specs=(
            P(None, "wide", None, "tensor"),
            P(None, "wide", None, "tensor"),
            P(None, None, "wide", "tensor"),
            P("wide", None, "tensor"),
            P("wide", None, "tensor"),
            P(None, "tensor"),
            P(None, "tensor"),
            P("tensor"),
            P("tensor"),
            P(None, "wide", "tensor"),
            P(None, "wide", "tensor"),
            P("tensor", "wide"),
            P("tensor", "wide"),
        ),
        check_vma=False,
    )
```

```python
import functools
import math

import jax
import jax.numpy as jnp
from jax import lax
from jax.experimental import pallas as pl
from jax.experimental.pallas import tpu as pltpu
from jax.sharding import PartitionSpec as P

C = 1024
GROUPS = 32
HEAD_DIM = 128
TEXT = 128
TEMB = 1024
MIB = 1 << 20
in_vmem = pl.BlockSpec(memory_space=pltpu.VMEM)
in_smem = pl.BlockSpec(memory_space=pltpu.SMEM)


def local_kernel(body, outs, operands, scratch, limit, flops, aliases=None, out_specs=None):
    size = sum(a.size * a.dtype.itemsize for a in operands)
    size += sum(math.prod(o.shape) * o.dtype.itemsize for o in outs)
    return pl.pallas_call(
        body,
        out_shape=outs,
        in_specs=[in_smem] + [in_vmem] * (len(operands) - 1),
        out_specs=[in_vmem] * len(outs) if out_specs is None else out_specs,
        scratch_shapes=scratch,
        input_output_aliases={} if aliases is None else aliases,
        compiler_params=pltpu.CompilerParams(vmem_limit_bytes=limit * MIB),
        cost_estimate=pl.CostEstimate(flops=flops, bytes_accessed=size, transcendentals=0),
    )(*operands)


def turned(values, width):
    rows = values.shape[0]
    wide = values.astype(jnp.float32)
    column = lax.rem(lax.broadcasted_iota(jnp.int32, values.shape, 0), width)
    before = jnp.where(column == 0, 0.0, pltpu.roll(wide, 1, 0))
    after = jnp.where(column == width - 1, 0.0, pltpu.roll(wide, rows - 1, 0))
    return before.astype(jnp.bfloat16), values, after.astype(jnp.bfloat16)


def halves_swapped(values, odd):
    half = values.shape[1] // 2
    other = jnp.concatenate([values[:, half:], values[:, :half]], axis=1)
    return jnp.where(odd, other, values)


class Weights:
    def __init__(self, refs, spot):
        self.refs = refs
        self.paired = len(refs) > 1
        self.wide = spot[0]
        self.odd = lax.rem(spot[0], 2) == 1

    def block(self, chunk):
        return lax.bitwise_xor(lax.div(self.wide, 2), chunk) if self.paired else chunk

    def tap(self, chunk, position):
        if not self.paired:
            span = self.refs[0].shape[1] // 4
            return self.refs[0][position, chunk * span : (chunk + 1) * span, :]
        parts = []
        for refs in (self.refs[:5], self.refs[5:]):
            if chunk < 3:
                parts.append(refs[chunk][position])
            else:
                first = refs[3].shape[0]
                parts.append(refs[3][position] if position < first else refs[4][position - first])
        return jnp.concatenate(parts, axis=0)

    def ordered(self, values):
        return halves_swapped(values, self.odd) if self.paired else values


def conv_body(groups, parts, rows, width, spot, *refs):
    pieces = refs[:groups]
    top, bottom = refs[groups : groups + 2]
    weights = Weights(refs[groups + 2 : groups + 2 + parts], spot)
    out, *sends, frame = refs[groups + 2 + parts :]
    span = pieces[0].shape[1]
    for mask in range(groups):
        block = lax.bitwise_xor(spot[1], mask)
        own = pieces[mask][...]
        lanes = slice(mask * span, (mask + 1) * span)
        framed = jnp.concatenate([top[:, lanes], own, bottom[:, lanes]], axis=0)
        for column, values in enumerate(turned(weights.ordered(framed), width)):
            frame[block, column] = values
    total_sum = jnp.zeros(out.shape, jnp.float32)
    for chunk in range(groups):
        block = weights.block(chunk)
        for position in range(9):
            start = (position // 3) * width
            window = frame[block, position % 3, start : start + rows * width, :]
            total_sum += jnp.dot(
                window, weights.tap(chunk, position), preferred_element_type=jnp.float32
            )
        center = frame[block, 1, width : (rows + 1) * width, :]
        if weights.paired:
            sends[2 * chunk][...] = center[:, : span // 2]
            sends[2 * chunk + 1][...] = center[:, span // 2 :]
        else:
            sends[0][:, chunk * span : (chunk + 1) * span] = center
    out[...] = total_sum


def back_body(groups, rows, width, spot, grad, top, bottom, *refs):
    frame, held = refs[-2:]
    outs = refs[-2 - groups : -2]
    weights = Weights(refs[: -2 - groups], spot)
    framed = jnp.concatenate([top[...], grad[...], bottom[...]], axis=0)
    for column, values in enumerate(turned(framed, width)):
        frame[column] = values
    for chunk in range(groups):
        total_sum = jnp.zeros(held.shape[1:], jnp.float32)
        for position in range(9):
            start = (2 - position // 3) * width
            total_sum += lax.dot_general(
                frame[2 - position % 3, start : start + rows * width, :],
                weights.tap(chunk, position),
                (((1,), (1,)), ((), ())),
                preferred_element_type=jnp.float32,
            )
        held[weights.block(chunk)] = weights.ordered(total_sum).astype(jnp.bfloat16)
    for mask in range(groups):
        outs[mask][...] = held[lax.bitwise_xor(spot[1], mask)]


def bf16_like(*shape):
    return jax.ShapeDtypeStruct(shape, jnp.bfloat16)


def f32_like(*shape):
    return jax.ShapeDtypeStruct(shape, jnp.float32)


def flipped(values, axis, mask):
    count = lax.axis_size(axis)
    return lax.ppermute(values, axis, [(i, i ^ mask) for i in range(count)])


def spread_slots(values, first):
    over_x, over_y = flipped(values, "wide", 2), flipped(values, "wide", 4)
    low, high = flipped(over_x[:first], "wide", 4), flipped(over_y[first:], "wide", 2)
    mine = [values, over_x, over_y, low, high]
    return mine + [flipped(part, "wide", 1) for part in mine]


def has_slots():
    return lax.axis_size("wide") == 8


def gathered_kernel(kernel):
    if has_slots():
        return spread_slots(kernel, 5)
    return [lax.all_gather(kernel, "wide", axis=1, tiled=True)]


def channel_pieces(values):
    count = lax.axis_size("tensor")
    return [values] + [flipped(values, "tensor", mask) for mask in range(1, count)]


def edge_rows(last, first):
    count = lax.axis_size("wide")
    above = lax.ppermute(last, "wide", [(i, i + 1) for i in range(count - 1)])
    below = lax.ppermute(first, "wide", [(i + 1, i) for i in range(count - 1)])
    return above, below


def convolve(spot, values, kernel, rows, width):
    pieces = channel_pieces(values)
    groups, area, span = len(pieces), rows * width, values.shape[1]
    above, below = edge_rows(
        jnp.concatenate([piece[-width:] for piece in pieces], axis=1),
        jnp.concatenate([piece[:width] for piece in pieces], axis=1),
    )
    sends = [bf16_like(area, span // 2)] * (2 * groups) if has_slots() else [bf16_like(area, C)]
    return local_kernel(
        functools.partial(conv_body, groups, len(kernel), rows, width),
        [f32_like(area, span)] + sends,
        [spot, *pieces, above, below, *kernel],
        [pltpu.VMEM((groups, 3, (rows + 2) * width, span), jnp.bfloat16)],
        28,
        2 * 9 * area * C * span,
    )


def convolve_back(spot, grad, kernel, rows, width):
    groups, area, span = lax.axis_size("tensor"), rows * width, grad.shape[1]
    above, below = edge_rows(grad[-width:], grad[:width])
    parts = local_kernel(
        functools.partial(back_body, groups, rows, width),
        [bf16_like(area, span)] * groups,
        [spot, grad, above, below, *kernel],
        [
            pltpu.VMEM((3, (rows + 2) * width, span), jnp.bfloat16),
            pltpu.VMEM((groups, area, span), jnp.bfloat16),
        ],
        24,
        2 * 9 * area * C * span,
    )
    return summed_parts(parts)


def summed_parts(parts):
    summed = parts[0].astype(jnp.float32)
    for mask in range(1, len(parts)):
        summed = summed + flipped(parts[mask], "tensor", mask).astype(jnp.float32)
    return summed


def kernel_grad_body(count, width, spot, *refs):
    pieces = refs[:count]
    grads = refs[count : count + 10]
    out, turned_all, grad_all = refs[-3:]
    wide = spot[0]
    area, span = pieces[0].shape
    depth = count * area
    turned_all[:, :width] = jnp.zeros((3 * span, width), jnp.bfloat16)
    turned_all[:, depth + width :] = jnp.zeros((3 * span, width), jnp.bfloat16)
    for mask in range(count):
        start = pl.multiple_of(lax.bitwise_xor(wide, mask) * area, area)
        for column, values in enumerate(turned(pieces[mask][...], width)):
            flat = jnp.transpose(values.astype(jnp.float32)).astype(jnp.bfloat16)
            turned_all[column * span : (column + 1) * span, pl.ds(start + width, area)] = flat
        half = grads[5 * (mask % 2) : 5 * (mask % 2) + 5]
        if mask < 6:
            grad_all[pl.ds(start, area), :] = half[mask // 2][...]
        else:
            grad_all[pl.ds(start, width), :] = half[3][...]
            grad_all[pl.ds(start + width, area - width), :] = half[4][...]
    for row in range(3):
        product = jnp.dot(
            turned_all[:, row * width : row * width + depth],
            grad_all[...],
            preferred_element_type=jnp.float32,
        )
        for column in range(3):
            out[0, 3 * row + column] = product[column * span : (column + 1) * span, :]


def kernel_grad(spot, sends, grad, rows, width, layer, earlier):
    count, area = len(sends), rows * width
    span, columns = sends[0].shape[1], grad.shape[1]
    pieces = [sends[0]] + [flipped(sends[mask], "wide", mask) for mask in range(1, count)]
    grads = spread_slots(grad, width)
    operands = [spot, *pieces, *grads]
    specs = [in_smem] + [in_vmem] * (len(operands) - 1)
    shape = f32_like(2, 9, span, columns)
    if earlier is not None:
        operands.append(earlier)
        specs.append(pl.BlockSpec(memory_space=pl.ANY))
    return pl.pallas_call(
        functools.partial(kernel_grad_body, count, width),
        out_shape=shape,
        in_specs=specs,
        grid=(1,),
        out_specs=pl.BlockSpec((1, 9, span, columns), lambda i: (layer, 0, 0, 0)),
        scratch_shapes=[
            pltpu.VMEM((3 * span, count * area + 2 * width), jnp.bfloat16),
            pltpu.VMEM((count * area, columns), jnp.bfloat16),
        ],
        input_output_aliases={} if earlier is None else {len(operands) - 1: 0},
        compiler_params=pltpu.CompilerParams(vmem_limit_bytes=24 * MIB),
        cost_estimate=pl.CostEstimate(
            flops=2 * 9 * count * area * span * columns, bytes_accessed=4 * MIB, transcendentals=0
        ),
    )(*operands)


def kernel_grad_whole(sends, grad, rows, width):
    natural = sends[0].reshape(1, rows, width, C)
    swapped = lax.all_to_all(natural, "wide", split_axis=3, concat_axis=1, tiled=True)
    framed = jnp.pad(swapped, ((0, 0), (1, 1), (1, 1), (0, 0)))
    low = lax.all_gather(
        grad.reshape(1, rows, width, grad.shape[1]), "wide", axis=1, tiled=True
    )
    return jnp.stack(
        [
            jnp.einsum(
                "mrwc,mrwd->cd",
                framed[:, tap // 3 : tap // 3 + low.shape[1], tap % 3 : tap % 3 + width, :],
                low,
                preferred_element_type=jnp.float32,
            )
            for tap in range(9)
        ]
    )


root_half = 1.0 / math.sqrt(2.0)
highest = lax.Precision.HIGHEST


def sinusoid(steps):
    half_width = TEMB // 2
    frequency = jnp.exp(-math.log(10000.0) * jnp.arange(half_width, dtype=jnp.float32) / half_width)
    angles = steps.astype(jnp.float32)[:, None] * frequency[None, :]
    return jnp.concatenate([jnp.cos(angles), jnp.sin(angles)], axis=1)


def silu_slope(values):
    logistic = jax.nn.sigmoid(values)
    return logistic * (1.0 + values * (1.0 - logistic))


def total(values, axis):
    mask = 1
    while mask < lax.axis_size(axis):
        values = values + flipped(values, axis, mask)
        mask *= 2
    return values


def wide_total(first, second):
    both = total(jnp.stack([first, second]), "wide")
    return both[0], both[1]


def token_total(first, second):
    both = total(jnp.stack([first, second]), "tensor")
    return both[0], both[1]


def full_channels(values):
    return lax.all_gather(values, "tensor", axis=3, tiled=True)


def own_part(values):
    return lax.psum_scatter(
        values.astype(jnp.bfloat16), "tensor", scatter_dimension=3, tiled=True
    ).astype(jnp.float32)


def group_mean(values, count):
    map_count = values.shape[0]
    per_group = C // GROUPS
    summed = jnp.sum(values.reshape(map_count, -1, per_group), axis=2) / count
    return jnp.repeat(summed, per_group, axis=1)[:, None, None, :]


def group_forward(values, count):
    sums, squares = wide_total(jnp.sum(values, axis=(1, 2)), jnp.sum(values * values, axis=(1, 2)))
    center = group_mean(sums, count)
    inverse = lax.rsqrt(group_mean(squares, count) - center * center + 1e-05)
    return ((values - center) * inverse, center, inverse)


def group_backward(grad_normed, scaled, gain, inverse, count, extra_first, extra_second):
    map_count = scaled.shape[0]
    first = jnp.sum(grad_normed * scaled, axis=(1, 2))
    second = jnp.sum(grad_normed, axis=(1, 2))
    first_all, second_all = wide_total(
        jnp.concatenate([first, extra_first], axis=0),
        jnp.concatenate([second, extra_second], axis=0),
    )
    gain_grad = jnp.sum(first_all[:map_count], axis=0)
    bias_grad = jnp.sum(second_all[:map_count], axis=0)
    dot_mean = group_mean(gain * first_all[:map_count], count)
    plain_mean = group_mean(gain * second_all[:map_count], count)
    grad_values = inverse * (grad_normed * gain - plain_mean - scaled * dot_mean)
    return (grad_values, gain_grad, bias_grad, first_all[map_count:], second_all[map_count:])


def key_blocks(array, block_rows):
    map_count = array.shape[0]
    length = array.shape[1]
    shaped = array.reshape((map_count, length // block_rows, block_rows) + array.shape[2:])
    return jnp.moveaxis(shaped, 1, 0)


def attend_forward(query, keys, values):
    score_scale = HEAD_DIM ** (-0.5)
    map_count, query_count, head_count = (query.shape[0], query.shape[1], query.shape[2])
    start_state = (
        jnp.full((map_count, query_count, head_count), -1e30, jnp.float32),
        jnp.zeros((map_count, query_count, head_count), jnp.float32),
        jnp.zeros(query.shape, jnp.float32),
    )
    pieces = (
        lax.all_gather(keys, "wide", axis=1, tiled=True),
        lax.all_gather(values, "wide", axis=1, tiled=True),
    )
    block_rows = math.gcd(pieces[0].shape[1], 1024)

    def attend_one_block(inner_state, blocks):
        running_max, weight_sum, weighted = inner_state
        key_block, value_block = blocks
        scores = (
            jnp.einsum("mqhd,mkhd->mqhk", query, key_block, preferred_element_type=jnp.float32)
            * score_scale
        )
        raised = jnp.maximum(running_max, jnp.max(scores, axis=-1))
        rescale = jnp.exp(running_max - raised)
        weights = jnp.exp(scores - raised[..., None])
        weight_sum = weight_sum * rescale + jnp.sum(weights, axis=-1)
        weighted = weighted * rescale[..., None] + jnp.einsum(
            "mqhk,mkhd->mqhd",
            weights.astype(jnp.bfloat16),
            value_block,
            preferred_element_type=jnp.float32,
        )
        return ((raised, weight_sum, weighted), None)

    outcome, unused = lax.scan(
        attend_one_block,
        start_state,
        (key_blocks(pieces[0], block_rows), key_blocks(pieces[1], block_rows)),
    )
    running_max, weight_sum, weighted = outcome
    return (weighted / weight_sum[..., None], running_max + jnp.log(weight_sum))


def query_grads(query, grad_out, log_sums, deltas, keys, values):
    score_scale = HEAD_DIM ** (-0.5)
    pieces = (
        lax.all_gather(keys, "wide", axis=1, tiled=True),
        lax.all_gather(values, "wide", axis=1, tiled=True),
    )
    block_rows = math.gcd(pieces[0].shape[1], 1024)

    def query_one_block(grad_sum, blocks):
        key_block, value_block = blocks
        scores = (
            jnp.einsum("mqhd,mkhd->mqhk", query, key_block, preferred_element_type=jnp.float32)
            * score_scale
        )
        probs = jnp.exp(scores - log_sums[..., None])
        grad_probs = jnp.einsum(
            "mqhd,mkhd->mqhk", grad_out, value_block, preferred_element_type=jnp.float32
        )
        grad_scores = (probs * (grad_probs - deltas[..., None])).astype(jnp.bfloat16)
        grad_sum = (
            grad_sum
            + jnp.einsum(
                "mqhk,mkhd->mqhd", grad_scores, key_block, preferred_element_type=jnp.float32
            )
            * score_scale
        )
        return (grad_sum, None)

    outcome, unused = lax.scan(
        query_one_block,
        jnp.zeros(query.shape, jnp.float32),
        (key_blocks(pieces[0], block_rows), key_blocks(pieces[1], block_rows)),
    )
    return outcome


def key_grads(keys, values, query_wide, grad_wide, log_sums, deltas):
    score_scale = HEAD_DIM ** (-0.5)
    start_state = (jnp.zeros(keys.shape, jnp.float32), jnp.zeros(keys.shape, jnp.float32))
    pieces = (
        lax.all_gather(query_wide, "wide", axis=1, tiled=True),
        lax.all_gather(grad_wide, "wide", axis=1, tiled=True),
        lax.all_gather(log_sums, "wide", axis=1, tiled=True),
        lax.all_gather(deltas, "wide", axis=1, tiled=True),
    )
    block_rows = math.gcd(pieces[0].shape[1], 1024)

    def key_one_block(sums, blocks):
        grad_keys, grad_values = sums
        query_block, grad_block, log_block, delta_block = blocks
        query_low = query_block.astype(jnp.bfloat16)
        grad_low = grad_block.astype(jnp.bfloat16)
        scores = (
            jnp.einsum("mqhd,mkhd->mqhk", query_low, keys, preferred_element_type=jnp.float32)
            * score_scale
        )
        probs = jnp.exp(scores - log_block[..., None])
        grad_values = grad_values + jnp.einsum(
            "mqhk,mqhd->mkhd",
            probs.astype(jnp.bfloat16),
            grad_low,
            preferred_element_type=jnp.float32,
        )
        grad_probs = jnp.einsum(
            "mqhd,mkhd->mqhk", grad_low, values, preferred_element_type=jnp.float32
        )
        grad_scores = (probs * (grad_probs - delta_block[..., None])).astype(jnp.bfloat16)
        grad_keys = (
            grad_keys
            + jnp.einsum(
                "mqhk,mqhd->mkhd", grad_scores, query_low, preferred_element_type=jnp.float32
            )
            * score_scale
        )
        return ((grad_keys, grad_values), None)

    blocks = (
        key_blocks(pieces[0], block_rows),
        key_blocks(pieces[1], block_rows),
        key_blocks(pieces[2], block_rows),
        key_blocks(pieces[3], block_rows),
    )
    outcome, unused = lax.scan(key_one_block, start_state, blocks)
    return outcome


def shards(
    pixels,
    text_states,
    text_length,
    timestep,
    conv_weights,
    film_time,
    film_text,
    group_gain,
    group_bias,
    layer_gain,
    layer_bias,
    attn_in,
    text_kv,
    out_self,
    out_cross,
    cotangent,
):
    map_count, row_count, col_count, width_own = pixels.shape
    head_count = width_own // HEAD_DIM
    token_count = row_count * col_count
    pixel_count = row_count * lax.axis_size("wide") * col_count * (C // GROUPS)
    score_scale = HEAD_DIM ** (-0.5)
    gathered = (
        None,
        lax.all_gather(attn_in, "wide", axis=1, tiled=True),
        lax.all_gather(out_self, "wide", axis=1, tiled=True),
        lax.all_gather(out_cross, "wide", axis=1, tiled=True),
    )
    unused, in_maps, self_out, cross_out = gathered
    spot = jnp.stack([lax.axis_index("wide"), lax.axis_index("tensor")]).astype(jnp.int32)
    own_shape = (map_count, row_count, col_count, width_own)
    flat = (token_count, width_own)
    kernel_one = gathered_kernel(conv_weights[0])
    later, kernel_one[-1] = lax.optimization_barrier((conv_weights[1], kernel_one[-1]))
    kernel_two = gathered_kernel(later)
    features = sinusoid(timestep).astype(jnp.bfloat16)
    present = jnp.arange(TEXT)[None, :] < text_length[:, None]
    pooled = jnp.einsum(
        "mtx,mt->mx", text_states, present.astype(jnp.bfloat16), preferred_element_type=jnp.float32
    )
    pooled = (pooled / text_length.astype(jnp.float32)[:, None]).astype(jnp.bfloat16)
    wide_index = lax.axis_index("wide")
    time_rows = film_time.shape[0]
    text_rows = film_text.shape[0]
    own_features = lax.dynamic_slice_in_dim(features, wide_index * time_rows, time_rows, 1)
    own_pooled = lax.dynamic_slice_in_dim(pooled, wide_index * text_rows, text_rows, 1)
    own_text = lax.dynamic_slice_in_dim(text_states, wide_index * text_rows, text_rows, 2)
    film_term = jnp.einsum(
        "mk,ksc->msc", own_features, film_time, preferred_element_type=jnp.float32
    ) + jnp.einsum("mk,ksc->msc", own_pooled, film_text, preferred_element_type=jnp.float32)
    text_term = jnp.einsum("mtx,pxd->pmtd", own_text, text_kv, preferred_element_type=jnp.float32)
    film = total(film_term, "wide")
    text_proj = lax.psum(text_term.astype(jnp.bfloat16), "wide")
    film_scale = film[:, 0][:, None, None, :]
    film_shift = film[:, 1][:, None, None, :]
    source = pixels.astype(jnp.float32)
    first_scaled, first_center, first_inverse = group_forward(source, pixel_count)
    first_normed = first_scaled * group_gain[0] + group_bias[0]
    first = jax.nn.silu(first_normed).astype(jnp.bfloat16).reshape(flat)
    inner, *first_sends = convolve(spot, first, kernel_one, row_count, col_count)
    inner = inner.reshape(own_shape)
    lifted = inner * (1.0 + film_scale) + film_shift
    second_scaled, second_center, second_inverse = group_forward(lifted, pixel_count)
    second_normed = second_scaled * group_gain[1] + group_bias[1]
    second = jax.nn.silu(second_normed).astype(jnp.bfloat16).reshape(flat)
    branch, *second_sends = convolve(spot, second, kernel_two, row_count, col_count)
    middle = (source + branch.reshape(own_shape)) * root_half
    token_sum, token_square = token_total(jnp.sum(middle, axis=3), jnp.sum(middle * middle, axis=3))
    token_center = token_sum / C
    token_inverse = lax.rsqrt(token_square / C - token_center * token_center + 1e-05)[..., None]
    token_scaled = (middle - token_center[..., None]) * token_inverse
    normed = full_channels((token_scaled * layer_gain + layer_bias).astype(jnp.bfloat16)).reshape(
        map_count, token_count, C
    )
    projected = jnp.einsum(
        "mnc,pcd->pmnd", normed, in_maps, preferred_element_type=jnp.float32
    ).astype(jnp.bfloat16)
    heads_shape = (map_count, token_count, head_count, HEAD_DIM)
    text_shape = (map_count, TEXT, head_count, HEAD_DIM)
    query = projected[0].reshape(heads_shape)
    keys = projected[1].reshape(heads_shape)
    values = projected[2].reshape(heads_shape)
    cross_query = projected[3].reshape(heads_shape)
    cross_keys = text_proj[0].reshape(text_shape)
    cross_values = text_proj[1].reshape(text_shape)
    attended, log_sums = attend_forward(query, keys, values)
    attended_low = attended.astype(jnp.bfloat16).reshape(map_count, token_count, width_own)
    cross_scores = (
        jnp.einsum("mqhd,mkhd->mqhk", cross_query, cross_keys, preferred_element_type=jnp.float32)
        * score_scale
    )
    cross_probs = jax.nn.softmax(jnp.where(present[:, None, None, :], cross_scores, -1e30), axis=-1)
    crossed = jnp.einsum(
        "mqhk,mkhd->mqhd",
        cross_probs.astype(jnp.bfloat16),
        cross_values,
        preferred_element_type=jnp.float32,
    )
    crossed_low = crossed.astype(jnp.bfloat16).reshape(map_count, token_count, width_own)
    mixed = jnp.einsum(
        "mnh,hc->mnc", attended_low, self_out, preferred_element_type=jnp.float32
    ) + jnp.einsum("mnh,hc->mnc", crossed_low, cross_out, preferred_element_type=jnp.float32)
    result = middle + own_part(mixed.reshape(map_count, row_count, col_count, C))
    grad_full = full_channels(cotangent.astype(jnp.bfloat16)).reshape(map_count, token_count, C)
    out_self_part = jnp.einsum(
        "mnh,mnc->hc", attended_low, grad_full, preferred_element_type=jnp.float32
    )
    out_cross_part = jnp.einsum(
        "mnh,mnc->hc", crossed_low, grad_full, preferred_element_type=jnp.float32
    )
    grad_attended = (
        jnp.einsum("mnc,hc->mnh", grad_full, self_out, preferred_element_type=jnp.float32)
        .astype(jnp.bfloat16)
        .reshape(heads_shape)
    )
    grad_crossed = (
        jnp.einsum("mnc,hc->mnh", grad_full, cross_out, preferred_element_type=jnp.float32)
        .astype(jnp.bfloat16)
        .reshape(heads_shape)
    )
    deltas = jnp.sum(grad_attended.astype(jnp.float32) * attended, axis=-1)
    grad_query = query_grads(query, grad_attended, log_sums, deltas, keys, values).astype(
        jnp.bfloat16
    )
    grad_keys, grad_values = key_grads(
        keys, values, query.astype(jnp.float32), grad_attended.astype(jnp.float32), log_sums, deltas
    )
    grad_cross_probs = jnp.einsum(
        "mqhd,mkhd->mqhk", grad_crossed, cross_values, preferred_element_type=jnp.float32
    )
    grad_cross_scores = cross_probs * (
        grad_cross_probs - jnp.sum(cross_probs * grad_cross_probs, axis=-1, keepdims=True)
    )
    grad_cross_low = grad_cross_scores.astype(jnp.bfloat16)
    grad_cross_query = (
        jnp.einsum(
            "mqhk,mkhd->mqhd", grad_cross_low, cross_keys, preferred_element_type=jnp.float32
        )
        * score_scale
    ).astype(jnp.bfloat16)
    grad_cross_keys = (
        jnp.einsum(
            "mqhk,mqhd->mkhd", grad_cross_low, cross_query, preferred_element_type=jnp.float32
        )
        * score_scale
    )
    grad_cross_values = jnp.einsum(
        "mqhk,mqhd->mkhd",
        cross_probs.astype(jnp.bfloat16),
        grad_crossed,
        preferred_element_type=jnp.float32,
    )
    text_grads = jnp.stack([grad_cross_keys, grad_cross_values]).reshape(
        2, map_count, TEXT, width_own
    )
    grad_projected = jnp.stack(
        [
            grad_query,
            grad_keys.astype(jnp.bfloat16),
            grad_values.astype(jnp.bfloat16),
            grad_cross_query,
        ]
    ).reshape(4, map_count, token_count, width_own)
    in_part = jnp.einsum(
        "mnc,pmnd->pcd", normed, grad_projected, preferred_element_type=jnp.float32
    )
    grad_normed = own_part(
        jnp.einsum(
            "pmnd,pcd->mnc", grad_projected, in_maps, preferred_element_type=jnp.float32
        ).reshape(map_count, row_count, col_count, C)
    )
    layer_gain_part = jnp.sum(grad_normed * token_scaled, axis=(0, 1, 2))
    layer_bias_part = jnp.sum(grad_normed, axis=(0, 1, 2))
    grad_scaled = grad_normed * layer_gain
    plain_sum, dot_sum = token_total(
        jnp.sum(grad_scaled, axis=3), jnp.sum(grad_scaled * token_scaled, axis=3)
    )
    grad_middle = (
        token_inverse
        * (grad_scaled - plain_sum[..., None] / C - token_scaled * dot_sum[..., None] / C)
        + cotangent
    )
    grad_two = (grad_middle * root_half).astype(jnp.bfloat16)
    grad_two = grad_two.reshape(flat)
    grad_second = convolve_back(spot, grad_two, kernel_two, row_count, col_count)
    grad_second = grad_second.reshape(own_shape)
    grad_lifted, gain_two, bias_two, layer_gain_sum, layer_bias_sum = group_backward(
        grad_second * silu_slope(second_normed),
        second_scaled,
        group_gain[1],
        second_inverse,
        pixel_count,
        layer_gain_part[None],
        layer_bias_part[None],
    )
    grad_film = jnp.stack(
        [jnp.sum(grad_lifted * inner, axis=(1, 2)), jnp.sum(grad_lifted, axis=(1, 2))], axis=1
    )
    film_all = total(grad_film, "wide")
    text_all = lax.psum(text_grads.astype(jnp.bfloat16), "wide").astype(jnp.float32)
    time_grad = jnp.einsum(
        "mk,msc->ksc", own_features.astype(jnp.float32), film_all, precision=highest
    )
    text_grad = jnp.einsum(
        "mx,msc->xsc", own_pooled.astype(jnp.float32), film_all, precision=highest
    )
    kv_grad = jnp.einsum("mtx,pmtd->pxd", own_text.astype(jnp.float32), text_all, precision=highest)
    grad_one = (grad_lifted * (1.0 + film_scale)).astype(jnp.bfloat16)
    grad_one = grad_one.reshape(flat)
    grad_first = convolve_back(spot, grad_one, kernel_one, row_count, col_count)
    grad_first = grad_first.reshape(own_shape)
    if has_slots():
        conv_grad = kernel_grad(spot, second_sends, grad_two, row_count, col_count, 1, None)
        conv_grad = kernel_grad(spot, first_sends, grad_one, row_count, col_count, 0, conv_grad)
    else:
        conv_grad = jnp.stack(
            [
                kernel_grad_whole(first_sends, grad_one, row_count, col_count),
                kernel_grad_whole(second_sends, grad_two, row_count, col_count),
            ]
        )
    empty_rows = jnp.zeros((0, width_own), jnp.float32)
    grad_source, gain_one, bias_one, unused_first, unused_second = group_backward(
        grad_first * silu_slope(first_normed),
        first_scaled,
        group_gain[0],
        first_inverse,
        pixel_count,
        empty_rows,
        empty_rows,
    )
    pixels_grad = grad_source + grad_middle * root_half
    parts = (
        lax.psum_scatter(
            in_part.astype(jnp.bfloat16), "wide", scatter_dimension=1, tiled=True
        ).astype(jnp.float32),
        lax.psum_scatter(
            jnp.concatenate([out_self_part, out_cross_part]).astype(jnp.bfloat16),
            "wide",
            scatter_dimension=1,
            tiled=True,
        ).astype(jnp.float32),
    )
    return (
        result,
        pixels_grad,
        conv_grad,
        time_grad,
        text_grad,
        jnp.stack([gain_one, gain_two]),
        jnp.stack([bias_one, bias_two]),
        layer_gain_sum[0],
        layer_bias_sum[0],
        parts[0],
        kv_grad,
        parts[1][:width_own],
        parts[1][width_own:],
    )


def solution(mesh):
    placed = (
        P(None, "wide", None, "tensor"),
        P(),
        P(),
        P(),
        P(None, None, "wide", "tensor"),
        P("wide", None, "tensor"),
        P("wide", None, "tensor"),
        P(None, "tensor"),
        P(None, "tensor"),
        P("tensor"),
        P("tensor"),
        P(None, "wide", "tensor"),
        P(None, "wide", "tensor"),
        P("tensor", "wide"),
        P("tensor", "wide"),
        P(None, "wide", None, "tensor"),
    )
    return jax.shard_map(
        shards,
        mesh=mesh,
        in_specs=placed,
        out_specs=(
            P(None, "wide", None, "tensor"),
            P(None, "wide", None, "tensor"),
            P(None, None, "wide", "tensor"),
            P("wide", None, "tensor"),
            P("wide", None, "tensor"),
            P(None, "tensor"),
            P(None, "tensor"),
            P("tensor"),
            P("tensor"),
            P(None, "wide", "tensor"),
            P(None, "wide", "tensor"),
            P("tensor", "wide"),
            P("tensor", "wide"),
        ),
        check_vma=False,
    )
```

```python
import functools
import math

import jax
import jax.numpy as jnp
from jax import lax
from jax.experimental import pallas as pl
from jax.experimental.pallas import tpu as pltpu
from jax.sharding import PartitionSpec as P

C = 1024
GROUPS = 32
HEAD_DIM = 128
TEXT = 128
TEMB = 1024
MIB = 1 << 20
in_vmem = pl.BlockSpec(memory_space=pltpu.VMEM)
in_smem = pl.BlockSpec(memory_space=pltpu.SMEM)


def local_kernel(body, outs, operands, scratch, limit, flops, aliases=None, out_specs=None):
    size = sum(a.size * a.dtype.itemsize for a in operands)
    size += sum(math.prod(o.shape) * o.dtype.itemsize for o in outs)
    return pl.pallas_call(
        body,
        grid=(1,),
        out_shape=outs,
        in_specs=[in_smem] + [in_vmem] * (len(operands) - 1),
        out_specs=[in_vmem] * len(outs) if out_specs is None else out_specs,
        scratch_shapes=scratch,
        input_output_aliases={} if aliases is None else aliases,
        compiler_params=pltpu.CompilerParams(vmem_limit_bytes=limit * MIB),
        cost_estimate=pl.CostEstimate(flops=flops, bytes_accessed=size, transcendentals=0),
    )(*operands)


def turned(values, width):
    rows = values.shape[0]
    wide = values.astype(jnp.float32)
    column = lax.rem(lax.broadcasted_iota(jnp.int32, values.shape, 0), width)
    before = jnp.where(column == 0, 0.0, pltpu.roll(wide, 1, 0))
    after = jnp.where(column == width - 1, 0.0, pltpu.roll(wide, rows - 1, 0))
    return before.astype(jnp.bfloat16), values, after.astype(jnp.bfloat16)


def halves_swapped(values, odd):
    half = values.shape[1] // 2
    other = jnp.concatenate([values[:, half:], values[:, :half]], axis=1)
    return jnp.where(odd, other, values)


class Weights:
    def __init__(self, refs, spot, axis=0):
        self.refs = refs
        self.axis = axis
        self.paired = len(refs) > 1
        self.wide = spot[0]
        self.odd = lax.rem(spot[0], 2) == 1

    def block(self, chunk):
        return lax.bitwise_xor(lax.div(self.wide, 2), chunk) if self.paired else chunk

    def tap(self, chunk, position):
        if not self.paired:
            span = self.refs[0].shape[1 + self.axis] // 4
            part = slice(chunk * span, (chunk + 1) * span)
            return self.refs[0][(position, slice(None), part) if self.axis else (position, part)]
        parts = []
        for refs in (self.refs[:5], self.refs[5:]):
            if chunk < 3:
                parts.append(refs[chunk][position])
            else:
                first = refs[3].shape[0]
                parts.append(refs[3][position] if position < first else refs[4][position - first])
        return jnp.concatenate(parts, axis=self.axis)

    def ordered(self, values):
        return halves_swapped(values, self.odd) if self.paired else values


def conv_body(groups, parts, rows, width, spot, *refs):
    pieces = refs[:groups]
    top, bottom = refs[groups : groups + 2]
    weights = Weights(refs[groups + 2 : groups + 2 + parts], spot)
    source, first_out, second_out, *sends, frame = refs[groups + 2 + parts :]
    span = pieces[0].shape[1]
    for mask in range(groups):
        block = lax.bitwise_xor(spot[1], mask)
        own = pieces[mask][...]
        lanes = slice(mask * span, (mask + 1) * span)
        framed = jnp.concatenate([top[:, lanes], own, bottom[:, lanes]], axis=0)
        for column, values in enumerate(turned(weights.ordered(framed), width)):
            frame[block, column] = values
    total_sum = jnp.zeros(first_out.shape, jnp.float32)
    for chunk in range(groups):
        block = weights.block(chunk)
        for position in range(9):
            start = (position // 3) * width
            window = frame[block, position % 3, start : start + rows * width, :]
            total_sum += jnp.dot(
                window, weights.tap(chunk, position), preferred_element_type=jnp.float32
            )
        center = frame[block, 1, width : (rows + 1) * width, :]
        if weights.paired:
            sends[2 * chunk][...] = center[:, : span // 2]
            sends[2 * chunk + 1][...] = center[:, span // 2 :]
        else:
            sends[0][:, chunk * span : (chunk + 1) * span] = center
    if second_out.shape[0] == 2:
        first_out[...] = total_sum
        second_out[...] = channel_sums(total_sum)
    else:
        middle = (source[...].astype(jnp.float32) + total_sum) * root_half
        first_out[...] = middle
        second_out[...] = middle.astype(jnp.bfloat16)


def back_body(groups, rows, width, spot, grad, top, bottom, *refs):
    frame, held = refs[-2:]
    outs = refs[-2 - groups : -2]
    weights = Weights(refs[: -2 - groups], spot)
    framed = jnp.concatenate([top[...], grad[...], bottom[...]], axis=0)
    for column, values in enumerate(turned(framed, width)):
        frame[column] = values
    for chunk in range(groups):
        total_sum = jnp.zeros(held.shape[1:], jnp.float32)
        for position in range(9):
            start = (2 - position // 3) * width
            total_sum += lax.dot_general(
                frame[2 - position % 3, start : start + rows * width, :],
                weights.tap(chunk, position),
                (((1,), (1,)), ((), ())),
                preferred_element_type=jnp.float32,
            )
        held[weights.block(chunk)] = weights.ordered(total_sum).astype(jnp.bfloat16)
    for mask in range(groups):
        outs[mask][...] = held[lax.bitwise_xor(spot[1], mask)]


def bf16_like(*shape):
    return jax.ShapeDtypeStruct(shape, jnp.bfloat16)


def f32_like(*shape):
    return jax.ShapeDtypeStruct(shape, jnp.float32)


def flipped(values, axis, mask):
    count = lax.axis_size(axis)
    return lax.ppermute(values, axis, [(i, i ^ mask) for i in range(count)])


def spread_slots(values, first):
    over_x, over_y = flipped(values, "wide", 2), flipped(values, "wide", 4)
    low, high = flipped(over_x[:first], "wide", 4), flipped(over_y[first:], "wide", 2)
    mine = [values, over_x, over_y, low, high]
    return mine + [flipped(part, "wide", 1) for part in mine]


def has_slots():
    return lax.axis_size("wide") == 8


def after(value, *others):
    return lax.optimization_barrier((value, others))[0]


def gathered_grads(grad, first):
    return spread_slots(grad, first) if has_slots() else [grad]


def gathered_blocks(blocks, first, axis=1):
    if has_slots():
        return spread_slots(blocks, first)
    return [lax.all_gather(blocks, "wide", axis=axis, tiled=True)]


def spread_chips(values, first):
    if has_slots():
        over_x, over_y = flipped(values, "wide", 2), flipped(values, "wide", 4)
        low, high = flipped(over_x[:first], "wide", 4), flipped(over_y[first:], "wide", 2)
        return [values, over_x, over_y, low, high]
    mask = 2
    while mask < lax.axis_size("wide"):
        values = jnp.concatenate([values, flipped(values, "wide", mask)])
        mask *= 2
    return [values]


def spread_stats(values):
    if has_slots():
        over_x, over_y = flipped(values, "wide", 2), flipped(values, "wide", 4)
        return [values, over_x, over_y, flipped(over_x, "wide", 4)]
    mask = 2
    while mask < lax.axis_size("wide"):
        values = jnp.concatenate([values, flipped(values, "wide", mask)], axis=1)
        mask *= 2
    return [values]


def channel_pieces(values):
    count = lax.axis_size("tensor")
    return [values] + [flipped(values, "tensor", mask) for mask in range(1, count)]


def edge_rows(last, first):
    count = lax.axis_size("wide")
    above = lax.ppermute(last, "wide", [(i, i + 1) for i in range(count - 1)])
    below = lax.ppermute(first, "wide", [(i + 1, i) for i in range(count - 1)])
    return above, below


def convolve(spot, pieces, edges, kernel, source, second_shape, rows, width):
    groups, (area, span) = len(pieces), pieces[0].shape
    sends = [bf16_like(area, span // 2)] * (2 * groups) if has_slots() else [bf16_like(area, C)]
    return local_kernel(
        functools.partial(conv_body, groups, len(kernel), rows, width),
        [f32_like(area, span), second_shape] + sends,
        [spot, *pieces, *edges, *kernel, source],
        [pltpu.VMEM((groups, 3, (rows + 2) * width, span), jnp.bfloat16)],
        32,
        2 * 9 * area * C * span,
    )


def piece_edges(pieces, width):
    return edge_rows(
        jnp.concatenate([piece[-width:] for piece in pieces], axis=1),
        jnp.concatenate([piece[:width] for piece in pieces], axis=1),
    )


def convolve_back(spot, grad, edges, kernel, rows, width):
    groups, (area, span) = lax.axis_size("tensor"), grad.shape
    return local_kernel(
        functools.partial(back_body, groups, rows, width),
        [bf16_like(area, span)] * groups,
        [spot, grad, *edges, *kernel],
        [
            pltpu.VMEM((3, (rows + 2) * width, span), jnp.bfloat16),
            pltpu.VMEM((groups, area, span), jnp.bfloat16),
        ],
        32,
        2 * 9 * area * C * span,
    )


def sent_parts(parts):
    return [parts[0]] + [flipped(parts[mask], "tensor", mask) for mask in range(1, len(parts))]


def kernel_grad_body(count, width, spot, *refs):
    pieces = refs[:count]
    grads = refs[count : count + 10]
    out, turned_all, grad_all = refs[-3:]
    wide = spot[0]
    area, span = pieces[0].shape
    depth = count * area
    turned_all[:, :width] = jnp.zeros((3 * span, width), jnp.bfloat16)
    turned_all[:, depth + width :] = jnp.zeros((3 * span, width), jnp.bfloat16)
    for mask in range(count):
        start = pl.multiple_of(lax.bitwise_xor(wide, mask) * area, area)
        for column, values in enumerate(turned(pieces[mask][...], width)):
            flat = jnp.transpose(values.astype(jnp.float32)).astype(jnp.bfloat16)
            turned_all[column * span : (column + 1) * span, pl.ds(start + width, area)] = flat
        half = grads[5 * (mask % 2) : 5 * (mask % 2) + 5]
        if mask < 6:
            grad_all[pl.ds(start, area), :] = half[mask // 2][...]
        else:
            grad_all[pl.ds(start, width), :] = half[3][...]
            grad_all[pl.ds(start + width, area - width), :] = half[4][...]
    for row in range(3):
        product = jnp.dot(
            turned_all[:, row * width : row * width + depth],
            grad_all[...],
            preferred_element_type=jnp.float32,
        )
        for column in range(3):
            out[0, 3 * row + column] = product[column * span : (column + 1) * span, :]


def swapped_blocks(sends):
    if not has_slots():
        return sends
    return [sends[0]] + [flipped(sends[mask], "wide", mask) for mask in range(1, len(sends))]


def kernel_grad(spot, pieces, grads, rows, width, layer, earlier):
    count, area = len(pieces), rows * width
    span, columns = pieces[0].shape[1], grads[0].shape[1]
    operands = [spot, *pieces, *grads]
    specs = [in_smem] + [in_vmem] * (len(operands) - 1)
    shape = f32_like(2, 9, span, columns)
    if earlier is not None:
        operands.append(earlier)
        specs.append(pl.BlockSpec(memory_space=pl.ANY))
    return pl.pallas_call(
        functools.partial(kernel_grad_body, count, width),
        out_shape=shape,
        in_specs=specs,
        grid=(1,),
        out_specs=pl.BlockSpec((1, 9, span, columns), lambda i: (layer, 0, 0, 0)),
        scratch_shapes=[
            pltpu.VMEM((3 * span, count * area + 2 * width), jnp.bfloat16),
            pltpu.VMEM((count * area, columns), jnp.bfloat16),
        ],
        input_output_aliases={} if earlier is None else {len(operands) - 1: 0},
        compiler_params=pltpu.CompilerParams(vmem_limit_bytes=24 * MIB),
        cost_estimate=pl.CostEstimate(
            flops=2 * 9 * count * area * span * columns, bytes_accessed=4 * MIB, transcendentals=0
        ),
    )(*operands)


def kernel_grad_whole(sends, grad, rows, width):
    natural = sends[0].reshape(1, rows, width, C)
    swapped = lax.all_to_all(natural, "wide", split_axis=3, concat_axis=1, tiled=True)
    framed = jnp.pad(swapped, ((0, 0), (1, 1), (1, 1), (0, 0)))
    low = lax.all_gather(
        grad.reshape(1, rows, width, grad.shape[1]), "wide", axis=1, tiled=True
    )
    return jnp.stack(
        [
            jnp.einsum(
                "mrwc,mrwd->cd",
                framed[:, tap // 3 : tap // 3 + low.shape[1], tap % 3 : tap % 3 + width, :],
                low,
                preferred_element_type=jnp.float32,
            )
            for tap in range(9)
        ]
    )


root_half = 1.0 / math.sqrt(2.0)
highest = lax.Precision.HIGHEST


def sinusoid(steps):
    half_width = TEMB // 2
    frequency = jnp.exp(-math.log(10000.0) * jnp.arange(half_width, dtype=jnp.float32) / half_width)
    angles = steps.astype(jnp.float32)[:, None] * frequency[None, :]
    return jnp.concatenate([jnp.cos(angles), jnp.sin(angles)], axis=1)


def total(values, axis):
    mask = 1
    while mask < lax.axis_size(axis):
        values = values + flipped(values, axis, mask)
        mask *= 2
    return values


def silu_slope(values):
    logistic = lax.logistic(values)
    return logistic * (1.0 + values * (1.0 - logistic))


def channel_sums(values):
    return jnp.concatenate(
        [
            jnp.sum(values, axis=0, keepdims=True),
            jnp.sum(values * values, axis=0, keepdims=True),
        ],
        axis=0,
    )


def group_means(first, second, pixel_count):
    channels = first.shape[1]
    per_group = C // GROUPS
    row = lax.div(lax.broadcasted_iota(jnp.int32, (channels, channels), 0), per_group)
    column = lax.div(lax.broadcasted_iota(jnp.int32, (channels, channels), 1), per_group)
    same = jnp.where(row == column, 1.0, 0.0)
    rows = jnp.concatenate([first, second, jnp.zeros((6, channels), jnp.float32)], axis=0)
    means = jnp.dot(rows, same, precision=highest, preferred_element_type=jnp.float32)
    means = means / (pixel_count * per_group)
    return means[0:1], means[1:2]


def group_scale(first, second, pixel_count):
    center, square = group_means(first, second, pixel_count)
    return center, lax.rsqrt(square - center * center + 1e-05)


def lifted_sums(sums, film, pixel_count):
    slope, shift = 1.0 + film[0:1], film[1:2]
    plain, square = sums[0:1], sums[1:2]
    return (
        slope * plain + pixel_count * shift,
        slope * slope * square + 2.0 * slope * shift * plain + pixel_count * shift * shift,
    )


def silu_low(values):
    return (values * lax.logistic(values)).astype(jnp.bfloat16)


def first_norm_body(pixel_count, spot, pixels, sums, affine, out):
    center, inverse = group_scale(sums[0:1], sums[1:2], pixel_count)
    scaled = (pixels[...].astype(jnp.float32) - center) * inverse
    out[...] = silu_low(scaled * affine[0:1] + affine[1:2])


def second_norm_body(pixel_count, spot, inner, sums, film, affine, out):
    center, inverse = group_scale(*lifted_sums(sums[...], film[...], pixel_count), pixel_count)
    lifted = inner[...] * (1.0 + film[0:1]) + film[1:2]
    out[...] = silu_low((lifted - center) * inverse * affine[0:1] + affine[1:2])


def parts_sum(refs):
    summed = refs[0][...].astype(jnp.float32)
    for ref in refs[1:]:
        summed += ref[...].astype(jnp.float32)
    return summed


def stacked_rows(rows):
    return jnp.concatenate([jnp.sum(row, axis=0, keepdims=True) for row in rows], axis=0)


def second_back_body(groups, pixel_count, spot, *refs):
    inner, sums, film, affine, terms, out, rows = refs[groups:]
    center, inverse = group_scale(*lifted_sums(sums[...], film[...], pixel_count), pixel_count)
    own = inner[...]
    scaled = (own * (1.0 + film[0:1]) + film[1:2] - center) * inverse
    back = parts_sum(refs[:groups]) * silu_slope(scaled * affine[0:1] + affine[1:2])
    out[...] = back
    rows[0:3, :] = stacked_rows([back * scaled, back, back * own])
    rows[3:5, :] = terms[...]
    rows[5:8, :] = jnp.zeros((3, own.shape[1]), jnp.float32)


def second_input_body(pixel_count, width, spot, back, inner, sums, film, affine, rows, *outs):
    low, last, first, film_rows = outs
    slope, shift, gain = 1.0 + film[0:1], film[1:2], affine[0:1]
    plain_sum, square_sum = sums[0:1], sums[1:2]
    lifted_sum, lifted_square = lifted_sums(sums[...], film[...], pixel_count)
    center, inverse = group_scale(lifted_sum, lifted_square, pixel_count)
    dotted, plain = group_means(gain * rows[0:1], gain * rows[1:2], pixel_count)
    scaled = (inner[...] * slope + shift - center) * inverse
    grad = inverse * (back[...] * gain - plain - scaled * dotted)
    grad_low = (grad * slope).astype(jnp.bfloat16)
    low[...] = grad_low
    last[...] = grad_low[-width:]
    first[...] = grad_low[:width]
    scaled_sum = inverse * (lifted_sum - pixel_count * center)
    scaled_inner = inverse * (slope * square_sum + (shift - center) * plain_sum)
    film_rows[0:1, :] = inverse * (
        gain * rows[2:3] - plain * plain_sum - dotted * scaled_inner
    )
    film_rows[1:2, :] = inverse * (
        gain * rows[1:2] - pixel_count * plain - dotted * scaled_sum
    )


def first_back_body(groups, pixel_count, spot, *refs):
    pixels, sums, affine, out, rows = refs[groups:]
    center, inverse = group_scale(sums[0:1], sums[1:2], pixel_count)
    scaled = (pixels[...].astype(jnp.float32) - center) * inverse
    back = parts_sum(refs[:groups]) * silu_slope(scaled * affine[0:1] + affine[1:2])
    out[...] = back
    rows[...] = stacked_rows([back * scaled, back])


def first_input_body(pixel_count, spot, back, pixels, sums, affine, rows, middle, out):
    gain = affine[0:1]
    center, inverse = group_scale(sums[0:1], sums[1:2], pixel_count)
    dotted, plain = group_means(gain * rows[0:1], gain * rows[1:2], pixel_count)
    scaled = (pixels[...].astype(jnp.float32) - center) * inverse
    out[...] = inverse * (back[...] * gain - plain - scaled * dotted) + middle[...] * root_half


def dot(left, right):
    return jnp.dot(left, right, preferred_element_type=jnp.float32)


def dot_last(left, right):
    return lax.dot_general(
        left, right, (((1,), (1,)), ((), ())), preferred_element_type=jnp.float32
    )


def flat_turn(values):
    return jnp.transpose(values.astype(jnp.float32)).astype(jnp.bfloat16)


def dot_first(left, right):
    return dot(flat_turn(left), right)


def head_choice(values, odd):
    first, second = values[:, :HEAD_DIM], values[:, HEAD_DIM:]
    return jnp.where(odd, second, first), jnp.where(odd, first, second)


def heads_joined(kept, received, odd):
    return jnp.where(
        odd,
        jnp.concatenate([received, kept], axis=1),
        jnp.concatenate([kept, received], axis=1),
    )


def project_body(groups, parts, spot, *refs):
    pieces, gains = refs[:groups], refs[groups : 2 * groups]
    own = refs[2 * groups]
    weights = Weights(refs[2 * groups + 1 : 2 * groups + 1 + parts], spot)
    keep_q, keep_kv, send, cross, normed, scaled, center, inverse = refs[2 * groups + 1 + parts :]
    odd = lax.rem(spot[0], 2) == 1
    token_sum = token_square = 0.0
    for piece in pieces:
        values = piece[...].astype(jnp.float32)
        token_sum += jnp.sum(values, axis=1, keepdims=True)
        token_square += jnp.sum(values * values, axis=1, keepdims=True)
    mean = token_sum / C
    scale = lax.rsqrt(token_square / C - mean * mean + 1e-05)
    for mask in range(groups):
        values = (pieces[mask][...].astype(jnp.float32) - mean) * scale
        values = (values * gains[mask][0:1] + gains[mask][1:2]).astype(jnp.bfloat16)
        normed[lax.bitwise_xor(spot[1], mask)] = weights.ordered(values)
    center[...] = mean
    inverse[...] = scale
    scaled[...] = (own[...] - mean) * scale
    projected = []
    for position in range(4):
        total_sum = 0.0
        for chunk in range(groups):
            total_sum += dot(normed[weights.block(chunk)], weights.tap(chunk, position))
        projected.append(total_sum.astype(jnp.bfloat16))
    cross[...] = projected[3]
    chosen = [head_choice(values, odd) for values in projected[:3]]
    keep_q[...] = chosen[0][0]
    keep_kv[...] = jnp.concatenate([chosen[1][0], chosen[2][0]], axis=1)
    send[...] = jnp.concatenate([pair[1] for pair in chosen], axis=1)


def out_grad_body(groups, parts, spot, *refs):
    pieces = refs[:groups]
    weights = Weights(refs[groups : groups + parts], spot, 1)
    keep, send, cross, frame = refs[groups + parts :]
    for mask in range(groups):
        frame[lax.bitwise_xor(spot[1], mask)] = weights.ordered(pieces[mask][...])
    sums = []
    for position in range(2):
        total_sum = 0.0
        for chunk in range(groups):
            total_sum += dot_last(frame[weights.block(chunk)], weights.tap(chunk, position))
        sums.append(total_sum.astype(jnp.bfloat16))
    kept, sent = head_choice(sums[0], lax.rem(spot[0], 2) == 1)
    keep[...] = kept
    send[...] = sent
    cross[...] = sums[1]


def mix_body(groups, parts, spot, kept, received, crossed, *refs):
    weights = Weights(refs[:parts], spot, 1)
    outs, held = refs[parts:-1], refs[-1]
    attended = heads_joined(kept[...], received[...], lax.rem(spot[0], 2) == 1)
    for chunk in range(groups):
        total_sum = dot(attended, weights.tap(chunk, 0)) + dot(crossed[...], weights.tap(chunk, 1))
        held[weights.block(chunk)] = weights.ordered(total_sum).astype(jnp.bfloat16)
    for mask in range(groups):
        outs[mask][...] = held[lax.bitwise_xor(spot[1], mask)]


def over_rows(refs, step, state):
    for index, ref in enumerate(refs):
        rows = ref.shape[0]
        if rows <= 512:
            state = step(state, ref[...], index, 0)
        else:
            state = lax.fori_loop(
                0,
                rows // 512,
                lambda i, held: step(
                    held, ref[pl.ds(pl.multiple_of(i * 512, 512), 512), :], index, i * 512
                ),
                state,
            )
    return state


score_scale = HEAD_DIM ** (-0.5)


def attend_body(count, spot, query_grad, *refs):
    pairs = refs[:count]
    keep, send, stats = refs[count:]
    query, grad = query_grad[:, :HEAD_DIM], query_grad[:, HEAD_DIM:]
    queries = query.shape[0]

    def step(state, pair, index, start):
        top, weight_sum, weighted = state
        scores = dot_last(pair[:, :HEAD_DIM], query) * score_scale
        raised = jnp.maximum(top, jnp.max(scores, axis=0, keepdims=True))
        rescale = jnp.exp(top - raised)
        weights = jnp.exp(scores - raised)
        weight_sum = weight_sum * rescale + jnp.sum(weights, axis=0, keepdims=True)
        weighted = weighted * rescale + dot_first(pair[:, HEAD_DIM:], weights.astype(jnp.bfloat16))
        return raised, weight_sum, weighted

    top, weight_sum, weighted = over_rows(
        pairs,
        step,
        (
            jnp.full((1, queries), -1e30, jnp.float32),
            jnp.zeros((1, queries), jnp.float32),
            jnp.zeros((HEAD_DIM, queries), jnp.float32),
        ),
    )
    attended = weighted / weight_sum
    delta = jnp.sum(attended * jnp.transpose(grad.astype(jnp.float32)), axis=0, keepdims=True)
    stats[...] = jnp.concatenate([top + jnp.log(weight_sum), delta], axis=0)
    turned_back = jnp.transpose(attended).astype(jnp.bfloat16)
    keep[...] = turned_back[: queries // 2]
    send[...] = turned_back[queries // 2 :]


def query_grad_body(count, spot, query_grad, stats, *refs):
    pairs = refs[:count]
    keep, send = refs[count:]
    query, grad = query_grad[:, :HEAD_DIM], query_grad[:, HEAD_DIM:]
    queries = query.shape[0]
    log_sum, delta = stats[0:1, :], stats[1:2, :]

    def step(state, pair, index, start):
        scores = dot_last(pair[:, :HEAD_DIM], query) * score_scale
        probs = jnp.exp(scores - log_sum)
        grad_probs = dot_last(pair[:, HEAD_DIM:], grad)
        grad_scores = (probs * (grad_probs - delta)).astype(jnp.bfloat16)
        return state + dot_first(pair[:, :HEAD_DIM], grad_scores)

    flat = over_rows(pairs, step, jnp.zeros((HEAD_DIM, queries), jnp.float32))
    result = jnp.transpose(flat * score_scale).astype(jnp.bfloat16)
    keep[...] = result[: queries // 2]
    send[...] = result[queries // 2 :]


def key_grad_body(count, spot, pair, *refs):
    queries, stats = refs[:count], refs[count:-2]
    keep, send = refs[-2:]
    keys, values = pair[:, :HEAD_DIM], pair[:, HEAD_DIM:]
    depth = keys.shape[0]

    def step(state, block, index, start):
        grad_keys, grad_values = state
        rows = block.shape[0]
        if index < len(stats):
            lanes = pl.ds(start if isinstance(start, int) else pl.multiple_of(start, 512), rows)
            log_sum, delta = stats[index][0:1, lanes], stats[index][1:2, lanes]
        else:
            log_sum, delta = stats[-1][0:1, rows:], stats[-1][1:2, rows:]
        query, grad = block[:, :HEAD_DIM], block[:, HEAD_DIM:]
        probs = jnp.exp(dot_last(keys, query) * score_scale - log_sum)
        grad_values += dot(probs.astype(jnp.bfloat16), grad)
        grad_scores = probs * (dot_last(values, grad) - delta)
        grad_keys += dot(grad_scores.astype(jnp.bfloat16), query)
        return grad_keys, grad_values

    zero = jnp.zeros((depth, HEAD_DIM), jnp.float32)
    grad_keys, grad_values = over_rows(queries, step, (zero, zero))
    both = jnp.concatenate([grad_keys * score_scale, grad_values], axis=1).astype(jnp.bfloat16)
    keep[...] = both[: depth // 2]
    send[...] = both[depth // 2 :]


def cross_body(spot, query, text, grad, crossed, grad_query, text_grad):
    live = lax.broadcasted_iota(jnp.int32, (query.shape[0], text.shape[1]), 1) < spot[2]
    for head in range(query.shape[1] // HEAD_DIM):
        lanes = slice(head * HEAD_DIM, (head + 1) * HEAD_DIM)
        own, keys, values, back = query[:, lanes], text[0, :, lanes], text[1, :, lanes], grad[:, lanes]
        scores = jnp.where(live, dot_last(own, keys) * score_scale, -1e30)
        weights = jnp.exp(scores - jnp.max(scores, axis=1, keepdims=True))
        probs = weights / jnp.sum(weights, axis=1, keepdims=True)
        low = probs.astype(jnp.bfloat16)
        crossed[:, lanes] = dot(low, values).astype(jnp.bfloat16)
        grad_probs = dot_last(back, values)
        grad_scores = probs * (grad_probs - jnp.sum(probs * grad_probs, axis=1, keepdims=True))
        grad_low = grad_scores.astype(jnp.bfloat16)
        grad_query[:, lanes] = (dot(grad_low, keys) * score_scale).astype(jnp.bfloat16)
        text_grad[0, :, lanes] = (dot_first(grad_low, own) * score_scale).astype(jnp.bfloat16)
        text_grad[1, :, lanes] = dot_first(low, back).astype(jnp.bfloat16)


def joined_grads(spot, kept_query, got_query, kept_pair, got_pair, cross):
    odd = lax.rem(spot[0], 2) == 1
    return [
        heads_joined(kept_query[...], got_query[...], odd),
        heads_joined(kept_pair[:, :HEAD_DIM], got_pair[:, :HEAD_DIM], odd),
        heads_joined(kept_pair[:, HEAD_DIM:], got_pair[:, HEAD_DIM:], odd),
        cross[...],
    ]


def project_back_body(groups, parts, spot, kq, gq, kp, gp, cross, center, inverse, *refs):
    pieces, gains = refs[:groups], refs[groups : 2 * groups]
    weights = Weights(refs[2 * groups : 2 * groups + parts], spot)
    *outs, sums, held = refs[2 * groups + parts :]
    grads = joined_grads(spot, kq, gq, kp, gp, cross)
    for chunk in range(groups):
        total_sum = 0.0
        for position in range(4):
            total_sum += dot_last(grads[position], weights.tap(chunk, position))
        held[weights.block(chunk)] = weights.ordered(total_sum)
    plain = dotted = 0.0
    ones = jnp.ones((8, held.shape[2]), jnp.float32)
    for mask in range(groups):
        part = held[lax.bitwise_xor(spot[1], mask)]
        outs[mask][...] = part.astype(jnp.bfloat16)
        eased = part * gains[mask][0:1]
        unit = (pieces[mask][...].astype(jnp.float32) - center[...]) * inverse[...]
        plain += eased
        dotted += eased * unit
    for row, values in enumerate((plain, dotted)):
        sums[row : row + 1, :] = lax.dot_general(
            ones,
            values,
            (((1,), (1,)), ((), ())),
            precision=highest,
            preferred_element_type=jnp.float32,
        )[0:1]


def weight_grad_body(groups, paired, spot, kq, gq, kp, gp, cross, kept, received, crossed, normed, *refs):
    cotangents, out = refs[:groups], refs[groups]
    odd = lax.rem(spot[0], 2) == 1
    area, span = cross.shape
    right = jnp.concatenate(joined_grads(spot, kq, gq, kp, gp, cross), axis=1)
    columns = right.shape[1]
    out_right = jnp.concatenate(
        [heads_joined(kept[...], received[...], odd), crossed[...]], axis=1
    )
    for chunk in range(groups):
        rows = slice(chunk * span, (chunk + 1) * span)
        values = normed[chunk]
        left = halves_swapped(values, odd) if paired else values
        out[rows, :columns] = dot_first(left, right).astype(jnp.bfloat16)
    for mask in range(groups):
        start = pl.multiple_of(lax.bitwise_xor(spot[1], mask) * span, span)
        out[pl.ds(start, span), columns:] = dot_first(cotangents[mask][...], out_right).astype(
            jnp.bfloat16
        )


def norm_back_body(groups, width, spot, *refs):
    sums, scaled, inverse, cotangent, gain, middle, low, last, first, terms = refs[groups:]
    grad = parts_sum(refs[:groups])
    area = grad.shape[0]
    same = lax.broadcasted_iota(jnp.int32, (area, area), 0) == lax.broadcasted_iota(
        jnp.int32, (area, area), 1
    )
    plain = jnp.sum(jnp.where(same, sums[0:1, :], 0.0), axis=1, keepdims=True) / C
    dotted = jnp.sum(jnp.where(same, sums[1:2, :], 0.0), axis=1, keepdims=True) / C
    unit = scaled[...]
    terms[0:1, :] = jnp.sum(grad * unit, axis=0, keepdims=True)
    terms[1:2, :] = jnp.sum(grad, axis=0, keepdims=True)
    back = inverse[...] * (grad * gain[...] - plain - unit * dotted) + cotangent[...]
    middle[...] = back
    grad_low = (back * root_half).astype(jnp.bfloat16)
    low[...] = grad_low
    last[...] = grad_low[-width:]
    first[...] = grad_low[:width]


def shards(
    pixels,
    text_states,
    text_length,
    timestep,
    conv_weights,
    film_time,
    film_text,
    group_gain,
    group_bias,
    layer_gain,
    layer_bias,
    attn_in,
    text_kv,
    out_self,
    out_cross,
    cotangent,
):
    map_count, row_count, col_count, width_own = pixels.shape
    token_count = row_count * col_count
    groups = lax.axis_size("tensor")
    pixel_count = token_count * lax.axis_size("wide")
    own_shape = (map_count, row_count, col_count, width_own)
    flat = (token_count, width_own)
    half = (token_count, HEAD_DIM)
    edge = (col_count, width_own)
    spot = jnp.stack([lax.axis_index("wide"), lax.axis_index("tensor"), text_length[0]])
    spot = spot.astype(jnp.int32)
    own_pixels = pixels.reshape(flat)
    flat_cotangent = cotangent.reshape(flat)
    affine = [jnp.stack([group_gain[layer], group_bias[layer]]) for layer in range(2)]

    first_sums = total(channel_sums(own_pixels.astype(jnp.float32)), "wide")
    norm_gains = channel_pieces(jnp.stack([layer_gain, layer_bias]))
    grad_pieces = channel_pieces(flat_cotangent.astype(jnp.bfloat16))
    kernel_one = gathered_blocks(after(conv_weights[0], first_sums), 5)

    features = sinusoid(timestep).astype(jnp.bfloat16)
    present = jnp.arange(TEXT)[None, :] < text_length[:, None]
    pooled = jnp.einsum(
        "mtx,mt->mx", text_states, present.astype(jnp.bfloat16), preferred_element_type=jnp.float32
    )
    pooled = (pooled / text_length.astype(jnp.float32)[:, None]).astype(jnp.bfloat16)
    wide_index = lax.axis_index("wide")
    time_rows = film_time.shape[0]
    text_rows = film_text.shape[0]
    own_features = lax.dynamic_slice_in_dim(features, wide_index * time_rows, time_rows, 1)
    own_pooled = lax.dynamic_slice_in_dim(pooled, wide_index * text_rows, text_rows, 1)
    own_text = lax.dynamic_slice_in_dim(text_states, wide_index * text_rows, text_rows, 2)
    film_term = jnp.einsum(
        "mk,ksc->msc", own_features, film_time, preferred_element_type=jnp.float32
    ) + jnp.einsum("mk,ksc->msc", own_pooled, film_text, preferred_element_type=jnp.float32)
    film = total(film_term[0], "wide")
    text_term = jnp.einsum("mtx,pxd->pmtd", own_text, text_kv, preferred_element_type=jnp.float32)
    text_term = text_term.astype(jnp.bfloat16).reshape(2, TEXT, width_own)

    (first,) = local_kernel(
        functools.partial(first_norm_body, pixel_count),
        [bf16_like(*flat)],
        [spot, own_pixels, first_sums, affine[0]],
        [],
        8,
        0,
    )
    pieces = channel_pieces(first)
    edges = piece_edges(pieces, col_count)
    inner, sums, *first_sends = convolve(
        spot, pieces, edges, kernel_one, own_pixels, f32_like(2, width_own), row_count, col_count
    )
    inner_sums = total(sums, "wide")
    kernel_two = gathered_blocks(after(conv_weights[1], inner_sums), 5)
    (second,) = local_kernel(
        functools.partial(second_norm_body, pixel_count),
        [bf16_like(*flat)],
        [spot, inner, inner_sums, film, affine[1]],
        [],
        8,
        0,
    )
    pieces = channel_pieces(second)
    edges = piece_edges(pieces, col_count)
    in_maps = gathered_blocks(after(attn_in, *kernel_two[:5], *edges), 2)
    text_proj = total(after(text_term, *in_maps[:5]), "wide")
    out_maps = gathered_blocks(after(jnp.stack([out_self, out_cross]), *in_maps[:5]), 1, 2)
    middle, middle_low, *second_sends = convolve(
        spot, pieces, edges, kernel_two, own_pixels, bf16_like(*flat), row_count, col_count
    )

    middle_pieces = channel_pieces(middle_low)
    parts = len(in_maps)
    column = f32_like(token_count, 1)
    square = 2 * token_count * C * width_own
    kept_query, kept_pair, sent, cross_query, normed, scaled, center, inverse = local_kernel(
        functools.partial(project_body, groups, parts),
        [
            bf16_like(*half),
            bf16_like(*flat),
            bf16_like(token_count, 3 * HEAD_DIM),
            bf16_like(*flat),
            bf16_like(groups, *flat),
            f32_like(*flat),
            column,
            column,
        ],
        [spot, *middle_pieces, *norm_gains, middle, *in_maps],
        [],
        24,
        4 * square,
    )
    got = flipped(sent, "wide", 1)
    kept_grad, sent_grad, grad_crossed = local_kernel(
        functools.partial(out_grad_body, groups, len(out_maps)),
        [bf16_like(*half), bf16_like(*half), bf16_like(*flat)],
        [spot, *grad_pieces, *out_maps],
        [pltpu.VMEM((groups, *flat), jnp.bfloat16)],
        16,
        2 * square,
    )
    got_grad = flipped(sent_grad, "wide", 1)
    pair = jnp.concatenate([kept_pair, got[:, HEAD_DIM:]])
    pairs = spread_chips(pair, token_count)
    query_grad = jnp.concatenate(
        [
            jnp.concatenate([kept_query, got[:, :HEAD_DIM]]),
            jnp.concatenate([kept_grad, got_grad]),
        ],
        axis=1,
    )
    query_grads = spread_chips(after(query_grad, *pairs), token_count)
    scores = 2 * (2 * token_count) * HEAD_DIM * pixel_count
    kept_out, sent_out, stats = local_kernel(
        functools.partial(attend_body, len(pairs)),
        [bf16_like(*half), bf16_like(*half), f32_like(2, 2 * token_count)],
        [spot, query_grad, *pairs],
        [],
        24,
        2 * scores,
    )
    all_stats = spread_stats(stats)
    got_out = flipped(sent_out, "wide", 1)
    crossed, grad_cross_query, text_grads = local_kernel(
        cross_body,
        [bf16_like(*flat), bf16_like(*flat), bf16_like(2, TEXT, width_own)],
        [spot, cross_query, text_proj, grad_crossed],
        [],
        8,
        12 * token_count * TEXT * width_own,
    )
    kept_dq, sent_dq = local_kernel(
        functools.partial(query_grad_body, len(pairs)),
        [bf16_like(*half), bf16_like(*half)],
        [spot, query_grad, stats, *pairs],
        [],
        24,
        3 * scores,
    )
    got_dq = flipped(sent_dq, "wide", 1)
    kept_dk, sent_dk = local_kernel(
        functools.partial(key_grad_body, len(query_grads)),
        [bf16_like(*flat), bf16_like(*flat)],
        [spot, pair, *query_grads, *all_stats],
        [],
        24,
        4 * scores,
    )
    got_dk = flipped(sent_dk, "wide", 1)
    text_all = total(after(text_grads, *all_stats), "wide").astype(jnp.float32)
    first_blocks = swapped_blocks([after(send, text_all) for send in first_sends])
    second_blocks = swapped_blocks([after(send, text_all) for send in second_sends])
    mixed = local_kernel(
        functools.partial(mix_body, groups, len(out_maps)),
        [bf16_like(*flat)] * groups,
        [spot, kept_out, got_out, crossed, *out_maps],
        [pltpu.VMEM((groups, *flat), jnp.bfloat16)],
        16,
        2 * square,
    )
    mixed = sent_parts(mixed)
    result = middle
    for part in mixed:
        result = result + part.astype(jnp.float32)
    projected_grads = [after(kept_dq, *mixed), got_dq, kept_dk, got_dk, grad_cross_query]
    *norm_parts, sums = local_kernel(
        functools.partial(project_back_body, groups, parts),
        [bf16_like(*flat)] * groups + [f32_like(2, token_count)],
        [spot, *projected_grads, center, inverse, *middle_pieces, *norm_gains, *in_maps],
        [pltpu.VMEM((groups, *flat), jnp.float32)],
        24,
        4 * square,
    )
    norm_parts = sent_parts(norm_parts)
    sums = total(sums, "tensor")
    (weight_parts,) = local_kernel(
        functools.partial(weight_grad_body, groups, has_slots()),
        [bf16_like(C, 6 * width_own)],
        [spot, *projected_grads, kept_out, got_out, crossed, normed, *grad_pieces],
        [],
        24,
        6 * square,
    )
    weight_sums = lax.psum_scatter(weight_parts, "wide", scatter_dimension=0, tiled=True)
    grad_middle, grad_two, last, head, terms = local_kernel(
        functools.partial(norm_back_body, groups, col_count),
        [
            f32_like(*flat),
            bf16_like(*flat),
            bf16_like(*edge),
            bf16_like(*edge),
            f32_like(2, width_own),
        ],
        [
            spot,
            *norm_parts,
            after(sums, weight_parts, first_blocks, second_blocks),
            scaled,
            inverse,
            flat_cotangent,
            layer_gain[None],
        ],
        [],
        16,
        0,
    )

    edges = edge_rows(last, head)
    grads_two = gathered_grads(after(grad_two, *edges), col_count)
    back_parts = sent_parts(
        convolve_back(spot, grad_two, edges, kernel_two, row_count, col_count)
    )
    back, rows = local_kernel(
        functools.partial(second_back_body, groups, pixel_count),
        [f32_like(*flat), f32_like(8, width_own)],
        [spot, *back_parts, inner, inner_sums, film, affine[1], terms],
        [],
        16,
        0,
    )
    second_rows = total(after(rows, *grads_two), "wide")
    grad_one, last, head, film_rows = local_kernel(
        functools.partial(second_input_body, pixel_count, col_count),
        [bf16_like(*flat), bf16_like(*edge), bf16_like(*edge), f32_like(2, width_own)],
        [spot, back, inner, inner_sums, film, affine[1], second_rows],
        [],
        16,
        0,
    )
    edges = edge_rows(last, head)
    grads_one = gathered_grads(after(grad_one, *edges), col_count)
    conv_grad = None
    if has_slots():
        conv_grad = kernel_grad(
            spot, second_blocks, grads_two, row_count, col_count, 1, conv_grad
        )
        second_rows = after(second_rows, conv_grad)
    time_grad = own_features.astype(jnp.float32)[0][:, None, None] * film_rows[None]
    text_grad = own_pooled.astype(jnp.float32)[0][:, None, None] * film_rows[None]
    kv_grad = jnp.einsum(
        "tx,ptd->pxd", own_text[0].astype(jnp.float32), text_all, precision=highest
    )
    back_parts = sent_parts(
        convolve_back(spot, grad_one, edges, kernel_one, row_count, col_count)
    )
    back, rows = local_kernel(
        functools.partial(first_back_body, groups, pixel_count),
        [f32_like(*flat), f32_like(2, width_own)],
        [spot, *back_parts, own_pixels, first_sums, affine[0]],
        [],
        16,
        0,
    )
    first_rows = total(rows, "wide")
    if has_slots():
        conv_grad = kernel_grad(
            spot, first_blocks, grads_one, row_count, col_count, 0, conv_grad
        )
    else:
        conv_grad = jnp.stack(
            [
                kernel_grad_whole(first_sends, grad_one, row_count, col_count),
                kernel_grad_whole(second_sends, grad_two, row_count, col_count),
            ]
        )
    (pixels_grad,) = local_kernel(
        functools.partial(first_input_body, pixel_count),
        [f32_like(*flat)],
        [spot, back, own_pixels, first_sums, affine[0], first_rows, grad_middle],
        [],
        16,
        0,
    )
    weight_sums = weight_sums.astype(jnp.float32)
    in_count = 4 * width_own
    attn_in_grad = jnp.moveaxis(weight_sums[:, :in_count].reshape(-1, 4, width_own), 1, 0)
    return (
        result.reshape(own_shape),
        pixels_grad.reshape(own_shape),
        conv_grad,
        time_grad,
        text_grad,
        jnp.stack([first_rows[0], second_rows[0]]),
        jnp.stack([first_rows[1], second_rows[1]]),
        second_rows[3],
        second_rows[4],
        attn_in_grad,
        kv_grad,
        weight_sums[:, in_count : in_count + width_own].T,
        weight_sums[:, in_count + width_own :].T,
    )


def solution(mesh):
    placed = (
        P(None, "wide", None, "tensor"),
        P(),
        P(),
        P(),
        P(None, None, "wide", "tensor"),
        P("wide", None, "tensor"),
        P("wide", None, "tensor"),
        P(None, "tensor"),
        P(None, "tensor"),
        P("tensor"),
        P("tensor"),
        P(None, "wide", "tensor"),
        P(None, "wide", "tensor"),
        P("tensor", "wide"),
        P("tensor", "wide"),
        P(None, "wide", None, "tensor"),
    )
    return jax.shard_map(
        shards,
        mesh=mesh,
        in_specs=placed,
        out_specs=(
            P(None, "wide", None, "tensor"),
            P(None, "wide", None, "tensor"),
            P(None, None, "wide", "tensor"),
            P("wide", None, "tensor"),
            P("wide", None, "tensor"),
            P(None, "tensor"),
            P(None, "tensor"),
            P("tensor"),
            P("tensor"),
            P(None, "wide", "tensor"),
            P(None, "wide", "tensor"),
            P("tensor", "wide"),
            P("tensor", "wide"),
        ),
        check_vma=False,
    )
```

```python
import functools
import math

import jax
import jax.numpy as jnp
from jax import lax
from jax.experimental import pallas as pl
from jax.experimental.pallas import tpu as pltpu
from jax.sharding import PartitionSpec as P

C = 1024
GROUPS = 32
HEAD_DIM = 128
TEXT = 128
TEMB = 1024
MIB = 1 << 20
in_vmem = pl.BlockSpec(memory_space=pltpu.VMEM)
in_smem = pl.BlockSpec(memory_space=pltpu.SMEM)


def local_kernel(body, outs, operands, scratch, limit, flops, aliases=None, out_specs=None):
    size = sum(a.size * a.dtype.itemsize for a in operands)
    size += sum(math.prod(o.shape) * o.dtype.itemsize for o in outs)
    return pl.pallas_call(
        body,
        grid=(1,),
        out_shape=outs,
        in_specs=[in_smem] + [in_vmem] * (len(operands) - 1),
        out_specs=[in_vmem] * len(outs) if out_specs is None else out_specs,
        scratch_shapes=scratch,
        input_output_aliases={} if aliases is None else aliases,
        compiler_params=pltpu.CompilerParams(vmem_limit_bytes=limit * MIB),
        cost_estimate=pl.CostEstimate(flops=flops, bytes_accessed=size, transcendentals=0),
    )(*operands)


def far(arrays):
    return [pltpu.with_memory_space_constraint(array, pltpu.HBM) for array in arrays]


def turned(values, width):
    rows = values.shape[0]
    wide = values.astype(jnp.float32)
    column = lax.rem(lax.broadcasted_iota(jnp.int32, values.shape, 0), width)
    before = jnp.where(column == 0, 0.0, pltpu.roll(wide, 1, 0))
    after = jnp.where(column == width - 1, 0.0, pltpu.roll(wide, rows - 1, 0))
    return before.astype(jnp.bfloat16), values, after.astype(jnp.bfloat16)


def halves_swapped(values, odd):
    half = values.shape[1] // 2
    other = jnp.concatenate([values[:, half:], values[:, :half]], axis=1)
    return jnp.where(odd, other, values)


class Weights:
    def __init__(self, refs, spot, groups):
        self.refs = refs
        self.paired = len(refs) > 1
        self.groups = groups
        self.spot = spot
        self.odd = lax.rem(spot[0], 2) == 1

    def block(self, chunk):
        return lax.bitwise_xor(lax.div(self.spot[0], 2) if self.paired else self.spot[1], chunk)

    def tap(self, chunk, position):
        if not self.paired:
            each = self.refs[0].shape[0] // self.groups
            start = self.block(chunk) * each
            parts = [self.refs[0][start + i, position] for i in range(each)]
            return jnp.concatenate(parts, axis=0)
        parts = [self.refs[chunk][position], self.refs[4 + chunk][position]]
        return jnp.concatenate(parts, axis=0)

    def ordered(self, values):
        return halves_swapped(values, self.odd) if self.paired else values


def conv_body(groups, parts, count, rows, width, spot, *refs):
    pieces = refs[:groups]
    top, bottom = refs[groups : groups + 2]
    weights = Weights(refs[groups + 2 : groups + 2 + parts], spot, groups)
    source, *rest = refs[groups + 2 + parts :]
    earlier, rest = rest[:count], rest[count:]
    first_out, second_out, *sends, frame = rest
    for send, held in zip(sends, earlier):
        send[:, 0] = held[...]
    if earlier:
        sends = [send.at[:, 1] for send in sends]
    span = pieces[0].shape[1]
    for mask in range(groups):
        block = lax.bitwise_xor(spot[1], mask)
        own = pieces[mask][...]
        lanes = slice(mask * span, (mask + 1) * span)
        framed = jnp.concatenate([top[:, lanes], own, bottom[:, lanes]], axis=0)
        for column, values in enumerate(turned(weights.ordered(framed), width)):
            frame[block, column] = values
    total_sum = jnp.zeros(first_out.shape, jnp.float32)
    for chunk in range(groups):
        block = weights.block(chunk)
        for position in range(9):
            start = (position // 3) * width
            window = frame[block, position % 3, start : start + rows * width, :]
            total_sum += jnp.dot(
                window, weights.tap(chunk, position), preferred_element_type=jnp.float32
            )
        if len(sends) == 1:
            sends[0][chunk] = frame[chunk, 1, width : (rows + 1) * width, :]
        else:
            near = lax.bitwise_xor(lax.div(spot[0], 2), chunk)
            center = frame[near, 1, width : (rows + 1) * width, :]
            center = center if weights.paired else halves_swapped(center, weights.odd)
            sends[0][chunk] = center[:, : span // 2]
            sends[1][chunk] = center[:, span // 2 :]
    if second_out.shape[0] == 2:
        first_out[...] = total_sum
        second_out[...] = channel_sums(total_sum)
    else:
        middle = (source[...].astype(jnp.float32) + total_sum) * root_half
        first_out[...] = middle
        second_out[...] = middle.astype(jnp.bfloat16)


def back_body(groups, rows, width, spot, grad, top, bottom, *refs):
    frame, held = refs[-2:]
    outs = refs[-2 - groups : -2]
    weights = Weights(refs[: -2 - groups], spot, groups)
    framed = jnp.concatenate([top[...], grad[...], bottom[...]], axis=0)
    for column, values in enumerate(turned(framed, width)):
        frame[column] = values
    for chunk in range(groups):
        total_sum = jnp.zeros(held.shape[1:], jnp.float32)
        for position in range(9):
            start = (2 - position // 3) * width
            total_sum += lax.dot_general(
                frame[2 - position % 3, start : start + rows * width, :],
                weights.tap(chunk, position),
                (((1,), (1,)), ((), ())),
                preferred_element_type=jnp.float32,
            )
        held[weights.block(chunk)] = weights.ordered(total_sum).astype(jnp.bfloat16)
    for mask in range(groups):
        outs[mask][...] = held[lax.bitwise_xor(spot[1], mask)]


def bf16_like(*shape):
    return jax.ShapeDtypeStruct(shape, jnp.bfloat16)


def f32_like(*shape):
    return jax.ShapeDtypeStruct(shape, jnp.float32)


def flipped(values, axis, mask):
    count = lax.axis_size(axis)
    return lax.ppermute(values, axis, [(i, i ^ mask) for i in range(count)])


def over_chips(values):
    over_x, over_y = flipped(values, "wide", 2), flipped(values, "wide", 4)
    odd = lax.rem(lax.axis_index("wide"), 2) == 1
    relayed = jnp.where(odd, over_y, over_x)
    far_pairs = [(i, i ^ (2 if i % 2 else 4)) for i in range(8)]
    return [values, over_x, over_y, lax.ppermute(relayed, "wide", far_pairs)]


def spread_slots(values):
    mine = over_chips(values)
    return mine + [flipped(part, "wide", 1) for part in mine]


def has_slots():
    return lax.axis_size("wide") == 8


def after(value, *others):
    return lax.optimization_barrier((value, others))[0]


def gathered_grads(grad):
    return lax.all_gather(grad, "wide", tiled=True)


def gathered_blocks(blocks):
    return [lax.all_gather(blocks, "wide")]


def spread_chips(values):
    if has_slots():
        return over_chips(values)
    mask = 2
    while mask < lax.axis_size("wide"):
        values = jnp.concatenate([values, flipped(values, "wide", mask)])
        mask *= 2
    return [values]


def spread_stats(values):
    if has_slots():
        over_x, over_y = flipped(values, "wide", 2), flipped(values, "wide", 4)
        return [values, over_x, over_y, flipped(over_x, "wide", 4)]
    mask = 2
    while mask < lax.axis_size("wide"):
        values = jnp.concatenate([values, flipped(values, "wide", mask)], axis=1)
        mask *= 2
    return [values]


def channel_pieces(values):
    count = lax.axis_size("tensor")
    return [values] + [flipped(values, "tensor", mask) for mask in range(1, count)]


def edge_rows(last, first):
    count = lax.axis_size("wide")
    above = lax.ppermute(last, "wide", [(i, i + 1) for i in range(count - 1)])
    below = lax.ppermute(first, "wide", [(i + 1, i) for i in range(count - 1)])
    return above, below


def convolve(spot, pieces, edges, kernel, source, second_shape, earlier, rows, width):
    groups, (area, span) = len(pieces), pieces[0].shape
    count, block = (2, span // 2) if has_slots() else (1, span)
    layers = (2,) if earlier else ()
    sends = [bf16_like(groups, *layers, area, block)] * count
    return local_kernel(
        functools.partial(conv_body, groups, len(kernel), len(earlier), rows, width),
        [f32_like(area, span), second_shape] + sends,
        [spot, *pieces, *edges, *far(kernel), source, *far(earlier)],
        [pltpu.VMEM((groups, 3, (rows + 2) * width, span), jnp.bfloat16)],
        32,
        2 * 9 * area * C * span,
    )


def piece_edges(pieces, width):
    return edge_rows(
        jnp.concatenate([piece[-width:] for piece in pieces], axis=1),
        jnp.concatenate([piece[:width] for piece in pieces], axis=1),
    )


def convolve_back(spot, grad, edges, kernel, rows, width):
    groups, (area, span) = lax.axis_size("tensor"), grad.shape
    return local_kernel(
        functools.partial(back_body, groups, rows, width),
        [bf16_like(area, span)] * groups,
        [spot, grad, *edges, *far(kernel)],
        [
            pltpu.VMEM((3, (rows + 2) * width, span), jnp.bfloat16),
            pltpu.VMEM((groups, area, span), jnp.bfloat16),
        ],
        32,
        2 * 9 * area * C * span,
    )


def sent_parts(parts):
    return [parts[0]] + [flipped(parts[mask], "tensor", mask) for mask in range(1, len(parts))]


def pair_blocks_body(spot, kept, got, *outs):
    for index, out in enumerate(outs):
        out[0] = kept[index + 1]
        out[1] = got[index + 1]


def kernel_grad_body(width, layer, spot, kept, got, *refs):
    *pairs, grads = refs[:4]
    out, turned_all = refs[-2:]
    area, span = kept.shape[2:]
    depth = 8 * area
    turned_all[:, :width] = jnp.zeros((3 * span, width), jnp.bfloat16)
    turned_all[:, depth + width :] = jnp.zeros((3 * span, width), jnp.bfloat16)
    pieces = [kept[0, layer], got[0, layer]]
    pieces += [pair[core, layer] for pair in pairs for core in range(2)]
    for mask, piece in enumerate(pieces):
        start = pl.multiple_of(lax.bitwise_xor(spot[0], mask) * area, area)
        for column, values in enumerate(turned(piece, width)):
            turned_all[column * span : (column + 1) * span, pl.ds(start + width, area)] = flat_turn(
                values
            )
    for row in range(3):
        product = jnp.dot(
            turned_all[:, row * width : row * width + depth],
            grads[...],
            preferred_element_type=jnp.float32,
        )
        for column in range(3):
            out[0, 3 * row + column] = product[column * span : (column + 1) * span, :]


def swapped_blocks(spot, kept, sent):
    got = flipped(sent, "wide", 1)
    pairs = local_kernel(
        pair_blocks_body, [bf16_like(2, *kept.shape[1:])] * 3, [spot, *far([kept, got])], [], 16, 0
    )
    return [kept, got, *pairs]


def traded_blocks(blocks):
    return blocks[:2] + [flipped(blocks[2 + k], "wide", 2 * k + 2) for k in range(3)]


def kernel_grad(spot, pieces, grads, rows, width, layer, earlier):
    area, span = pieces[0].shape[2:]
    columns, depth = grads.shape[1], grads.shape[0]
    operands = [spot, *far(pieces), *far([grads])]
    specs = [in_smem] + [in_vmem] * (len(operands) - 1)
    shape = f32_like(2, 9, span, columns)
    if earlier is not None:
        operands.append(earlier)
        specs.append(pl.BlockSpec(memory_space=pl.ANY))
    return pl.pallas_call(
        functools.partial(kernel_grad_body, width, layer),
        out_shape=shape,
        in_specs=specs,
        grid=(1,),
        out_specs=pl.BlockSpec((1, 9, span, columns), lambda i: (layer, 0, 0, 0)),
        scratch_shapes=[
            pltpu.VMEM((3 * span, depth + 2 * width), jnp.bfloat16),
        ],
        input_output_aliases={} if earlier is None else {len(operands) - 1: 0},
        compiler_params=pltpu.CompilerParams(vmem_limit_bytes=24 * MIB),
        cost_estimate=pl.CostEstimate(
            flops=2 * 9 * depth * span * columns, bytes_accessed=4 * MIB, transcendentals=0
        ),
    )(*operands)


def kernel_grad_whole(send, grads, rows, width):
    natural = jnp.moveaxis(send, 0, 1).reshape(1, rows, width, C)
    swapped = lax.all_to_all(natural, "wide", split_axis=3, concat_axis=1, tiled=True)
    framed = jnp.pad(swapped, ((0, 0), (1, 1), (1, 1), (0, 0)))
    low = grads.reshape(1, -1, width, grads.shape[1])
    return jnp.stack(
        [
            jnp.einsum(
                "mrwc,mrwd->cd",
                framed[:, tap // 3 : tap // 3 + low.shape[1], tap % 3 : tap % 3 + width, :],
                low,
                preferred_element_type=jnp.float32,
            )
            for tap in range(9)
        ]
    )


root_half = 1.0 / math.sqrt(2.0)
highest = lax.Precision.HIGHEST


def sinusoid(steps):
    half_width = TEMB // 2
    frequency = jnp.exp(-math.log(10000.0) * jnp.arange(half_width, dtype=jnp.float32) / half_width)
    angles = steps.astype(jnp.float32)[:, None] * frequency[None, :]
    return jnp.concatenate([jnp.cos(angles), jnp.sin(angles)], axis=1)


def part_totals(rows):
    if not has_slots():
        return [total(rows, "wide")]
    rows = rows + flipped(rows, "wide", 1)
    return [rows] + [flipped(rows, "wide", mask) for mask in (2, 4, 6)]


def sum_of_parts(refs):
    if len(refs) == 1:
        return refs[0][...]
    return (refs[0][...] + refs[1][...]) + (refs[2][...] + refs[3][...])


def total(values, axis):
    mask = 1
    while mask < lax.axis_size(axis):
        values = values + flipped(values, axis, mask)
        mask *= 2
    return values


def silu_slope(values):
    logistic = lax.logistic(values)
    return logistic * (1.0 + values * (1.0 - logistic))


def channel_sums(values):
    return jnp.concatenate(
        [
            jnp.sum(values, axis=0, keepdims=True),
            jnp.sum(values * values, axis=0, keepdims=True),
        ],
        axis=0,
    )


def group_means(first, second, pixel_count):
    channels = first.shape[1]
    per_group = C // GROUPS
    row = lax.div(lax.broadcasted_iota(jnp.int32, (channels, channels), 0), per_group)
    column = lax.div(lax.broadcasted_iota(jnp.int32, (channels, channels), 1), per_group)
    same = jnp.where(row == column, 1.0, 0.0)
    rows = jnp.concatenate([first, second, jnp.zeros((6, channels), jnp.float32)], axis=0)
    means = jnp.dot(rows, same, precision=highest, preferred_element_type=jnp.float32)
    means = means / (pixel_count * per_group)
    return means[0:1], means[1:2]


def group_scale(first, second, pixel_count):
    center, square = group_means(first, second, pixel_count)
    return center, lax.rsqrt(square - center * center + 1e-05)


def lifted_sums(sums, film, pixel_count):
    slope, shift = 1.0 + film[0:1], film[1:2]
    plain, square = sums[0:1], sums[1:2]
    return (
        slope * plain + pixel_count * shift,
        slope * slope * square + 2.0 * slope * shift * plain + pixel_count * shift * shift,
    )


def silu_low(values):
    return (values * lax.logistic(values)).astype(jnp.bfloat16)


def first_norm_body(pixel_count, spot, pixels, affine, *refs):
    *parts, out, sums = refs
    sums[...] = sum_of_parts(parts)
    center, inverse = group_scale(sums[0:1], sums[1:2], pixel_count)
    scaled = (pixels[...].astype(jnp.float32) - center) * inverse
    out[...] = silu_low(scaled * affine[0:1] + affine[1:2])


def second_norm_body(pixel_count, spot, inner, affine, *refs):
    *parts, out, film, sums = refs
    summed = sum_of_parts(parts)
    film[...], sums[...] = summed[:2], summed[2:]
    center, inverse = group_scale(*lifted_sums(sums[...], film[...], pixel_count), pixel_count)
    lifted = inner[...] * (1.0 + film[0:1]) + film[1:2]
    out[...] = silu_low((lifted - center) * inverse * affine[0:1] + affine[1:2])


def parts_sum(refs):
    summed = refs[0][...].astype(jnp.float32)
    for ref in refs[1:]:
        summed += ref[...].astype(jnp.float32)
    return summed


def stacked_rows(rows):
    return jnp.concatenate([jnp.sum(row, axis=0, keepdims=True) for row in rows], axis=0)


def second_back_body(groups, pixel_count, spot, *refs):
    inner, sums, film, affine, terms, out, rows = refs[groups:]
    center, inverse = group_scale(*lifted_sums(sums[...], film[...], pixel_count), pixel_count)
    own = inner[...]
    scaled = (own * (1.0 + film[0:1]) + film[1:2] - center) * inverse
    back = parts_sum(refs[:groups]) * silu_slope(scaled * affine[0:1] + affine[1:2])
    out[...] = back
    rows[0:3, :] = stacked_rows([back * scaled, back, back * own])
    rows[3:5, :] = terms[...]
    rows[5:8, :] = jnp.zeros((3, own.shape[1]), jnp.float32)


def second_input_body(pixel_count, width, spot, back, inner, sums, film, affine, *refs):
    *parts, low, last, first, film_rows, rows = refs
    rows[...] = sum_of_parts(parts)
    slope, shift, gain = 1.0 + film[0:1], film[1:2], affine[0:1]
    plain_sum, square_sum = sums[0:1], sums[1:2]
    lifted_sum, lifted_square = lifted_sums(sums[...], film[...], pixel_count)
    center, inverse = group_scale(lifted_sum, lifted_square, pixel_count)
    dotted, plain = group_means(gain * rows[0:1], gain * rows[1:2], pixel_count)
    scaled = (inner[...] * slope + shift - center) * inverse
    grad = inverse * (back[...] * gain - plain - scaled * dotted)
    grad_low = (grad * slope).astype(jnp.bfloat16)
    low[...] = grad_low
    last[...] = grad_low[-width:]
    first[...] = grad_low[:width]
    scaled_sum = inverse * (lifted_sum - pixel_count * center)
    scaled_inner = inverse * (slope * square_sum + (shift - center) * plain_sum)
    film_rows[0:1, :] = inverse * (
        gain * rows[2:3] - plain * plain_sum - dotted * scaled_inner
    )
    film_rows[1:2, :] = inverse * (
        gain * rows[1:2] - pixel_count * plain - dotted * scaled_sum
    )


def first_back_body(groups, pixel_count, spot, *refs):
    pixels, sums, affine, out, rows = refs[groups:]
    center, inverse = group_scale(sums[0:1], sums[1:2], pixel_count)
    scaled = (pixels[...].astype(jnp.float32) - center) * inverse
    back = parts_sum(refs[:groups]) * silu_slope(scaled * affine[0:1] + affine[1:2])
    out[...] = back
    rows[...] = stacked_rows([back * scaled, back])


def first_input_body(pixel_count, spot, back, pixels, sums, affine, middle, *refs):
    *parts, out, rows = refs
    rows[...] = sum_of_parts(parts)
    gain = affine[0:1]
    center, inverse = group_scale(sums[0:1], sums[1:2], pixel_count)
    dotted, plain = group_means(gain * rows[0:1], gain * rows[1:2], pixel_count)
    scaled = (pixels[...].astype(jnp.float32) - center) * inverse
    out[...] = inverse * (back[...] * gain - plain - scaled * dotted) + middle[...] * root_half


def dot(left, right):
    return jnp.dot(left, right, preferred_element_type=jnp.float32)


def dot_last(left, right):
    return lax.dot_general(
        left, right, (((1,), (1,)), ((), ())), preferred_element_type=jnp.float32
    )


def flat_turn(values):
    return jnp.transpose(values.astype(jnp.float32)).astype(jnp.bfloat16)


def dot_first(left, right):
    return dot(flat_turn(left), right)


def head_choice(values, odd):
    first, second = values[:, :HEAD_DIM], values[:, HEAD_DIM:]
    return jnp.where(odd, second, first), jnp.where(odd, first, second)


def heads_joined(kept, received, odd):
    return jnp.where(
        odd,
        jnp.concatenate([received, kept], axis=1),
        jnp.concatenate([kept, received], axis=1),
    )


def packed_rows(values):
    rows = []
    for _ in range(3):
        rows.append(values.astype(jnp.bfloat16).astype(jnp.float32))
        values = values - rows[-1]
    rows.append(jnp.zeros((10, values.shape[1]), jnp.float32))
    return jnp.concatenate(rows, axis=0).astype(jnp.bfloat16)


def unpacked_rows(packed, area):
    rows = packed[area:, :].astype(jnp.float32)
    return rows[0:1] + rows[2:3] + rows[4:5], rows[1:2] + rows[3:4] + rows[5:6]


def prepare_body(spot, pixels, cotangent, terms, pack, sums):
    area = cotangent.shape[0]
    pack[:area] = cotangent[...].astype(jnp.bfloat16)
    pack[area:] = packed_rows(terms[...])
    sums[...] = channel_sums(pixels[...].astype(jnp.float32))


def project_body(groups, spot, *refs):
    pieces, packs = refs[:groups], refs[groups : 2 * groups]
    own, maps, keep_q, keep_kv, send, cross, normed, scaled, center, inverse = refs[2 * groups :]
    weights = Weights([maps], spot, groups)
    odd = lax.rem(spot[0], 2) == 1
    area = own.shape[0]
    token_sum = token_square = 0.0
    for piece in pieces:
        values = piece[...].astype(jnp.float32)
        token_sum += jnp.sum(values, axis=1, keepdims=True)
        token_square += jnp.sum(values * values, axis=1, keepdims=True)
    mean = token_sum / C
    scale = lax.rsqrt(token_square / C - mean * mean + 1e-05)
    lows = []
    for mask in range(groups):
        gain, bias = unpacked_rows(packs[mask], area)
        values = (pieces[mask][...].astype(jnp.float32) - mean) * scale
        lows.append((values * gain + bias).astype(jnp.bfloat16))
        normed[lax.bitwise_xor(spot[1], mask)] = lows[-1]
    center[...] = mean
    inverse[...] = scale
    scaled[...] = (own[...] - mean) * scale
    projected = []
    for position in range(4):
        total_sum = 0.0
        for mask in range(groups):
            total_sum += dot(lows[mask], weights.tap(mask, position))
        projected.append(total_sum.astype(jnp.bfloat16))
    cross[...] = projected[3]
    chosen = [head_choice(values, odd) for values in projected[:3]]
    keep_q[...] = chosen[0][0]
    keep_kv[...] = jnp.concatenate([chosen[1][0], chosen[2][0]], axis=1)
    send[...] = jnp.concatenate([pair[1] for pair in chosen], axis=1)


def out_grad_body(groups, spot, *refs):
    packs = refs[:groups]
    maps, keep, send, cross = refs[groups:]
    weights = Weights([maps], spot, groups)
    sums = []
    for position in (4, 5):
        total_sum = 0.0
        for mask in range(groups):
            total_sum += dot(packs[mask][: cross.shape[0]], weights.tap(mask, position))
        sums.append(total_sum.astype(jnp.bfloat16))
    kept, sent = head_choice(sums[0], lax.rem(spot[0], 2) == 1)
    keep[...] = kept
    send[...] = sent
    cross[...] = sums[1]


def mix_body(groups, spot, kept, received, crossed, maps, out):
    weights = Weights([maps], spot, groups)
    area = kept.shape[0]
    attended = heads_joined(
        kept[...], received[:, 3 * HEAD_DIM :], lax.rem(spot[0], 2) == 1
    )
    for mask in range(groups):
        total_sum = dot_last(attended, weights.tap(mask, 4))
        total_sum += dot_last(crossed[...], weights.tap(mask, 5))
        start = pl.multiple_of(weights.block(mask) * area, area)
        out[pl.ds(start, area), :] = total_sum.astype(jnp.bfloat16)


def over_rows(refs, step, state):
    for index, ref in enumerate(refs):
        rows = ref.shape[0]
        if rows <= 512:
            state = step(state, ref[...], index, 0)
        else:
            state = lax.fori_loop(
                0,
                rows // 512,
                lambda i, held: step(
                    held, ref[pl.ds(pl.multiple_of(i * 512, 512), 512), :], index, i * 512
                ),
                state,
            )
    return state


score_scale = HEAD_DIM ** (-0.5)


def attend_body(count, spot, query_grad, *refs):
    pairs = refs[:count]
    keep, send, stats = refs[count:]
    query, grad = query_grad[:, :HEAD_DIM], query_grad[:, HEAD_DIM:]
    queries = query.shape[0]

    def step(state, pair, index, start):
        top, weight_sum, weighted = state
        scores = dot_last(pair[:, :HEAD_DIM], query) * score_scale
        raised = jnp.maximum(top, jnp.max(scores, axis=0, keepdims=True))
        rescale = jnp.exp(top - raised)
        weights = jnp.exp(scores - raised)
        weight_sum = weight_sum * rescale + jnp.sum(weights, axis=0, keepdims=True)
        weighted = weighted * rescale + dot_first(pair[:, HEAD_DIM:], weights.astype(jnp.bfloat16))
        return raised, weight_sum, weighted

    top, weight_sum, weighted = over_rows(
        pairs,
        step,
        (
            jnp.full((1, queries), -1e30, jnp.float32),
            jnp.zeros((1, queries), jnp.float32),
            jnp.zeros((HEAD_DIM, queries), jnp.float32),
        ),
    )
    attended = weighted / weight_sum
    delta = jnp.sum(attended * jnp.transpose(grad.astype(jnp.float32)), axis=0, keepdims=True)
    stats[...] = jnp.concatenate([top + jnp.log(weight_sum), delta], axis=0)
    turned_back = jnp.transpose(attended).astype(jnp.bfloat16)
    keep[...] = turned_back[: queries // 2]
    send[...] = turned_back[queries // 2 :]


def query_grad_body(count, spot, query_grad, stats, *refs):
    pairs = refs[:count]
    keep, send = refs[count:]
    query, grad = query_grad[:, :HEAD_DIM], query_grad[:, HEAD_DIM:]
    queries = query.shape[0]
    log_sum, delta = stats[0:1, :], stats[1:2, :]

    def step(state, pair, index, start):
        scores = dot_last(pair[:, :HEAD_DIM], query) * score_scale
        probs = jnp.exp(scores - log_sum)
        grad_probs = dot_last(pair[:, HEAD_DIM:], grad)
        grad_scores = (probs * (grad_probs - delta)).astype(jnp.bfloat16)
        return state + dot_first(pair[:, :HEAD_DIM], grad_scores)

    flat = over_rows(pairs, step, jnp.zeros((HEAD_DIM, queries), jnp.float32))
    result = jnp.transpose(flat * score_scale).astype(jnp.bfloat16)
    keep[...] = result[: queries // 2]
    send[...] = result[queries // 2 :]


def key_grad_body(count, spot, pair, sent_query, sent_out, *refs):
    queries, stats = refs[:count], refs[count:-2]
    keep, send = refs[-2:]
    keys, values = pair[:, :HEAD_DIM], pair[:, HEAD_DIM:]
    depth = keys.shape[0]

    def step(state, block, index, start):
        grad_keys, grad_values = state
        rows = block.shape[0]
        lanes = pl.ds(start if isinstance(start, int) else pl.multiple_of(start, 512), rows)
        log_sum, delta = stats[index][0:1, lanes], stats[index][1:2, lanes]
        query, grad = block[:, :HEAD_DIM], block[:, HEAD_DIM:]
        probs = jnp.exp(dot_last(keys, query) * score_scale - log_sum)
        grad_values += dot(probs.astype(jnp.bfloat16), grad)
        grad_scores = probs * (dot_last(values, grad) - delta)
        grad_keys += dot(grad_scores.astype(jnp.bfloat16), query)
        return grad_keys, grad_values

    zero = jnp.zeros((depth, HEAD_DIM), jnp.float32)
    grad_keys, grad_values = over_rows(queries, step, (zero, zero))
    both = jnp.concatenate([grad_keys * score_scale, grad_values], axis=1).astype(jnp.bfloat16)
    keep[...] = both[: depth // 2]
    send[:, : 2 * HEAD_DIM] = both[depth // 2 :]
    send[:, 2 * HEAD_DIM : 3 * HEAD_DIM] = sent_query[...]
    send[:, 3 * HEAD_DIM :] = sent_out[...]


def cross_body(spot, query, text, grad, crossed, grad_query, text_grad):
    live = lax.broadcasted_iota(jnp.int32, (query.shape[0], text.shape[1]), 1) < spot[2]
    for head in range(query.shape[1] // HEAD_DIM):
        lanes = slice(head * HEAD_DIM, (head + 1) * HEAD_DIM)
        own, keys, values, back = query[:, lanes], text[0, :, lanes], text[1, :, lanes], grad[:, lanes]
        scores = jnp.where(live, dot_last(own, keys) * score_scale, -1e30)
        weights = jnp.exp(scores - jnp.max(scores, axis=1, keepdims=True))
        probs = weights / jnp.sum(weights, axis=1, keepdims=True)
        low = probs.astype(jnp.bfloat16)
        crossed[:, lanes] = dot(low, values).astype(jnp.bfloat16)
        grad_probs = dot_last(back, values)
        grad_scores = probs * (grad_probs - jnp.sum(probs * grad_probs, axis=1, keepdims=True))
        grad_low = grad_scores.astype(jnp.bfloat16)
        grad_query[:, lanes] = (dot(grad_low, keys) * score_scale).astype(jnp.bfloat16)
        text_grad[0, :, lanes] = (dot_first(grad_low, own) * score_scale).astype(jnp.bfloat16)
        text_grad[1, :, lanes] = dot_first(low, back).astype(jnp.bfloat16)


def joined_grads(spot, kept_query, kept_pair, got, cross):
    odd = lax.rem(spot[0], 2) == 1
    parts = [got[:, i * HEAD_DIM : (i + 1) * HEAD_DIM] for i in range(3)]
    return [
        heads_joined(kept_query[...], parts[2], odd),
        heads_joined(kept_pair[:, :HEAD_DIM], parts[0], odd),
        heads_joined(kept_pair[:, HEAD_DIM:], parts[1], odd),
        cross[...],
    ]


def project_back_body(groups, spot, kq, kp, got, cross, center, inverse, maps, *refs):
    pieces, packs = refs[:groups], refs[groups : 2 * groups]
    outs = refs[2 * groups :]
    weights = Weights([maps], spot, groups)
    grads = joined_grads(spot, kq, kp, got, cross)
    area = cross.shape[0]
    plain = dotted = 0.0
    for mask in range(groups):
        part = 0.0
        for position in range(4):
            part += dot_last(grads[position], weights.tap(mask, position))
        outs[mask][:area] = part.astype(jnp.bfloat16)
        eased = part * unpacked_rows(packs[mask], part.shape[0])[0]
        unit = (pieces[mask][...].astype(jnp.float32) - center[...]) * inverse[...]
        plain += eased
        dotted += eased * unit
    ones = jnp.ones((8, plain.shape[1]), jnp.float32)
    sums = [
        lax.dot_general(
            ones,
            values,
            (((1,), (1,)), ((), ())),
            precision=highest,
            preferred_element_type=jnp.float32,
        )[0:1]
        for values in (plain, dotted)
    ]
    packed = packed_rows(jnp.concatenate(sums, axis=0))
    for out in outs:
        out[area:] = packed


def weight_grad_body(groups, spot, kq, kp, got, cross, kept, crossed, normed, *refs):
    packs, outs, frame = refs[:groups], refs[groups:-1], refs[-1]
    odd = lax.rem(spot[0], 2) == 1
    area, span = cross.shape
    right = jnp.concatenate(joined_grads(spot, kq, kp, got, cross), axis=1)
    out_right = jnp.concatenate(
        [heads_joined(kept[...], got[:, 3 * HEAD_DIM :], odd), crossed[...]], axis=1
    )
    for mask in range(groups):
        frame[lax.bitwise_xor(spot[1], mask)] = packs[mask][:area]
    for chunk in range(groups):
        near = lax.bitwise_xor(lax.div(spot[0], 2), chunk) if len(outs) == 2 else chunk
        product = jnp.concatenate(
            [dot_first(normed[near], right), dot_first(frame[near], out_right)], axis=1
        ).astype(jnp.bfloat16)
        if len(outs) == 2:
            low, high = product[: span // 2], product[span // 2 :]
            outs[0][chunk] = jnp.where(odd, high, low)
            outs[1][chunk] = jnp.where(odd, low, high)
        else:
            outs[0][chunk * span : (chunk + 1) * span, :] = product


def weight_sum_body(spot, kept, got, own, *outs):
    for index, out in enumerate((own,) + outs):
        both = kept[index].astype(jnp.float32) + got[index].astype(jnp.float32)
        out[...] = both.astype(out.dtype)


def weight_out_body(spot, own, *refs):
    *parts, in_grad, self_grad, cross_grad = refs
    summed = own[...] + parts_sum(parts)
    span = in_grad.shape[2]
    for position in range(4):
        in_grad[position] = summed[:, position * span : (position + 1) * span]
    self_grad[...] = jnp.transpose(summed[:, 4 * span : 5 * span])
    cross_grad[...] = jnp.transpose(summed[:, 5 * span :])


def norm_back_body(groups, width, spot, *refs):
    scaled, inverse, cotangent, gain, middle, low, last, first, terms = refs[groups:]
    area = scaled.shape[0]
    grad = plain = dotted = 0.0
    for ref in refs[:groups]:
        grad += ref[:area].astype(jnp.float32)
        sums = unpacked_rows(ref, area)
        plain, dotted = plain + sums[0], dotted + sums[1]
    same = lax.broadcasted_iota(jnp.int32, (area, area), 0) == lax.broadcasted_iota(
        jnp.int32, (area, area), 1
    )
    plain = jnp.sum(jnp.where(same, plain, 0.0), axis=1, keepdims=True) / C
    dotted = jnp.sum(jnp.where(same, dotted, 0.0), axis=1, keepdims=True) / C
    unit = scaled[...]
    terms[0:1, :] = jnp.sum(grad * unit, axis=0, keepdims=True)
    terms[1:2, :] = jnp.sum(grad, axis=0, keepdims=True)
    back = inverse[...] * (grad * gain[...] - plain - unit * dotted) + cotangent[...]
    middle[...] = back
    grad_low = (back * root_half).astype(jnp.bfloat16)
    low[...] = grad_low
    last[...] = grad_low[-width:]
    first[...] = grad_low[:width]


def shards(
    pixels,
    text_states,
    text_length,
    timestep,
    conv_weights,
    film_time,
    film_text,
    group_gain,
    group_bias,
    layer_gain,
    layer_bias,
    attn_in,
    text_kv,
    out_self,
    out_cross,
    cotangent,
):
    map_count, row_count, col_count, width_own = pixels.shape
    token_count = row_count * col_count
    groups = lax.axis_size("tensor")
    pixel_count = token_count * lax.axis_size("wide")
    own_shape = (map_count, row_count, col_count, width_own)
    flat = (token_count, width_own)
    half = (token_count, HEAD_DIM)
    edge = (col_count, width_own)
    spot = jnp.stack([lax.axis_index("wide"), lax.axis_index("tensor"), text_length[0]])
    spot = spot.astype(jnp.int32)
    own_pixels = pixels.reshape(flat)
    flat_cotangent = cotangent.reshape(flat)
    affine = [jnp.stack([group_gain[layer], group_bias[layer]]) for layer in range(2)]

    pack, sums = local_kernel(
        prepare_body,
        [bf16_like(token_count + 16, width_own), f32_like(2, width_own)],
        [spot, own_pixels, flat_cotangent, jnp.stack([layer_gain, layer_bias])],
        [],
        8,
        0,
    )
    first_parts = part_totals(sums)
    if has_slots():
        kernel_one = spread_slots(after(conv_weights[0], first_parts))
    else:
        kernel_one = gathered_blocks(conv_weights[0])
    kernel_two = gathered_blocks(conv_weights[1])
    maps = jnp.concatenate(
        [attn_in, jnp.transpose(jnp.stack([out_self, out_cross]), (0, 2, 1))], axis=0
    )
    maps = gathered_blocks(maps)[0]

    features = sinusoid(timestep).astype(jnp.bfloat16)
    present = jnp.arange(TEXT)[None, :] < text_length[:, None]
    pooled = jnp.einsum(
        "mtx,mt->mx", text_states, present.astype(jnp.bfloat16), preferred_element_type=jnp.float32
    )
    pooled = (pooled / text_length.astype(jnp.float32)[:, None]).astype(jnp.bfloat16)
    wide_index = lax.axis_index("wide")
    time_rows = film_time.shape[0]
    text_rows = film_text.shape[0]
    own_features = lax.dynamic_slice_in_dim(features, wide_index * time_rows, time_rows, 1)
    own_pooled = lax.dynamic_slice_in_dim(pooled, wide_index * text_rows, text_rows, 1)
    own_text = lax.dynamic_slice_in_dim(text_states, wide_index * text_rows, text_rows, 2)
    film_term = jnp.einsum(
        "mk,ksc->msc", own_features, film_time, preferred_element_type=jnp.float32
    ) + jnp.einsum("mk,ksc->msc", own_pooled, film_text, preferred_element_type=jnp.float32)
    text_term = jnp.einsum("mtx,pxd->pmtd", own_text, text_kv, preferred_element_type=jnp.float32)
    text_term = text_term.astype(jnp.bfloat16).reshape(2, TEXT, width_own)

    row_pair = f32_like(2, width_own)
    first, first_sums = local_kernel(
        functools.partial(first_norm_body, pixel_count),
        [bf16_like(*flat), row_pair],
        [spot, own_pixels, affine[0], *first_parts],
        [],
        8,
        0,
    )
    pieces = channel_pieces(first)
    packs = channel_pieces(after(pack, pieces))
    edges = piece_edges(pieces, col_count)
    pieces[0] = after(pieces[0], film_term)
    inner, sums, *first_sends = convolve(
        spot,
        pieces,
        edges,
        kernel_one,
        own_pixels,
        f32_like(2, width_own),
        [],
        row_count,
        col_count,
    )
    inner_parts = part_totals(jnp.concatenate([film_term[0], sums]))
    second, film, inner_sums = local_kernel(
        functools.partial(second_norm_body, pixel_count),
        [bf16_like(*flat), row_pair, row_pair],
        [spot, inner, affine[1], *inner_parts],
        [],
        8,
        0,
    )
    pieces = channel_pieces(second)
    edges = piece_edges(pieces, col_count)
    pieces[0] = after(pieces[0], packs)
    middle, middle_low, *both_sends = convolve(
        spot,
        pieces,
        edges,
        kernel_two,
        own_pixels,
        bf16_like(*flat),
        first_sends,
        row_count,
        col_count,
    )

    middle_pieces = channel_pieces(middle_low)
    text_proj = total(after(text_term, middle_low), "wide")
    column = f32_like(token_count, 1)
    square = 2 * token_count * C * width_own
    kept_query, kept_pair, sent, cross_query, normed, scaled, center, inverse = local_kernel(
        functools.partial(project_body, groups),
        [
            bf16_like(*half),
            bf16_like(*flat),
            bf16_like(token_count, 3 * HEAD_DIM),
            bf16_like(*flat),
            bf16_like(groups, *flat),
            f32_like(*flat),
            column,
            column,
        ],
        [spot, *middle_pieces, *far(packs), middle, *far([maps])],
        [],
        24,
        4 * square,
    )
    got = flipped(sent, "wide", 1)
    kept_grad, sent_grad, grad_crossed = local_kernel(
        functools.partial(out_grad_body, groups),
        [bf16_like(*half), bf16_like(*half), bf16_like(*flat)],
        [spot, *far(packs), *far([maps])],
        [],
        16,
        2 * square,
    )
    got_grad = flipped(sent_grad, "wide", 1)
    pair = jnp.concatenate([kept_pair, got[:, HEAD_DIM:]])
    pairs = spread_chips(pair)
    query_grad = jnp.concatenate(
        [
            jnp.concatenate([kept_query, got[:, :HEAD_DIM]]),
            jnp.concatenate([kept_grad, got_grad]),
        ],
        axis=1,
    )
    query_grads = spread_chips(after(query_grad, *pairs))
    scores = 2 * (2 * token_count) * HEAD_DIM * pixel_count
    kept_out, sent_out, stats = local_kernel(
        functools.partial(attend_body, len(pairs)),
        [bf16_like(*half), bf16_like(*half), f32_like(2, 2 * token_count)],
        [spot, query_grad, *pairs],
        [],
        24,
        2 * scores,
    )
    all_stats = spread_stats(stats)
    crossed, grad_cross_query, text_grads = local_kernel(
        cross_body,
        [bf16_like(*flat), bf16_like(*flat), bf16_like(2, TEXT, width_own)],
        [spot, cross_query, text_proj, grad_crossed],
        [],
        8,
        12 * token_count * TEXT * width_own,
    )
    kept_dq, sent_dq = local_kernel(
        functools.partial(query_grad_body, len(pairs)),
        [bf16_like(*half), bf16_like(*half)],
        [spot, query_grad, stats, *pairs],
        [],
        24,
        3 * scores,
    )
    kept_dk, sent_all = local_kernel(
        functools.partial(key_grad_body, len(query_grads)),
        [bf16_like(*flat), bf16_like(token_count, 4 * HEAD_DIM)],
        [spot, pair, sent_dq, sent_out, *query_grads, *all_stats],
        [],
        24,
        4 * scores,
    )
    got_all = flipped(sent_all, "wide", 1)
    if has_slots():
        both_blocks = swapped_blocks(spot, after(both_sends[0], kept_pair), both_sends[1])
        kept_dk = after(kept_dk, both_blocks)
        both_blocks = traded_blocks(both_blocks)
    text_all = total(after(text_grads, *all_stats), "wide").astype(jnp.float32)
    (mixed,) = local_kernel(
        functools.partial(mix_body, groups),
        [bf16_like(groups * token_count, width_own)],
        [spot, kept_out, got_all, crossed, *far([maps])],
        [],
        16,
        2 * square,
    )
    mixed = lax.psum_scatter(mixed, "tensor", scatter_dimension=0, tiled=True)
    result = middle + mixed.astype(jnp.float32)
    projected_grads = [kept_dq, kept_dk, got_all, grad_cross_query]
    norm_parts = local_kernel(
        functools.partial(project_back_body, groups),
        [bf16_like(token_count + 16, width_own)] * groups,
        [spot, *projected_grads, center, inverse, *far([maps]), *far(middle_pieces), *far(packs)],
        [],
        24,
        4 * square,
    )
    norm_parts = sent_parts(norm_parts)
    columns = 6 * width_own
    width_block = C // lax.axis_size("wide")
    if has_slots():
        weight_shapes = [bf16_like(groups, width_block, columns)] * 2
    else:
        weight_shapes = [bf16_like(C, columns)]
    weight_parts = local_kernel(
        functools.partial(weight_grad_body, groups),
        weight_shapes,
        [spot, *projected_grads, kept_out, crossed, *far([normed]), *far(packs)],
        [pltpu.VMEM((groups, *flat), jnp.bfloat16)],
        24,
        6 * square,
    )
    if has_slots():
        weight_own, *weight_sends = local_kernel(
            weight_sum_body,
            [f32_like(width_block, columns)] + [bf16_like(width_block, columns)] * 3,
            [spot, weight_parts[0], flipped(weight_parts[1], "wide", 1)],
            [],
            24,
            0,
        )
        norm_parts[0] = after(norm_parts[0], weight_sends)
        weight_got = [flipped(weight_sends[k], "wide", 2 * k + 2) for k in range(3)]
        attn_in_grad, self_grad, cross_grad = local_kernel(
            weight_out_body,
            [f32_like(4, width_block, width_own)] + [f32_like(width_own, width_block)] * 2,
            [spot, weight_own, *weight_got],
            [],
            16,
            0,
        )
    else:
        weight_sums = lax.psum_scatter(weight_parts[0], "wide", scatter_dimension=0, tiled=True)
        weight_sums = weight_sums.astype(jnp.float32)
        in_count = 4 * width_own
        attn_in_grad = jnp.moveaxis(weight_sums[:, :in_count].reshape(-1, 4, width_own), 1, 0)
        self_grad = weight_sums[:, in_count : in_count + width_own].T
        cross_grad = weight_sums[:, in_count + width_own :].T
    grad_middle, grad_two, last, head, terms = local_kernel(
        functools.partial(norm_back_body, groups, col_count),
        [
            f32_like(*flat),
            bf16_like(*flat),
            bf16_like(*edge),
            bf16_like(*edge),
            f32_like(2, width_own),
        ],
        [
            spot,
            *norm_parts,
            scaled,
            inverse,
            flat_cotangent,
            layer_gain[None],
        ],
        [],
        16,
        0,
    )

    edges = edge_rows(last, head)
    grads_two = gathered_grads(grad_two)
    back_parts = convolve_back(spot, grad_two, edges, kernel_two, row_count, col_count)
    back_parts = sent_parts(back_parts)
    back_parts[0] = after(back_parts[0], text_all, attn_in_grad)
    back, rows = local_kernel(
        functools.partial(second_back_body, groups, pixel_count),
        [f32_like(*flat), f32_like(8, width_own)],
        [spot, *back_parts, inner, inner_sums, film, affine[1], terms],
        [],
        16,
        0,
    )
    grad_one, last, head, film_rows, second_rows = local_kernel(
        functools.partial(second_input_body, pixel_count, col_count),
        [bf16_like(*flat), bf16_like(*edge), bf16_like(*edge), row_pair, f32_like(8, width_own)],
        [spot, back, inner, inner_sums, film, affine[1], *part_totals(rows)],
        [],
        16,
        0,
    )
    edges = edge_rows(last, head)
    grads_one = gathered_grads(grad_one)
    conv_grad = None
    if has_slots():
        conv_grad = kernel_grad(spot, both_blocks, grads_two, row_count, col_count, 1, conv_grad)
    time_grad = own_features.astype(jnp.float32)[0][:, None, None] * film_rows[None]
    text_grad = own_pooled.astype(jnp.float32)[0][:, None, None] * film_rows[None]
    kv_grad = jnp.einsum(
        "tx,ptd->pxd", own_text[0].astype(jnp.float32), text_all, precision=highest
    )
    back_parts = sent_parts(
        convolve_back(spot, grad_one, edges, kernel_one, row_count, col_count)
    )
    back_parts[0], conv_grad, time_grad, text_grad, kv_grad, result = lax.optimization_barrier(
        (back_parts[0], conv_grad, time_grad, text_grad, kv_grad, result)
    )
    back, rows = local_kernel(
        functools.partial(first_back_body, groups, pixel_count),
        [f32_like(*flat), f32_like(2, width_own)],
        [spot, *back_parts, own_pixels, first_sums, affine[0]],
        [],
        16,
        0,
    )
    row_parts = part_totals(rows)
    if has_slots():
        conv_grad = kernel_grad(spot, both_blocks, grads_one, row_count, col_count, 0, conv_grad)
    else:
        conv_grad = jnp.stack(
            [
                kernel_grad_whole(both_sends[0][:, 0], grads_one, row_count, col_count),
                kernel_grad_whole(both_sends[0][:, 1], grads_two, row_count, col_count),
            ]
        )
    back, conv_grad = lax.optimization_barrier((back, conv_grad))
    pixels_grad, first_rows = local_kernel(
        functools.partial(first_input_body, pixel_count),
        [f32_like(*flat), row_pair],
        [spot, back, own_pixels, first_sums, affine[0], grad_middle, *row_parts],
        [],
        16,
        0,
    )
    return (
        result.reshape(own_shape),
        pixels_grad.reshape(own_shape),
        conv_grad,
        time_grad,
        text_grad,
        jnp.stack([first_rows[0], second_rows[0]]),
        jnp.stack([first_rows[1], second_rows[1]]),
        second_rows[3],
        second_rows[4],
        attn_in_grad,
        kv_grad,
        self_grad,
        cross_grad,
    )


def solution(mesh):
    placed = (
        P(None, "wide", None, "tensor"),
        P(),
        P(),
        P(),
        P(None, None, "wide", "tensor"),
        P("wide", None, "tensor"),
        P("wide", None, "tensor"),
        P(None, "tensor"),
        P(None, "tensor"),
        P("tensor"),
        P("tensor"),
        P(None, "wide", "tensor"),
        P(None, "wide", "tensor"),
        P("tensor", "wide"),
        P("tensor", "wide"),
        P(None, "wide", None, "tensor"),
    )
    return jax.shard_map(
        shards,
        mesh=mesh,
        in_specs=placed,
        out_specs=(
            P(None, "wide", None, "tensor"),
            P(None, "wide", None, "tensor"),
            P(None, None, "wide", "tensor"),
            P("wide", None, "tensor"),
            P("wide", None, "tensor"),
            P(None, "tensor"),
            P(None, "tensor"),
            P("tensor"),
            P("tensor"),
            P(None, "wide", "tensor"),
            P(None, "wide", "tensor"),
            P("tensor", "wide"),
            P("tensor", "wide"),
        ),
        check_vma=False,
    )
```

```python
import functools
import math

import jax
import jax.numpy as jnp
from jax import lax
from jax.experimental import pallas as pl
from jax.experimental.pallas import tpu as pltpu
from jax.sharding import PartitionSpec as P

C = 1024
GROUPS = 32
HEAD_DIM = 128
TEXT = 128
TEMB = 1024
MIB = 1 << 20
in_vmem = pl.BlockSpec(memory_space=pltpu.VMEM)
in_smem = pl.BlockSpec(memory_space=pltpu.SMEM)


def local_kernel(body, outs, operands, scratch, limit, flops, aliases=None, out_specs=None):
    size = sum(a.size * a.dtype.itemsize for a in operands)
    size += sum(math.prod(o.shape) * o.dtype.itemsize for o in outs)
    return pl.pallas_call(
        body,
        grid=(1,),
        out_shape=outs,
        in_specs=[in_smem] + [in_vmem] * (len(operands) - 1),
        out_specs=[in_vmem] * len(outs) if out_specs is None else out_specs,
        scratch_shapes=scratch,
        input_output_aliases={} if aliases is None else aliases,
        compiler_params=pltpu.CompilerParams(vmem_limit_bytes=limit * MIB),
        cost_estimate=pl.CostEstimate(flops=flops, bytes_accessed=size, transcendentals=0),
        name=getattr(body, "func", body).__name__,
    )(*operands)


def far(arrays):
    return [pltpu.with_memory_space_constraint(array, pltpu.HBM) for array in arrays]


def turned(values, width):
    rows = values.shape[0]
    wide = values.astype(jnp.float32)
    column = lax.rem(lax.broadcasted_iota(jnp.int32, values.shape, 0), width)
    before = jnp.where(column == 0, 0.0, pltpu.roll(wide, 1, 0))
    after = jnp.where(column == width - 1, 0.0, pltpu.roll(wide, rows - 1, 0))
    return before.astype(jnp.bfloat16), values, after.astype(jnp.bfloat16)


def halves_swapped(values, odd):
    half = values.shape[1] // 2
    other = jnp.concatenate([values[:, half:], values[:, :half]], axis=1)
    return jnp.where(odd, other, values)


class Weights:
    def __init__(self, refs, spot, groups):
        self.refs = refs
        self.paired = len(refs) > 1
        self.groups = groups
        self.spot = spot
        self.odd = lax.rem(spot[0], 2) == 1

    def block(self, chunk):
        return lax.bitwise_xor(lax.div(self.spot[0], 2) if self.paired else self.spot[1], chunk)

    def tap(self, chunk, position):
        if not self.paired:
            each = self.refs[0].shape[0] // self.groups
            start = self.block(chunk) * each
            parts = [self.refs[0][start + i, position] for i in range(each)]
            return jnp.concatenate(parts, axis=0)
        parts = [self.refs[chunk][position], self.refs[4 + chunk][position]]
        return jnp.concatenate(parts, axis=0)

    def ordered(self, values):
        return halves_swapped(values, self.odd) if self.paired else values


def conv_body(groups, parts, count, rows, width, spot, *refs):
    pieces = refs[:groups]
    top, bottom = refs[groups : groups + 2]
    weights = Weights(refs[groups + 2 : groups + 2 + parts], spot, groups)
    source, *rest = refs[groups + 2 + parts :]
    earlier, rest = rest[:count], rest[count:]
    first_out, second_out, *sends, frame = rest
    for send, held in zip(sends, earlier):
        send[:, 0] = held[...]
    if earlier:
        sends = [send.at[:, 1] for send in sends]
    span = pieces[0].shape[1]
    for mask in range(groups):
        block = lax.bitwise_xor(spot[1], mask)
        own = pieces[mask][...]
        lanes = slice(mask * span, (mask + 1) * span)
        framed = jnp.concatenate([top[:, lanes], own, bottom[:, lanes]], axis=0)
        for column, values in enumerate(turned(weights.ordered(framed), width)):
            frame[block, column] = values
    total_sum = jnp.zeros(first_out.shape, jnp.float32)
    for chunk in range(groups):
        block = weights.block(chunk)
        for position in range(9):
            start = (position // 3) * width
            window = frame[block, position % 3, start : start + rows * width, :]
            total_sum += jnp.dot(
                window, weights.tap(chunk, position), preferred_element_type=jnp.float32
            )
        if len(sends) == 1:
            sends[0][chunk] = frame[chunk, 1, width : (rows + 1) * width, :]
        else:
            near = lax.bitwise_xor(lax.div(spot[0], 2), chunk)
            center = frame[near, 1, width : (rows + 1) * width, :]
            center = center if weights.paired else halves_swapped(center, weights.odd)
            sends[0][chunk] = center[:, : span // 2]
            sends[1][chunk] = center[:, span // 2 :]
    if second_out.shape[0] == 2:
        first_out[...] = total_sum
        second_out[...] = channel_sums(total_sum)
    else:
        middle = (source[...].astype(jnp.float32) + total_sum) * root_half
        first_out[...] = middle
        second_out[...] = middle.astype(jnp.bfloat16)


def back_body(groups, rows, width, spot, grad, top, bottom, *refs):
    frame, held = refs[-2:]
    outs = refs[-2 - groups : -2]
    weights = Weights(refs[: -2 - groups], spot, groups)
    framed = jnp.concatenate([top[...], grad[...], bottom[...]], axis=0)
    for column, values in enumerate(turned(framed, width)):
        frame[column] = values
    for chunk in range(groups):
        total_sum = jnp.zeros(held.shape[1:], jnp.float32)
        for position in range(9):
            start = (2 - position // 3) * width
            total_sum += lax.dot_general(
                frame[2 - position % 3, start : start + rows * width, :],
                weights.tap(chunk, position),
                (((1,), (1,)), ((), ())),
                preferred_element_type=jnp.float32,
            )
        held[weights.block(chunk)] = weights.ordered(total_sum).astype(jnp.bfloat16)
    for mask in range(groups):
        outs[mask][...] = held[lax.bitwise_xor(spot[1], mask)]


def bf16_like(*shape):
    return jax.ShapeDtypeStruct(shape, jnp.bfloat16)


def f32_like(*shape):
    return jax.ShapeDtypeStruct(shape, jnp.float32)


def flipped(values, axis, mask):
    count = lax.axis_size(axis)
    return lax.ppermute(values, axis, [(i, i ^ mask) for i in range(count)])


def relayed_block(over_x, over_y):
    odd = lax.rem(lax.axis_index("wide"), 2) == 1
    far_pairs = [(i, i ^ (2 if i % 2 else 4)) for i in range(8)]
    return lax.ppermute(jnp.where(odd, over_y, over_x), "wide", far_pairs)


def over_chips(values):
    over_x, over_y = flipped(values, "wide", 2), flipped(values, "wide", 4)
    return [values, over_x, over_y, relayed_block(over_x, over_y)]


def has_slots():
    return lax.axis_size("wide") == 8


def after(value, *others):
    return lax.optimization_barrier((value, others))[0]


def gathered_blocks(blocks):
    return [lax.all_gather(blocks, "wide")]


def spread_chips(values):
    if has_slots():
        return over_chips(values)
    mask = 2
    while mask < lax.axis_size("wide"):
        values = jnp.concatenate([values, flipped(values, "wide", mask)])
        mask *= 2
    return [values]


def gathered_sums(parts):
    if has_slots():
        return [parts[0]] + [flipped(parts[k], "wide", 2 * k) for k in range(1, 4)]
    values = parts[0]
    mask = lax.axis_size("wide") // 2
    while mask > 1:
        half = values.shape[0] // 2
        values = values[:half] + flipped(values[half:], "wide", mask)
        mask //= 2
    return [values]


def channel_pieces(values):
    count = lax.axis_size("tensor")
    return [values] + [flipped(values, "tensor", mask) for mask in range(1, count)]


def edge_rows(last, first):
    count = lax.axis_size("wide")
    above = lax.ppermute(last, "wide", [(i, i + 1) for i in range(count - 1)])
    below = lax.ppermute(first, "wide", [(i + 1, i) for i in range(count - 1)])
    return above, below


def convolve(spot, pieces, edges, kernel, source, second_shape, earlier, rows, width):
    groups, (area, span) = len(pieces), pieces[0].shape
    count, block = (2, span // 2) if has_slots() else (1, span)
    layers = (2,) if earlier else ()
    sends = [bf16_like(groups, *layers, area, block)] * count
    return local_kernel(
        functools.partial(conv_body, groups, len(kernel), len(earlier), rows, width),
        [f32_like(area, span), second_shape] + sends,
        [spot, *pieces, *edges, *far(kernel), source, *far(earlier)],
        [pltpu.VMEM((groups, 3, (rows + 2) * width, span), jnp.bfloat16)],
        32,
        2 * 9 * area * C * span,
    )


def piece_edges(pieces, width):
    return edge_rows(
        jnp.concatenate([piece[-width:] for piece in pieces], axis=1),
        jnp.concatenate([piece[:width] for piece in pieces], axis=1),
    )


def convolve_back(spot, grad, edges, kernel, rows, width):
    groups, (area, span) = lax.axis_size("tensor"), grad.shape
    return local_kernel(
        functools.partial(back_body, groups, rows, width),
        [bf16_like(area, span)] * groups,
        [spot, grad, *edges, *far(kernel)],
        [
            pltpu.VMEM((3, (rows + 2) * width, span), jnp.bfloat16),
            pltpu.VMEM((groups, area, span), jnp.bfloat16),
        ],
        32,
        2 * 9 * area * C * span,
    )


def sent_parts(parts):
    return [parts[0]] + [flipped(parts[mask], "tensor", mask) for mask in range(1, len(parts))]


def pair_blocks_body(spot, kept, got, *outs):
    for index, out in enumerate(outs):
        out[0] = kept[index + 1]
        out[1] = got[index + 1]


def kernel_grad_body(width, layer, spot, kept, got, *refs):
    *pairs, grads = refs[:4]
    out, turned_all = refs[-2:]
    area, span = kept.shape[2:]
    depth = 8 * area
    turned_all[:, :width] = jnp.zeros((3 * span, width), jnp.bfloat16)
    turned_all[:, depth + width :] = jnp.zeros((3 * span, width), jnp.bfloat16)
    pieces = [kept[0, layer], got[0, layer]]
    pieces += [pair[core, layer] for pair in pairs for core in range(2)]
    for mask, piece in enumerate(pieces):
        start = pl.multiple_of(lax.bitwise_xor(spot[0], mask) * area, area)
        for column, values in enumerate(turned(piece, width)):
            turned_all[column * span : (column + 1) * span, pl.ds(start + width, area)] = flat_turn(
                values
            )
    for row in range(3):
        product = jnp.dot(
            turned_all[:, row * width : row * width + depth],
            grads[layer],
            preferred_element_type=jnp.float32,
        )
        for column in range(3):
            out[0, 3 * row + column] = product[column * span : (column + 1) * span, :]


def swapped_blocks(spot, kept, sent):
    got = flipped(sent, "wide", 1)
    pairs = local_kernel(
        pair_blocks_body, [bf16_like(2, *kept.shape[1:])] * 3, [spot, *far([kept, got])], [], 16, 0
    )
    return [kept, got, *pairs]


def kernel_grad(spot, pieces, grads, rows, width, layer, earlier):
    span = pieces[0].shape[3]
    depth, columns = grads.shape[1:]
    operands = [spot, *far(pieces), *far([grads])]
    specs = [in_smem] + [in_vmem] * (len(operands) - 1)
    shape = f32_like(2, 9, span, columns)
    if earlier is not None:
        operands.append(earlier)
        specs.append(pl.BlockSpec(memory_space=pl.ANY))
    return pl.pallas_call(
        functools.partial(kernel_grad_body, width, layer),
        out_shape=shape,
        in_specs=specs,
        grid=(1,),
        out_specs=pl.BlockSpec((1, 9, span, columns), lambda i: (layer, 0, 0, 0)),
        scratch_shapes=[
            pltpu.VMEM((3 * span, depth + 2 * width), jnp.bfloat16),
        ],
        input_output_aliases={} if earlier is None else {len(operands) - 1: 0},
        compiler_params=pltpu.CompilerParams(vmem_limit_bytes=24 * MIB),
        cost_estimate=pl.CostEstimate(
            flops=2 * 9 * depth * span * columns, bytes_accessed=4 * MIB, transcendentals=0
        ),
    )(*operands)


def kernel_grad_whole(send, grads, rows, width):
    natural = jnp.moveaxis(send, 0, 1).reshape(1, rows, width, C)
    swapped = lax.all_to_all(natural, "wide", split_axis=3, concat_axis=1, tiled=True)
    framed = jnp.pad(swapped, ((0, 0), (1, 1), (1, 1), (0, 0)))
    low = grads.reshape(1, -1, width, grads.shape[1])
    return jnp.stack(
        [
            jnp.einsum(
                "mrwc,mrwd->cd",
                framed[:, tap // 3 : tap // 3 + low.shape[1], tap % 3 : tap % 3 + width, :],
                low,
                preferred_element_type=jnp.float32,
            )
            for tap in range(9)
        ]
    )


root_half = 1.0 / math.sqrt(2.0)
highest = lax.Precision.HIGHEST


def sinusoid(steps):
    half_width = TEMB // 2
    frequency = jnp.exp(-math.log(10000.0) * jnp.arange(half_width, dtype=jnp.float32) / half_width)
    angles = steps.astype(jnp.float32)[:, None] * frequency[None, :]
    return jnp.concatenate([jnp.cos(angles), jnp.sin(angles)], axis=1)


def chip_parts(values):
    if has_slots():
        return [values] + [flipped(values, "wide", mask) for mask in (2, 4, 6)]
    mask = 2
    while mask < lax.axis_size("wide"):
        values = values + flipped(values, "wide", mask)
        mask *= 2
    return [values]


def part_totals(rows):
    return chip_parts(rows + flipped(rows, "wide", 1))


def sum_of_parts(refs):
    if len(refs) == 1:
        return refs[0][...]
    return (refs[0][...] + refs[1][...]) + (refs[2][...] + refs[3][...])


def total(values, axis, mask=1):
    while mask < lax.axis_size(axis):
        values = values + flipped(values, axis, mask)
        mask *= 2
    return values


def silu_slope(values):
    logistic = lax.logistic(values)
    return logistic * (1.0 + values * (1.0 - logistic))


def channel_sums(values):
    return jnp.concatenate(
        [
            jnp.sum(values, axis=0, keepdims=True),
            jnp.sum(values * values, axis=0, keepdims=True),
        ],
        axis=0,
    )


def group_means(first, second, pixel_count):
    channels = first.shape[1]
    per_group = C // GROUPS
    row = lax.div(lax.broadcasted_iota(jnp.int32, (channels, channels), 0), per_group)
    column = lax.div(lax.broadcasted_iota(jnp.int32, (channels, channels), 1), per_group)
    same = jnp.where(row == column, 1.0, 0.0)
    rows = jnp.concatenate([first, second, jnp.zeros((6, channels), jnp.float32)], axis=0)
    means = jnp.dot(rows, same, precision=highest, preferred_element_type=jnp.float32)
    means = means / (pixel_count * per_group)
    return means[0:1], means[1:2]


def group_scale(first, second, pixel_count):
    center, square = group_means(first, second, pixel_count)
    return center, lax.rsqrt(square - center * center + 1e-05)


def lifted_sums(sums, film, pixel_count):
    slope, shift = 1.0 + film[0:1], film[1:2]
    plain, square = sums[0:1], sums[1:2]
    return (
        slope * plain + pixel_count * shift,
        slope * slope * square + 2.0 * slope * shift * plain + pixel_count * shift * shift,
    )


def silu_low(values):
    return (values * lax.logistic(values)).astype(jnp.bfloat16)


def first_norm_body(pixel_count, spot, pixels, affine, *refs):
    *parts, out, sums = refs
    sums[...] = sum_of_parts(parts)
    center, inverse = group_scale(sums[0:1], sums[1:2], pixel_count)
    scaled = (pixels[...].astype(jnp.float32) - center) * inverse
    out[...] = silu_low(scaled * affine[0:1] + affine[1:2])


def second_norm_body(pixel_count, spot, inner, affine, *refs):
    *parts, out, film, sums = refs
    summed = sum_of_parts(parts)
    film[...], sums[...] = summed[:2], summed[2:]
    center, inverse = group_scale(*lifted_sums(sums[...], film[...], pixel_count), pixel_count)
    lifted = inner[...] * (1.0 + film[0:1]) + film[1:2]
    out[...] = silu_low((lifted - center) * inverse * affine[0:1] + affine[1:2])


def parts_sum(refs):
    summed = refs[0][...].astype(jnp.float32)
    for ref in refs[1:]:
        summed += ref[...].astype(jnp.float32)
    return summed


def stacked_rows(rows):
    return jnp.concatenate([jnp.sum(row, axis=0, keepdims=True) for row in rows], axis=0)


def second_back_body(groups, pixel_count, spot, *refs):
    inner, sums, film, affine, terms, out, rows = refs[groups:]
    center, inverse = group_scale(*lifted_sums(sums[...], film[...], pixel_count), pixel_count)
    own = inner[...]
    scaled = (own * (1.0 + film[0:1]) + film[1:2] - center) * inverse
    back = parts_sum(refs[:groups]) * silu_slope(scaled * affine[0:1] + affine[1:2])
    out[...] = back
    rows[0:3, :] = stacked_rows([back * scaled, back, back * own])
    rows[3:5, :] = terms[...]
    rows[5:8, :] = jnp.zeros((3, own.shape[1]), jnp.float32)


def second_input_body(pixel_count, width, spot, back, inner, sums, film, affine, *refs):
    *parts, low, last, first, film_rows, rows = refs
    rows[...] = sum_of_parts(parts)
    slope, shift, gain = 1.0 + film[0:1], film[1:2], affine[0:1]
    plain_sum, square_sum = sums[0:1], sums[1:2]
    lifted_sum, lifted_square = lifted_sums(sums[...], film[...], pixel_count)
    center, inverse = group_scale(lifted_sum, lifted_square, pixel_count)
    dotted, plain = group_means(gain * rows[0:1], gain * rows[1:2], pixel_count)
    scaled = (inner[...] * slope + shift - center) * inverse
    grad = inverse * (back[...] * gain - plain - scaled * dotted)
    grad_low = (grad * slope).astype(jnp.bfloat16)
    low[...] = grad_low
    last[...] = grad_low[-width:]
    first[...] = grad_low[:width]
    scaled_sum = inverse * (lifted_sum - pixel_count * center)
    scaled_inner = inverse * (slope * square_sum + (shift - center) * plain_sum)
    film_rows[0:1, :] = inverse * (
        gain * rows[2:3] - plain * plain_sum - dotted * scaled_inner
    )
    film_rows[1:2, :] = inverse * (
        gain * rows[1:2] - pixel_count * plain - dotted * scaled_sum
    )


def first_back_body(groups, pixel_count, spot, *refs):
    pixels, sums, affine, out, rows = refs[groups:]
    center, inverse = group_scale(sums[0:1], sums[1:2], pixel_count)
    scaled = (pixels[...].astype(jnp.float32) - center) * inverse
    back = parts_sum(refs[:groups]) * silu_slope(scaled * affine[0:1] + affine[1:2])
    out[...] = back
    rows[...] = stacked_rows([back * scaled, back])


def first_input_body(pixel_count, spot, back, pixels, sums, affine, middle, second, *refs):
    *parts, out, gains, biases = refs
    rows = sum_of_parts(parts)
    gains[...] = jnp.concatenate([rows[0:1], second[0:1]], axis=0)
    biases[...] = jnp.concatenate([rows[1:2], second[1:2]], axis=0)
    gain = affine[0:1]
    center, inverse = group_scale(sums[0:1], sums[1:2], pixel_count)
    dotted, plain = group_means(gain * rows[0:1], gain * rows[1:2], pixel_count)
    scaled = (pixels[...].astype(jnp.float32) - center) * inverse
    out[...] = inverse * (back[...] * gain - plain - scaled * dotted) + middle[...] * root_half


def dot(left, right):
    return jnp.dot(left, right, preferred_element_type=jnp.float32)


def dot_last(left, right):
    return lax.dot_general(
        left, right, (((1,), (1,)), ((), ())), preferred_element_type=jnp.float32
    )


def flat_turn(values):
    return jnp.transpose(values.astype(jnp.float32)).astype(jnp.bfloat16)


def dot_first(left, right):
    return dot(flat_turn(left), right)


def head_choice(values, odd):
    first, second = values[:, :HEAD_DIM], values[:, HEAD_DIM:]
    return jnp.where(odd, second, first), jnp.where(odd, first, second)


def heads_joined(kept, received, odd):
    return jnp.where(
        odd,
        jnp.concatenate([received, kept], axis=1),
        jnp.concatenate([kept, received], axis=1),
    )


def packed_rows(values):
    rows = []
    for _ in range(3):
        rows.append(values.astype(jnp.bfloat16).astype(jnp.float32))
        values = values - rows[-1]
    rows.append(jnp.zeros((10, values.shape[1]), jnp.float32))
    return jnp.concatenate(rows, axis=0).astype(jnp.bfloat16)


def unpacked_rows(packed, area):
    rows = packed[area:, :].astype(jnp.float32)
    return rows[0:1] + rows[2:3] + rows[4:5], rows[1:2] + rows[3:4] + rows[5:6]


def prepare_body(spot, pixels, cotangent, gain, bias, pack, sums):
    area = cotangent.shape[0]
    pack[:area] = cotangent[...].astype(jnp.bfloat16)
    pack[area:] = packed_rows(jnp.concatenate([gain[...], bias[...]], axis=0))
    sums[...] = channel_sums(pixels[...].astype(jnp.float32))


def project_body(groups, spot, *refs):
    pieces, packs = refs[:groups], refs[groups : 2 * groups]
    own, maps, keep_query, keep, send, cross, normed, scaled, center, inverse = refs[2 * groups :]
    weights = Weights([maps], spot, groups)
    odd = lax.rem(spot[0], 2) == 1
    area = own.shape[0]
    token_sum = token_square = 0.0
    for piece in pieces:
        values = piece[...].astype(jnp.float32)
        token_sum += jnp.sum(values, axis=1, keepdims=True)
        token_square += jnp.sum(values * values, axis=1, keepdims=True)
    mean = token_sum / C
    scale = lax.rsqrt(token_square / C - mean * mean + 1e-05)
    lows = []
    for mask in range(groups):
        gain, bias = unpacked_rows(packs[mask], area)
        values = (pieces[mask][...].astype(jnp.float32) - mean) * scale
        lows.append((values * gain + bias).astype(jnp.bfloat16))
        normed[lax.bitwise_xor(spot[1], mask)] = lows[-1]
    center[...] = mean
    inverse[...] = scale
    scaled[...] = (own[...] - mean) * scale
    projected = []
    for position in range(4):
        total_sum = 0.0
        for mask in range(groups):
            total_sum += dot(lows[mask], weights.tap(mask, position))
        projected.append(total_sum.astype(jnp.bfloat16))
    cross[...] = projected[3]
    chosen = [head_choice(values, odd) for values in projected[:3]]
    chosen = chosen[1:] + chosen[:1]
    keep_query[...] = chosen[2][0]
    keep[...] = jnp.concatenate([pair[0] for pair in chosen[:2]], axis=1)
    send[...] = jnp.concatenate([pair[1] for pair in chosen], axis=1)


def out_grad_body(groups, spot, *refs):
    packs = refs[:groups]
    maps, keep, send, cross = refs[groups:]
    weights = Weights([maps], spot, groups)
    sums = []
    for position in (4, 5):
        total_sum = 0.0
        for mask in range(groups):
            total_sum += dot(packs[mask][: cross.shape[0]], weights.tap(mask, position))
        sums.append(total_sum.astype(jnp.bfloat16))
    kept, sent = head_choice(sums[0], lax.rem(spot[0], 2) == 1)
    keep[...] = kept
    send[...] = sent
    cross[...] = sums[1]


def text_out_body(spot, film, features, pooled, text, parts, time_grad, text_grad, kv_grad):
    for rows, out in ((features, time_grad), (pooled, text_grad)):
        column = jnp.transpose(jnp.broadcast_to(rows[...].astype(jnp.float32), (8, rows.shape[1])))
        for part in range(2):
            out[:, part, :] = column[:, 0:1] * film[part : part + 1, :]
    summed = leading_sum(parts)
    turned_text = flat_turn(text[...])
    for part in range(2):
        high = summed[part].astype(jnp.bfloat16)
        low = (summed[part] - high.astype(jnp.float32)).astype(jnp.bfloat16)
        kv_grad[part] = dot(turned_text, high) + dot(turned_text, low)


def mix_body(groups, spot, kept, received, crossed, maps, *outs):
    weights = Weights([maps], spot, groups)
    attended = heads_joined(
        kept[...], received[:, 3 * HEAD_DIM :], lax.rem(spot[0], 2) == 1
    )
    for mask in range(groups):
        total_sum = dot_last(attended, weights.tap(mask, 4))
        total_sum += dot_last(crossed[...], weights.tap(mask, 5))
        outs[mask][...] = total_sum.astype(jnp.bfloat16)


def over_rows(refs, step, state):
    for index, ref in enumerate(refs):
        rows = ref.shape[0]
        if rows <= 512:
            state = step(state, ref[...], index, 0)
        else:
            state = lax.fori_loop(
                0,
                rows // 512,
                lambda i, held: step(
                    held, ref[pl.ds(pl.multiple_of(i * 512, 512), 512), :], index, i * 512
                ),
                state,
            )
    return state


score_scale = HEAD_DIM ** (-0.5)


def attend_body(count, spot, kept_query, got, kept_grad, got_grad, *refs):
    blocks, parts = refs[:count], refs[count : 2 * count]
    keep_out, send_out, keep_query, send_query = refs[2 * count :]
    query = jnp.concatenate([kept_query[...], got[:, 2 * HEAD_DIM :]], axis=0)
    grad = jnp.concatenate([kept_grad[...], got_grad[...]], axis=0)
    queries = query.shape[0]

    def forward(state, block, index, start):
        top, weight_sum, weighted = state
        scores = dot_last(block[:, :HEAD_DIM], query) * score_scale
        raised = jnp.maximum(top, jnp.max(scores, axis=0, keepdims=True))
        rescale = jnp.exp(top - raised)
        weights = jnp.exp(scores - raised)
        weight_sum = weight_sum * rescale + jnp.sum(weights, axis=0, keepdims=True)
        values = block[:, HEAD_DIM:]
        weighted = weighted * rescale + dot_first(values, weights.astype(jnp.bfloat16))
        return raised, weight_sum, weighted

    top, weight_sum, weighted = over_rows(
        blocks,
        forward,
        (
            jnp.full((1, queries), -1e30, jnp.float32),
            jnp.zeros((1, queries), jnp.float32),
            jnp.zeros((HEAD_DIM, queries), jnp.float32),
        ),
    )
    attended = weighted / weight_sum
    delta = jnp.sum(attended * jnp.transpose(grad.astype(jnp.float32)), axis=0, keepdims=True)
    log_sum = top + jnp.log(weight_sum)

    def backward(state, block, index, start):
        keys, values = block[:, :HEAD_DIM], block[:, HEAD_DIM:]
        probs = jnp.exp(dot_last(keys, query) * score_scale - log_sum)
        grad_values = dot(probs.astype(jnp.bfloat16), grad)
        grad_scores = (probs * (dot_last(values, grad) - delta)).astype(jnp.bfloat16)
        grad_keys = dot(grad_scores, query) * score_scale
        rows = pl.ds(start if isinstance(start, int) else pl.multiple_of(start, 512), block.shape[0])
        parts[index][rows, :] = jnp.concatenate([grad_keys, grad_values], axis=1).astype(
            jnp.bfloat16
        )
        return state + dot_first(keys, grad_scores)

    flat = over_rows(blocks, backward, jnp.zeros((HEAD_DIM, queries), jnp.float32))
    for values, keep, send in (
        (attended, keep_out, send_out),
        (flat * score_scale, keep_query, send_query),
    ):
        turned_back = jnp.transpose(values).astype(jnp.bfloat16)
        keep[...] = turned_back[: queries // 2]
        send[...] = turned_back[queries // 2 :]


def key_sum_body(spot, sent_query, sent_out, *refs):
    *parts, keep, send = refs
    both = parts_sum(parts).astype(jnp.bfloat16)
    half = keep.shape[0]
    keep[...] = both[:half]
    send[:, : 2 * HEAD_DIM] = both[half:]
    send[:, 2 * HEAD_DIM : 3 * HEAD_DIM] = sent_query[...]
    send[:, 3 * HEAD_DIM :] = sent_out[...]


def leading_sum(ref):
    summed = ref[0].astype(jnp.float32)
    for index in range(1, ref.shape[0]):
        summed += ref[index].astype(jnp.float32)
    return summed


def cross_body(spot, query, grad, parts, crossed, grad_query, text_grad):
    text = leading_sum(parts).astype(jnp.bfloat16)
    live = lax.broadcasted_iota(jnp.int32, (query.shape[0], text.shape[1]), 1) < spot[2]
    for head in range(query.shape[1] // HEAD_DIM):
        lanes = slice(head * HEAD_DIM, (head + 1) * HEAD_DIM)
        own, keys, values, back = query[:, lanes], text[0, :, lanes], text[1, :, lanes], grad[:, lanes]
        scores = jnp.where(live, dot_last(own, keys) * score_scale, -1e30)
        weights = jnp.exp(scores - jnp.max(scores, axis=1, keepdims=True))
        probs = weights / jnp.sum(weights, axis=1, keepdims=True)
        low = probs.astype(jnp.bfloat16)
        crossed[:, lanes] = dot(low, values).astype(jnp.bfloat16)
        grad_probs = dot_last(back, values)
        grad_scores = probs * (grad_probs - jnp.sum(probs * grad_probs, axis=1, keepdims=True))
        grad_low = grad_scores.astype(jnp.bfloat16)
        grad_query[:, lanes] = (dot(grad_low, keys) * score_scale).astype(jnp.bfloat16)
        text_grad[0, :, lanes] = (dot_first(grad_low, own) * score_scale).astype(jnp.bfloat16)
        text_grad[1, :, lanes] = dot_first(low, back).astype(jnp.bfloat16)


def joined_grads(spot, kept_query, kept_pair, got, cross):
    odd = lax.rem(spot[0], 2) == 1
    parts = [got[:, i * HEAD_DIM : (i + 1) * HEAD_DIM] for i in range(3)]
    return [
        heads_joined(kept_query[...], parts[2], odd),
        heads_joined(kept_pair[:, :HEAD_DIM], parts[0], odd),
        heads_joined(kept_pair[:, HEAD_DIM:], parts[1], odd),
        cross[...],
    ]


def project_back_body(groups, spot, kq, kp, got, cross, center, inverse, maps, *refs):
    pieces, packs = refs[:groups], refs[groups : 2 * groups]
    outs = refs[2 * groups :]
    weights = Weights([maps], spot, groups)
    grads = joined_grads(spot, kq, kp, got, cross)
    area = cross.shape[0]
    plain = dotted = 0.0
    for mask in range(groups):
        part = 0.0
        for position in range(4):
            part += dot_last(grads[position], weights.tap(mask, position))
        outs[mask][:area] = part.astype(jnp.bfloat16)
        eased = part * unpacked_rows(packs[mask], part.shape[0])[0]
        unit = (pieces[mask][...].astype(jnp.float32) - center[...]) * inverse[...]
        plain += eased
        dotted += eased * unit
    ones = jnp.ones((8, plain.shape[1]), jnp.float32)
    sums = [
        lax.dot_general(
            ones,
            values,
            (((1,), (1,)), ((), ())),
            precision=highest,
            preferred_element_type=jnp.float32,
        )[0:1]
        for values in (plain, dotted)
    ]
    packed = packed_rows(jnp.concatenate(sums, axis=0))
    for out in outs:
        out[area:] = packed


def weight_grad_body(groups, spot, kq, kp, got, cross, kept, crossed, normed, *refs):
    packs, (out, frame) = refs[:groups], refs[groups:]
    odd = lax.rem(spot[0], 2) == 1
    area, span = cross.shape
    right = jnp.concatenate(joined_grads(spot, kq, kp, got, cross), axis=1)
    out_right = jnp.concatenate(
        [heads_joined(kept[...], got[:, 3 * HEAD_DIM :], odd), crossed[...]], axis=1
    )
    for mask in range(groups):
        frame[lax.bitwise_xor(spot[1], mask)] = packs[mask][:area]
    for chunk in range(groups):
        rows = slice(chunk * span, (chunk + 1) * span)
        out[rows, : 4 * span] = dot_first(normed[chunk], right).astype(jnp.bfloat16)
        out[rows, 4 * span :] = dot_first(frame[chunk], out_right).astype(jnp.bfloat16)


def weight_out_body(spot, sums, in_grad, self_grad, cross_grad):
    summed = sums[...].astype(jnp.float32)
    span = in_grad.shape[2]
    for position in range(4):
        in_grad[position] = summed[:, position * span : (position + 1) * span]
    self_grad[...] = jnp.transpose(summed[:, 4 * span : 5 * span])
    cross_grad[...] = jnp.transpose(summed[:, 5 * span :])


def norm_back_body(groups, width, spot, *refs):
    scaled, inverse, cotangent, gain, middle, low, last, first, terms = refs[groups:]
    area = scaled.shape[0]
    grad = plain = dotted = 0.0
    for ref in refs[:groups]:
        grad += ref[:area].astype(jnp.float32)
        sums = unpacked_rows(ref, area)
        plain, dotted = plain + sums[0], dotted + sums[1]
    same = lax.broadcasted_iota(jnp.int32, (area, area), 0) == lax.broadcasted_iota(
        jnp.int32, (area, area), 1
    )
    plain = jnp.sum(jnp.where(same, plain, 0.0), axis=1, keepdims=True) / C
    dotted = jnp.sum(jnp.where(same, dotted, 0.0), axis=1, keepdims=True) / C
    unit = scaled[...]
    terms[0:1, :] = jnp.sum(grad * unit, axis=0, keepdims=True)
    terms[1:2, :] = jnp.sum(grad, axis=0, keepdims=True)
    back = inverse[...] * (grad * gain[...] - plain - unit * dotted) + cotangent[...]
    middle[...] = back
    grad_low = (back * root_half).astype(jnp.bfloat16)
    low[...] = grad_low
    last[...] = grad_low[-width:]
    first[...] = grad_low[:width]


def shards(
    pixels,
    text_states,
    text_length,
    timestep,
    conv_weights,
    film_time,
    film_text,
    group_gain,
    group_bias,
    layer_gain,
    layer_bias,
    attn_in,
    text_kv,
    out_self,
    out_cross,
    cotangent,
):
    map_count, row_count, col_count, width_own = pixels.shape
    token_count = row_count * col_count
    groups = lax.axis_size("tensor")
    pixel_count = token_count * lax.axis_size("wide")
    own_shape = (map_count, row_count, col_count, width_own)
    flat = (token_count, width_own)
    half = (token_count, HEAD_DIM)
    square = 2 * token_count * C * width_own
    edge = (col_count, width_own)
    spot = jnp.stack([lax.axis_index("wide"), lax.axis_index("tensor"), text_length[0]])
    spot = spot.astype(jnp.int32)
    own_pixels = pixels.reshape(flat)
    flat_cotangent = cotangent.reshape(flat)
    affine = [jnp.stack([group_gain[layer], group_bias[layer]]) for layer in range(2)]

    pack, sums = local_kernel(
        prepare_body,
        [bf16_like(token_count + 16, width_own), f32_like(2, width_own)],
        [spot, *far([own_pixels, flat_cotangent, layer_gain[None], layer_bias[None]])],
        [],
        8,
        0,
    )
    first_parts = part_totals(sums)
    kernel_one = gathered_blocks(conv_weights[0])
    maps = jnp.concatenate(
        [attn_in, jnp.transpose(jnp.stack([out_self, out_cross]), (0, 2, 1))], axis=0
    )
    maps = gathered_blocks(maps)[0]

    features = sinusoid(timestep).astype(jnp.bfloat16)
    present = jnp.arange(TEXT)[None, :] < text_length[:, None]
    pooled = jnp.einsum(
        "mtx,mt->mx", text_states, present.astype(jnp.bfloat16), preferred_element_type=jnp.float32
    )
    pooled = (pooled / text_length.astype(jnp.float32)[:, None]).astype(jnp.bfloat16)
    wide_index = lax.axis_index("wide")
    time_rows = film_time.shape[0]
    text_rows = film_text.shape[0]
    own_features = lax.dynamic_slice_in_dim(features, wide_index * time_rows, time_rows, 1)
    own_pooled = lax.dynamic_slice_in_dim(pooled, wide_index * text_rows, text_rows, 1)
    own_text = lax.dynamic_slice_in_dim(text_states, wide_index * text_rows, text_rows, 2)
    film_term = jnp.einsum(
        "mk,ksc->msc", own_features, film_time, preferred_element_type=jnp.float32
    ) + jnp.einsum("mk,ksc->msc", own_pooled, film_text, preferred_element_type=jnp.float32)
    text_term = jnp.einsum("mtx,pxd->pmtd", own_text, text_kv, preferred_element_type=jnp.float32)
    text_term = text_term.astype(jnp.bfloat16).reshape(2, TEXT, width_own)

    row_pair = f32_like(2, width_own)
    first, first_sums = local_kernel(
        functools.partial(first_norm_body, pixel_count),
        [bf16_like(*flat), row_pair],
        [spot, own_pixels, affine[0], *first_parts],
        [],
        8,
        0,
    )
    pieces = channel_pieces(first)
    edges = piece_edges(pieces, col_count)
    later = after(conv_weights, first)[1]
    if has_slots():
        kernel_two = over_chips(later)
        kernel_two += [flipped(part, "wide", 1) for part in kernel_two]
    else:
        kernel_two = gathered_blocks(later)
    packs = channel_pieces(after(pack, pieces))
    pieces[0] = after(pieces[0], film_term, packs, text_term)
    inner, sums, *first_sends = convolve(
        spot, pieces, edges, kernel_one, own_pixels, row_pair, [], row_count, col_count
    )
    inner_parts = part_totals(jnp.concatenate([film_term[0], sums]))
    second, film, inner_sums = local_kernel(
        functools.partial(second_norm_body, pixel_count),
        [bf16_like(*flat), row_pair, row_pair],
        [spot, inner, affine[1], *inner_parts],
        [],
        8,
        0,
    )
    text_all = lax.all_gather(after(text_term, second), "wide")
    second = after(second, kernel_two)
    pieces = channel_pieces(second)
    edges = piece_edges(pieces, col_count)
    middle, middle_low, *both_sends = convolve(
        spot,
        pieces,
        edges,
        kernel_two,
        own_pixels,
        bf16_like(*flat),
        first_sends,
        row_count,
        col_count,
    )

    middle_pieces = channel_pieces(middle_low)
    kept_grad, sent_grad, grad_crossed = local_kernel(
        functools.partial(out_grad_body, groups),
        [bf16_like(*half), bf16_like(*half), bf16_like(*flat)],
        [spot, *far([after(packs[0], middle_low)] + packs[1:]), *far([maps])],
        [],
        16,
        2 * square,
    )
    got_grad = flipped(sent_grad, "wide", 1)
    middle_pieces[0] = after(middle_pieces[0], got_grad)
    column = f32_like(token_count, 1)
    triple = bf16_like(token_count, 3 * HEAD_DIM)
    kept_query, kept_pair, sent, cross_query, normed, scaled, center, inverse = local_kernel(
        functools.partial(project_body, groups),
        [
            bf16_like(*half),
            bf16_like(*flat),
            triple,
            bf16_like(*flat),
            bf16_like(groups, *flat),
            f32_like(*flat),
            column,
            column,
        ],
        [spot, *middle_pieces, *far(packs), middle, *far([maps])],
        [],
        24,
        4 * square,
    )
    got = flipped(sent, "wide", 1)
    blocks = spread_chips(jnp.concatenate([kept_pair, got[:, : 2 * HEAD_DIM]]))
    if has_slots():
        both_blocks = swapped_blocks(spot, after(both_sends[0], blocks[:2][-1]), both_sends[1])
        got_grad = after(got_grad, both_blocks)
    crossed, grad_cross_query, text_grads = local_kernel(
        cross_body,
        [bf16_like(*flat), bf16_like(*flat), bf16_like(2, TEXT, width_own)],
        [spot, after(cross_query, blocks[:2][-1]), grad_crossed, *far([text_all])],
        [],
        24,
        12 * token_count * TEXT * width_own,
    )
    got_grad = after(got_grad, crossed)
    text_sums = lax.all_gather(text_grads, "wide")
    *key_parts, kept_out, sent_out, kept_dq, sent_dq = local_kernel(
        functools.partial(attend_body, len(blocks)),
        [bf16_like(*block.shape) for block in blocks] + [bf16_like(*half)] * 4,
        [spot, kept_query, got, kept_grad, got_grad, *blocks],
        [],
        40,
        14 * (2 * token_count) * HEAD_DIM * pixel_count,
    )
    kept_dk, sent_all = local_kernel(
        key_sum_body,
        [bf16_like(*flat), bf16_like(token_count, 4 * HEAD_DIM)],
        [spot, sent_dq, sent_out, *gathered_sums(key_parts)],
        [],
        16,
        0,
    )
    got_all = flipped(sent_all, "wide", 1)
    projected_grads = [kept_dq, kept_dk, got_all, grad_cross_query]
    norm_parts = local_kernel(
        functools.partial(project_back_body, groups),
        [bf16_like(token_count + 16, width_own)] * groups,
        [spot, *projected_grads, center, inverse, *far([maps]), *far(middle_pieces), *far(packs)],
        [],
        24,
        4 * square,
    )
    received = sent_parts(norm_parts)
    if has_slots():
        near = [flipped(after(both_blocks[2 + k], norm_parts[0]), "wide", 2 * k + 2) for k in range(2)]
        received[0] = after(received[0], near)
    grad_middle, grad_two, last, head, terms = local_kernel(
        functools.partial(norm_back_body, groups, col_count),
        [
            f32_like(*flat),
            bf16_like(*flat),
            bf16_like(*edge),
            bf16_like(*edge),
            f32_like(2, width_own),
        ],
        [
            spot,
            *received,
            scaled,
            inverse,
            flat_cotangent,
            layer_gain[None],
        ],
        [],
        16,
        0,
    )

    edges = edge_rows(last, head)
    weight_parts, = local_kernel(
        functools.partial(weight_grad_body, groups),
        [bf16_like(C, 6 * width_own)],
        [
            spot,
            after(projected_grads[0], grad_two),
            *projected_grads[1:],
            kept_out,
            crossed,
            *far([normed]),
            *far(packs),
        ],
        [pltpu.VMEM((groups, *flat), jnp.bfloat16)],
        24,
        6 * square,
    )
    weight_sums = lax.psum_scatter(weight_parts, "wide", scatter_dimension=0, tiled=True)
    back_parts = convolve_back(
        spot, after(grad_two, weight_parts), edges, kernel_two, row_count, col_count
    )
    back_parts = sent_parts(back_parts)
    back, rows = local_kernel(
        functools.partial(second_back_body, groups, pixel_count),
        [f32_like(*flat), f32_like(8, width_own)],
        [spot, *back_parts, inner, inner_sums, film, affine[1], terms],
        [],
        16,
        0,
    )
    mixed = local_kernel(
        functools.partial(mix_body, groups),
        [bf16_like(*flat)] * groups,
        [spot, after(kept_out, back), got_all, crossed, *far([maps])],
        [],
        16,
        2 * square,
    )
    grad_one, last, head, film_rows, second_rows = local_kernel(
        functools.partial(second_input_body, pixel_count, col_count),
        [bf16_like(*flat), bf16_like(*edge), bf16_like(*edge), row_pair, f32_like(8, width_own)],
        [spot, back, inner, inner_sums, film, affine[1], *part_totals(rows)],
        [],
        16,
        0,
    )
    edges = edge_rows(last, head)
    mixed = sent_parts([after(part, grad_one) for part in mixed])
    both_grads = lax.all_gather(jnp.stack([grad_one, grad_two]), "wide", axis=1, tiled=True)
    back_parts = convolve_back(spot, grad_one, edges, kernel_one, row_count, col_count)
    if has_slots():
        distant = flipped(after(both_blocks[4], back_parts[0]), "wide", 6)
        both_blocks = both_blocks[:2] + near + [distant]
    attn_in_grad, self_grad, cross_grad = local_kernel(
        weight_out_body,
        [f32_like(4, C // lax.axis_size("wide"), width_own)]
        + [f32_like(width_own, C // lax.axis_size("wide"))] * 2,
        [spot, after(weight_sums, back_parts[0])],
        [],
        16,
        0,
    )
    back_parts = sent_parts(back_parts)
    film_rows = after(film_rows, back_parts[1])
    result = middle
    for part in mixed:
        result = result + part.astype(jnp.float32)
    time_grad, text_grad, kv_grad = local_kernel(
        text_out_body,
        [
            f32_like(time_rows, 2, width_own),
            f32_like(text_rows, 2, width_own),
            f32_like(2, text_rows, width_own),
        ],
        [spot, film_rows, own_features, own_pooled, own_text[0], *far([text_sums])],
        [],
        24,
        4 * TEXT * text_rows * width_own,
    )
    back_parts[0], attn_in_grad, result, time_grad = lax.optimization_barrier(
        (back_parts[0], attn_in_grad, result, time_grad)
    )
    back, rows = local_kernel(
        functools.partial(first_back_body, groups, pixel_count),
        [f32_like(*flat), f32_like(2, width_own)],
        [spot, *back_parts, own_pixels, first_sums, affine[0]],
        [],
        16,
        0,
    )
    row_parts = part_totals(rows)
    if has_slots():
        conv_grad = kernel_grad(spot, both_blocks, both_grads, row_count, col_count, 1, None)
        conv_grad = kernel_grad(spot, both_blocks, both_grads, row_count, col_count, 0, conv_grad)
    else:
        conv_grad = jnp.stack(
            [
                kernel_grad_whole(both_sends[0][:, k], both_grads[k], row_count, col_count)
                for k in range(2)
            ]
        )
    pixels_grad, gain_grad, bias_grad = local_kernel(
        functools.partial(first_input_body, pixel_count),
        [f32_like(*flat), row_pair, row_pair],
        [spot, back, own_pixels, first_sums, affine[0], grad_middle, second_rows, *row_parts],
        [],
        16,
        0,
    )
    return (
        result.reshape(own_shape),
        pixels_grad.reshape(own_shape),
        conv_grad,
        time_grad,
        text_grad,
        gain_grad,
        bias_grad,
        second_rows[3],
        second_rows[4],
        attn_in_grad,
        kv_grad,
        self_grad,
        cross_grad,
    )


def solution(mesh):
    placed = (
        P(None, "wide", None, "tensor"),
        P(),
        P(),
        P(),
        P(None, None, "wide", "tensor"),
        P("wide", None, "tensor"),
        P("wide", None, "tensor"),
        P(None, "tensor"),
        P(None, "tensor"),
        P("tensor"),
        P("tensor"),
        P(None, "wide", "tensor"),
        P(None, "wide", "tensor"),
        P("tensor", "wide"),
        P("tensor", "wide"),
        P(None, "wide", None, "tensor"),
    )
    return jax.shard_map(
        shards,
        mesh=mesh,
        in_specs=placed,
        out_specs=(
            P(None, "wide", None, "tensor"),
            P(None, "wide", None, "tensor"),
            P(None, None, "wide", "tensor"),
            P("wide", None, "tensor"),
            P("wide", None, "tensor"),
            P(None, "tensor"),
            P(None, "tensor"),
            P("tensor"),
            P("tensor"),
            P(None, "wide", "tensor"),
            P(None, "wide", "tensor"),
            P("tensor", "wide"),
            P("tensor", "wide"),
        ),
        check_vma=False,
    )
```

```python
import functools
import math

import jax
import jax.numpy as jnp
from jax import lax
from jax.experimental import pallas as pl
from jax.experimental.pallas import tpu as pltpu
from jax.sharding import PartitionSpec as P

C = 1024
GROUPS = 32
HEAD_DIM = 128
TEXT = 128
TEMB = 1024
MIB = 1 << 20
in_vmem = pl.BlockSpec(memory_space=pltpu.VMEM)
in_smem = pl.BlockSpec(memory_space=pltpu.SMEM)


def local_kernel(body, outs, operands, scratch, limit, flops, aliases=None, out_specs=None):
    size = sum(a.size * a.dtype.itemsize for a in operands)
    size += sum(math.prod(o.shape) * o.dtype.itemsize for o in outs)
    return pl.pallas_call(
        body,
        grid=(1,),
        out_shape=outs,
        in_specs=[in_smem] + [in_vmem] * (len(operands) - 1),
        out_specs=[in_vmem] * len(outs) if out_specs is None else out_specs,
        scratch_shapes=scratch,
        input_output_aliases={} if aliases is None else aliases,
        compiler_params=pltpu.CompilerParams(vmem_limit_bytes=limit * MIB),
        cost_estimate=pl.CostEstimate(flops=flops, bytes_accessed=size, transcendentals=0),
        name=getattr(body, "func", body).__name__,
    )(*operands)


def far(arrays):
    return [pltpu.with_memory_space_constraint(array, pltpu.HBM) for array in arrays]


def turned(values, width):
    rows = values.shape[0]
    wide = values.astype(jnp.float32)
    column = lax.rem(lax.broadcasted_iota(jnp.int32, values.shape, 0), width)
    before = jnp.where(column == 0, 0.0, pltpu.roll(wide, 1, 0))
    after = jnp.where(column == width - 1, 0.0, pltpu.roll(wide, rows - 1, 0))
    return before.astype(jnp.bfloat16), values, after.astype(jnp.bfloat16)


def halves_swapped(values, odd):
    half = values.shape[1] // 2
    other = jnp.concatenate([values[:, half:], values[:, :half]], axis=1)
    return jnp.where(odd, other, values)


class Weights:
    def __init__(self, refs, spot, groups):
        self.refs = refs
        self.paired = len(refs) > 1
        self.groups = groups
        self.spot = spot
        self.odd = lax.rem(spot[0], 2) == 1

    def block(self, chunk):
        return lax.bitwise_xor(lax.div(self.spot[0], 2) if self.paired else self.spot[1], chunk)

    def tap(self, chunk, position):
        if not self.paired:
            each = self.refs[0].shape[0] // self.groups
            start = self.block(chunk) * each
            parts = [self.refs[0][start + i, position] for i in range(each)]
            return jnp.concatenate(parts, axis=0)
        parts = [self.refs[chunk][position], self.refs[4 + chunk][position]]
        return jnp.concatenate(parts, axis=0)

    def ordered(self, values):
        return halves_swapped(values, self.odd) if self.paired else values


def conv_body(groups, parts, count, rows, width, spot, *refs):
    pieces = refs[:groups]
    near, far_row = refs[groups : groups + 2]
    weights = Weights(refs[groups + 2 : groups + 2 + parts], spot, groups)
    source, *rest = refs[groups + 2 + parts :]
    earlier, rest = rest[:count], rest[count:]
    first_out, second_out, *sends, frame = rest
    for send, held in zip(sends, earlier):
        send[:, 0] = held[...]
    if earlier:
        sends = [send.at[:, 1] for send in sends]
    span = pieces[0].shape[1]
    for mask in range(groups):
        block = lax.bitwise_xor(spot[1], mask)
        own = pieces[mask][...]
        lanes = slice(mask * span, (mask + 1) * span)
        framed = framed_rows(near[:, lanes], far_row[:, lanes], own, weights.odd)
        for column, values in enumerate(turned(weights.ordered(framed), width)):
            frame[block, column] = values
    total_sum = jnp.zeros(first_out.shape, jnp.float32)
    for chunk in range(groups):
        block = weights.block(chunk)
        for position in range(9):
            start = (position // 3) * width
            window = frame[block, position % 3, start : start + rows * width, :]
            total_sum += jnp.dot(
                window, weights.tap(chunk, position), preferred_element_type=jnp.float32
            )
        if len(sends) == 1:
            sends[0][chunk] = frame[chunk, 1, width : (rows + 1) * width, :]
        else:
            near = lax.bitwise_xor(lax.div(spot[0], 2), chunk)
            center = frame[near, 1, width : (rows + 1) * width, :]
            center = center if weights.paired else halves_swapped(center, weights.odd)
            sends[0][chunk] = center[:, : span // 2]
            sends[1][chunk] = center[:, span // 2 :]
    if second_out.shape[0] == 2:
        first_out[...] = total_sum
        second_out[...] = channel_sums(total_sum)
    else:
        middle = (source[...].astype(jnp.float32) + total_sum) * root_half
        first_out[...] = middle
        second_out[...] = middle.astype(jnp.bfloat16)


def back_body(groups, rows, width, spot, grad, near, far_row, *refs):
    frame, held = refs[-2:]
    outs = refs[-2 - groups : -2]
    weights = Weights(refs[: -2 - groups], spot, groups)
    framed = framed_rows(near[...], far_row[...], grad[...], weights.odd)
    for column, values in enumerate(turned(framed, width)):
        frame[column] = values
    for chunk in range(groups):
        total_sum = jnp.zeros(held.shape[1:], jnp.float32)
        for position in range(9):
            start = (2 - position // 3) * width
            total_sum += lax.dot_general(
                frame[2 - position % 3, start : start + rows * width, :],
                weights.tap(chunk, position),
                (((1,), (1,)), ((), ())),
                preferred_element_type=jnp.float32,
            )
        held[weights.block(chunk)] = weights.ordered(total_sum).astype(jnp.bfloat16)
    for mask in range(groups):
        outs[mask][...] = held[lax.bitwise_xor(spot[1], mask)]


def bf16_like(*shape):
    return jax.ShapeDtypeStruct(shape, jnp.bfloat16)


def far_like(shape):
    return pltpu.HBM(shape.shape, shape.dtype)


def f32_like(*shape):
    return jax.ShapeDtypeStruct(shape, jnp.float32)


def flipped(values, axis, mask):
    count = lax.axis_size(axis)
    return lax.ppermute(values, axis, [(i, i ^ mask) for i in range(count)])


def relayed_block(over_x, over_y):
    odd = lax.rem(lax.axis_index("wide"), 2) == 1
    far_pairs = [(i, i ^ (2 if i % 2 else 4)) for i in range(8)]
    return lax.ppermute(jnp.where(odd, over_y, over_x), "wide", far_pairs)


def over_chips(values):
    over_x, over_y = flipped(values, "wide", 2), flipped(values, "wide", 4)
    return [values, over_x, over_y, relayed_block(over_x, over_y)]


def has_slots():
    return lax.axis_size("wide") == 8


def after(value, *others):
    return lax.optimization_barrier((value, others))[0]


def gathered_blocks(blocks):
    return [lax.all_gather(blocks, "wide")]


def spread_chips(values):
    if has_slots():
        return over_chips(values)
    mask = 2
    while mask < lax.axis_size("wide"):
        values = jnp.concatenate([values, flipped(values, "wide", mask)])
        mask *= 2
    return [values]


def gathered_sums(parts):
    if has_slots():
        return [parts[0]] + [flipped(parts[k], "wide", 2 * k) for k in range(1, 4)]
    values = parts[0]
    mask = lax.axis_size("wide") // 2
    while mask > 1:
        half = values.shape[0] // 2
        values = values[:half] + flipped(values[half:], "wide", mask)
        mask //= 2
    return [values]


def channel_pieces(values):
    count = lax.axis_size("tensor")
    return [values] + [flipped(values, "tensor", mask) for mask in range(1, count)]


def edge_rows(near, far_row):
    count = lax.axis_size("wide")
    beyond = [(i, i + 1) for i in range(1, count - 1, 2)]
    beyond += [(i + 1, i) for i in range(1, count - 1, 2)]
    from_far = lax.ppermute(far_row, "wide", beyond)
    return flipped(after(near, far_row), "wide", 1), from_far


def framed_rows(near, far_row, own, odd):
    top = jnp.where(odd, near, far_row)
    bottom = jnp.where(odd, far_row, near)
    return jnp.concatenate([top, own, bottom], axis=0)


def convolve(spot, pieces, edges, kernel, source, second_shape, earlier, rows, width):
    groups, (area, span) = len(pieces), pieces[0].shape
    count, block = (2, span // 2) if has_slots() else (1, span)
    layers = (2,) if earlier else ()
    sends = [bf16_like(groups, *layers, area, block)] * count
    return local_kernel(
        functools.partial(conv_body, groups, len(kernel), len(earlier), rows, width),
        [f32_like(area, span), second_shape] + sends,
        [spot, *pieces, *edges, *far(kernel), source, *far(earlier)],
        [pltpu.VMEM((groups, 3, (rows + 2) * width, span), jnp.bfloat16)],
        32,
        2 * 9 * area * C * span,
    )


def piece_edges(pieces, width):
    odd = lax.rem(lax.axis_index("wide"), 2) == 1
    last = jnp.concatenate([piece[-width:] for piece in pieces], axis=1)
    first = jnp.concatenate([piece[:width] for piece in pieces], axis=1)
    return edge_rows(jnp.where(odd, first, last), jnp.where(odd, last, first))


def convolve_back(spot, grad, edges, kernel, rows, width):
    groups, (area, span) = lax.axis_size("tensor"), grad.shape
    return local_kernel(
        functools.partial(back_body, groups, rows, width),
        [bf16_like(area, span)] * groups,
        [spot, grad, *edges, *far(kernel)],
        [
            pltpu.VMEM((3, (rows + 2) * width, span), jnp.bfloat16),
            pltpu.VMEM((groups, area, span), jnp.bfloat16),
        ],
        32,
        2 * 9 * area * C * span,
    )


def sent_parts(parts):
    return [parts[0]] + [flipped(parts[mask], "tensor", mask) for mask in range(1, len(parts))]


def kernel_grad_body(width, spot, kept, got, *refs):
    *pairs, grads, out, turned_all = refs
    layer = pl.program_id(0)
    area, span = kept.shape[2:]
    depth = 8 * area
    turned_all[:, :width] = jnp.zeros((3 * span, width), jnp.bfloat16)
    turned_all[:, depth + width :] = jnp.zeros((3 * span, width), jnp.bfloat16)
    pieces = [kept[0, layer], got[0, layer]]
    pieces += [pair[core, layer] for pair in pairs for core in range(2)]
    lane = lax.broadcasted_iota(jnp.int32, (span, width), 1)
    for mask, piece in enumerate(pieces):
        start = pl.multiple_of(lax.bitwise_xor(spot[0], mask) * area, area)
        flat = jnp.transpose(piece.astype(jnp.float32))
        for row in range(area // width):
            center = flat[:, row * width : (row + 1) * width]
            before = jnp.where(lane == 0, 0.0, pltpu.roll(center, 1, 1))
            behind = jnp.where(lane == width - 1, 0.0, pltpu.roll(center, width - 1, 1))
            lanes = pl.ds(start + (row + 1) * width, width)
            for column, values in enumerate((before, center, behind)):
                turned_all[column * span : (column + 1) * span, lanes] = values.astype(jnp.bfloat16)
    for row in range(3):
        product = dot(turned_all[:, row * width : row * width + depth], grads[0])
        for column in range(3):
            out[0, 3 * row + column] = product[column * span : (column + 1) * span, :]


def kernel_grad(spot, pieces, grads, width):
    span = pieces[0].shape[3]
    depth, columns = grads.shape[1:]
    return pl.pallas_call(
        functools.partial(kernel_grad_body, width),
        out_shape=f32_like(2, 9, span, columns),
        grid=(2,),
        in_specs=[in_smem]
        + [in_vmem] * len(pieces)
        + [pl.BlockSpec((1, depth, columns), lambda i: (i, 0, 0))],
        out_specs=pl.BlockSpec((1, 9, span, columns), lambda i: (i, 0, 0, 0)),
        scratch_shapes=[pltpu.VMEM((3 * span, depth + 2 * width), jnp.bfloat16)],
        compiler_params=pltpu.CompilerParams(vmem_limit_bytes=24 * MIB),
        cost_estimate=pl.CostEstimate(
            flops=4 * 9 * depth * span * columns, bytes_accessed=6 * MIB, transcendentals=0
        ),
        name="kernel_grad_body",
    )(spot, *far(pieces), *far([grads]))


def kernel_grad_whole(send, grads, rows, width):
    natural = jnp.moveaxis(send, 0, 1).reshape(1, rows, width, C)
    swapped = lax.all_to_all(natural, "wide", split_axis=3, concat_axis=1, tiled=True)
    framed = jnp.pad(swapped, ((0, 0), (1, 1), (1, 1), (0, 0)))
    low = grads.reshape(1, -1, width, grads.shape[1])
    return jnp.stack(
        [
            jnp.einsum(
                "mrwc,mrwd->cd",
                framed[:, tap // 3 : tap // 3 + low.shape[1], tap % 3 : tap % 3 + width, :],
                low,
                preferred_element_type=jnp.float32,
            )
            for tap in range(9)
        ]
    )


root_half = 1.0 / math.sqrt(2.0)
highest = lax.Precision.HIGHEST


def sinusoid(steps):
    half_width = TEMB // 2
    frequency = jnp.exp(-math.log(10000.0) * jnp.arange(half_width, dtype=jnp.float32) / half_width)
    angles = steps.astype(jnp.float32)[:, None] * frequency[None, :]
    return jnp.concatenate([jnp.cos(angles), jnp.sin(angles)], axis=1)


def chip_parts(values):
    if has_slots():
        return [values] + [flipped(values, "wide", mask) for mask in (2, 4, 6)]
    mask = 2
    while mask < lax.axis_size("wide"):
        values = values + flipped(values, "wide", mask)
        mask *= 2
    return [values]


def part_totals(rows):
    return chip_parts(rows + flipped(rows, "wide", 1))


def sum_of_parts(refs):
    if len(refs) == 1:
        return refs[0][...]
    return (refs[0][...] + refs[1][...]) + (refs[2][...] + refs[3][...])


def total(values, axis, mask=1):
    while mask < lax.axis_size(axis):
        values = values + flipped(values, axis, mask)
        mask *= 2
    return values


def silu_slope(values):
    logistic = lax.logistic(values)
    return logistic * (1.0 + values * (1.0 - logistic))


def channel_sums(values):
    return jnp.concatenate(
        [
            jnp.sum(values, axis=0, keepdims=True),
            jnp.sum(values * values, axis=0, keepdims=True),
        ],
        axis=0,
    )


def group_means(first, second, pixel_count):
    channels = first.shape[1]
    per_group = C // GROUPS
    row = lax.div(lax.broadcasted_iota(jnp.int32, (channels, channels), 0), per_group)
    column = lax.div(lax.broadcasted_iota(jnp.int32, (channels, channels), 1), per_group)
    same = jnp.where(row == column, 1.0, 0.0)
    rows = jnp.concatenate([first, second, jnp.zeros((6, channels), jnp.float32)], axis=0)
    means = jnp.dot(rows, same, precision=highest, preferred_element_type=jnp.float32)
    means = means / (pixel_count * per_group)
    return means[0:1], means[1:2]


def group_scale(first, second, pixel_count):
    center, square = group_means(first, second, pixel_count)
    return center, lax.rsqrt(square - center * center + 1e-05)


def lifted_sums(sums, film, pixel_count):
    slope, shift = 1.0 + film[0:1], film[1:2]
    plain, square = sums[0:1], sums[1:2]
    return (
        slope * plain + pixel_count * shift,
        slope * slope * square + 2.0 * slope * shift * plain + pixel_count * shift * shift,
    )


def silu_low(values):
    return (values * lax.logistic(values)).astype(jnp.bfloat16)


def first_norm_body(pixel_count, spot, pixels, affine, *refs):
    *parts, out, sums = refs
    sums[...] = sum_of_parts(parts)
    center, inverse = group_scale(sums[0:1], sums[1:2], pixel_count)
    scaled = (pixels[...].astype(jnp.float32) - center) * inverse
    out[...] = silu_low(scaled * affine[0:1] + affine[1:2])


def second_norm_body(pixel_count, spot, inner, affine, *refs):
    *parts, out, film, sums = refs
    summed = sum_of_parts(parts)
    film[...], sums[...] = summed[:2], summed[2:]
    center, inverse = group_scale(*lifted_sums(sums[...], film[...], pixel_count), pixel_count)
    lifted = inner[...] * (1.0 + film[0:1]) + film[1:2]
    out[...] = silu_low((lifted - center) * inverse * affine[0:1] + affine[1:2])


def parts_sum(refs):
    summed = refs[0][...].astype(jnp.float32)
    for ref in refs[1:]:
        summed += ref[...].astype(jnp.float32)
    return summed


def stacked_rows(rows):
    return jnp.concatenate([jnp.sum(row, axis=0, keepdims=True) for row in rows], axis=0)


def second_back_body(groups, pixel_count, spot, *refs):
    inner, sums, film, affine, terms, out, rows = refs[groups:]
    center, inverse = group_scale(*lifted_sums(sums[...], film[...], pixel_count), pixel_count)
    own = inner[...]
    scaled = (own * (1.0 + film[0:1]) + film[1:2] - center) * inverse
    back = parts_sum(refs[:groups]) * silu_slope(scaled * affine[0:1] + affine[1:2])
    out[...] = back
    rows[0:3, :] = stacked_rows([back * scaled, back, back * own])
    rows[3:5, :] = terms[...]
    rows[5:8, :] = jnp.zeros((3, own.shape[1]), jnp.float32)


def second_input_body(pixel_count, width, spot, back, inner, sums, film, affine, *refs):
    *parts, low, near, far_row, film_rows, rows = refs
    rows[...] = sum_of_parts(parts)
    slope, shift, gain = 1.0 + film[0:1], film[1:2], affine[0:1]
    plain_sum, square_sum = sums[0:1], sums[1:2]
    lifted_sum, lifted_square = lifted_sums(sums[...], film[...], pixel_count)
    center, inverse = group_scale(lifted_sum, lifted_square, pixel_count)
    dotted, plain = group_means(gain * rows[0:1], gain * rows[1:2], pixel_count)
    scaled = (inner[...] * slope + shift - center) * inverse
    grad = inverse * (back[...] * gain - plain - scaled * dotted)
    grad_low = (grad * slope).astype(jnp.bfloat16)
    low[...] = grad_low
    odd = lax.rem(spot[0], 2) == 1
    near[...] = jnp.where(odd, grad_low[:width], grad_low[-width:])
    far_row[...] = jnp.where(odd, grad_low[-width:], grad_low[:width])
    scaled_sum = inverse * (lifted_sum - pixel_count * center)
    scaled_inner = inverse * (slope * square_sum + (shift - center) * plain_sum)
    film_rows[0:1, :] = inverse * (
        gain * rows[2:3] - plain * plain_sum - dotted * scaled_inner
    )
    film_rows[1:2, :] = inverse * (
        gain * rows[1:2] - pixel_count * plain - dotted * scaled_sum
    )


def first_back_body(groups, pixel_count, spot, *refs):
    pixels, sums, affine, out, rows = refs[groups:]
    center, inverse = group_scale(sums[0:1], sums[1:2], pixel_count)
    scaled = (pixels[...].astype(jnp.float32) - center) * inverse
    back = parts_sum(refs[:groups]) * silu_slope(scaled * affine[0:1] + affine[1:2])
    out[...] = back
    rows[...] = stacked_rows([back * scaled, back])


def first_input_body(pixel_count, spot, back, pixels, sums, affine, middle, second, *refs):
    *parts, out, gains, biases = refs
    rows = sum_of_parts(parts)
    gains[...] = jnp.concatenate([rows[0:1], second[0:1]], axis=0)
    biases[...] = jnp.concatenate([rows[1:2], second[1:2]], axis=0)
    gain = affine[0:1]
    center, inverse = group_scale(sums[0:1], sums[1:2], pixel_count)
    dotted, plain = group_means(gain * rows[0:1], gain * rows[1:2], pixel_count)
    scaled = (pixels[...].astype(jnp.float32) - center) * inverse
    out[...] = inverse * (back[...] * gain - plain - scaled * dotted) + middle[...] * root_half


def dot(left, right):
    return jnp.dot(left, right, preferred_element_type=jnp.float32)


def dot_last(left, right):
    return lax.dot_general(
        left, right, (((1,), (1,)), ((), ())), preferred_element_type=jnp.float32
    )


def flat_turn(values):
    return jnp.transpose(values.astype(jnp.float32)).astype(jnp.bfloat16)


def dot_first(left, right):
    return dot(flat_turn(left), right)


def head_choice(values, odd):
    first, second = values[:, :HEAD_DIM], values[:, HEAD_DIM:]
    return jnp.where(odd, second, first), jnp.where(odd, first, second)


def heads_joined(kept, received, odd):
    return jnp.where(
        odd,
        jnp.concatenate([received, kept], axis=1),
        jnp.concatenate([kept, received], axis=1),
    )


def packed_rows(values):
    rows = []
    for _ in range(3):
        rows.append(values.astype(jnp.bfloat16).astype(jnp.float32))
        values = values - rows[-1]
    rows.append(jnp.zeros((10, values.shape[1]), jnp.float32))
    return jnp.concatenate(rows, axis=0).astype(jnp.bfloat16)


def unpacked_rows(packed, area):
    rows = packed[area:, :].astype(jnp.float32)
    return rows[0:1] + rows[2:3] + rows[4:5], rows[1:2] + rows[3:4] + rows[5:6]


def prepare_body(spot, pixels, cotangent, gain, bias, pack, sums):
    area = cotangent.shape[0]
    pack[:area] = cotangent[...].astype(jnp.bfloat16)
    pack[area:] = packed_rows(jnp.concatenate([gain[...], bias[...]], axis=0))
    sums[...] = channel_sums(pixels[...].astype(jnp.float32))


def project_body(groups, spot, *refs):
    pieces, packs = refs[:groups], refs[groups : 2 * groups]
    own, maps, keep_query, keep, send, cross, normed, scaled, center, inverse = refs[2 * groups :]
    weights = Weights([maps], spot, groups)
    odd = lax.rem(spot[0], 2) == 1
    area = own.shape[0]
    token_sum = token_square = 0.0
    for piece in pieces:
        values = piece[...].astype(jnp.float32)
        token_sum += jnp.sum(values, axis=1, keepdims=True)
        token_square += jnp.sum(values * values, axis=1, keepdims=True)
    mean = token_sum / C
    scale = lax.rsqrt(token_square / C - mean * mean + 1e-05)
    lows = []
    for mask in range(groups):
        gain, bias = unpacked_rows(packs[mask], area)
        values = (pieces[mask][...].astype(jnp.float32) - mean) * scale
        lows.append((values * gain + bias).astype(jnp.bfloat16))
        normed[lax.bitwise_xor(spot[1], mask)] = lows[-1]
    center[...] = mean
    inverse[...] = scale
    scaled[...] = (own[...] - mean) * scale
    projected = []
    for position in range(4):
        total_sum = 0.0
        for mask in range(groups):
            total_sum += dot(lows[mask], weights.tap(mask, position))
        projected.append(total_sum.astype(jnp.bfloat16))
    cross[...] = projected[3]
    chosen = [head_choice(values, odd) for values in projected[:3]]
    chosen = chosen[1:] + chosen[:1]
    keep_query[...] = chosen[2][0]
    keep[...] = jnp.concatenate([pair[0] for pair in chosen[:2]], axis=1)
    send[...] = jnp.concatenate([pair[1] for pair in chosen], axis=1)


def out_grad_body(groups, spot, *refs):
    packs = refs[:groups]
    maps, keep, send, cross = refs[groups:]
    weights = Weights([maps], spot, groups)
    sums = []
    for position in (4, 5):
        total_sum = 0.0
        for mask in range(groups):
            total_sum += dot(packs[mask][: cross.shape[0]], weights.tap(mask, position))
        sums.append(total_sum.astype(jnp.bfloat16))
    kept, sent = head_choice(sums[0], lax.rem(spot[0], 2) == 1)
    keep[...] = kept
    send[...] = sent
    cross[...] = sums[1]


def text_out_body(spot, film, features, pooled, text, parts, time_grad, text_grad, kv_grad):
    for rows, out in ((features, time_grad), (pooled, text_grad)):
        column = jnp.transpose(jnp.broadcast_to(rows[...].astype(jnp.float32), (8, rows.shape[1])))
        for part in range(2):
            out[:, part, :] = column[:, 0:1] * film[part : part + 1, :]
    summed = leading_sum(parts)
    turned_text = flat_turn(text[...])
    for part in range(2):
        high = summed[part].astype(jnp.bfloat16)
        low = (summed[part] - high.astype(jnp.float32)).astype(jnp.bfloat16)
        kv_grad[part] = dot(turned_text, high) + dot(turned_text, low)


def mix_body(groups, spot, kept, other, crossed, maps, *outs):
    weights = Weights([maps], spot, groups)
    attended = heads_joined(kept[...], other[...], lax.rem(spot[0], 2) == 1)
    for mask in range(groups):
        total_sum = dot_last(attended, weights.tap(mask, 4))
        total_sum += dot_last(crossed[...], weights.tap(mask, 5))
        outs[mask][...] = total_sum.astype(jnp.bfloat16)


def over_rows(refs, step, state):
    for index, ref in enumerate(refs):
        rows = ref.shape[0]
        if rows <= 512:
            state = step(state, ref[...], index, 0)
        else:
            state = lax.fori_loop(
                0,
                rows // 512,
                lambda i, held: step(
                    held, ref[pl.ds(pl.multiple_of(i * 512, 512), 512), :], index, i * 512
                ),
                state,
            )
    return state


score_scale = HEAD_DIM ** (-0.5)


def cross_body(spot, query, grad, parts, *refs):
    *blocks, crossed, grad_query, text_grad = refs
    if blocks:
        kept_block, got_block, *pairs = blocks
        for index, pair in enumerate(pairs):
            pair[0] = kept_block[index + 1]
            pair[1] = got_block[index + 1]
    text = leading_sum(parts).astype(jnp.bfloat16)
    live = lax.broadcasted_iota(jnp.int32, (query.shape[0], text.shape[1]), 1) < spot[2]
    for head in range(query.shape[1] // HEAD_DIM):
        lanes = slice(head * HEAD_DIM, (head + 1) * HEAD_DIM)
        own, keys, values, back = query[:, lanes], text[0, :, lanes], text[1, :, lanes], grad[:, lanes]
        scores = jnp.where(live, dot_last(own, keys) * score_scale, -1e30)
        weights = jnp.exp(scores - jnp.max(scores, axis=1, keepdims=True))
        probs = weights / jnp.sum(weights, axis=1, keepdims=True)
        low = probs.astype(jnp.bfloat16)
        crossed[:, lanes] = dot(low, values).astype(jnp.bfloat16)
        grad_probs = dot_last(back, values)
        grad_scores = probs * (grad_probs - jnp.sum(probs * grad_probs, axis=1, keepdims=True))
        grad_low = grad_scores.astype(jnp.bfloat16)
        grad_query[:, lanes] = (dot(grad_low, keys) * score_scale).astype(jnp.bfloat16)
        text_grad[0, :, lanes] = (dot_first(grad_low, own) * score_scale).astype(jnp.bfloat16)
        text_grad[1, :, lanes] = dot_first(low, back).astype(jnp.bfloat16)


def attend_body(count, extra, spot, kept_query, got, kept_grad, got_grad, *refs):
    blocks, refs = refs[:count], refs[count:]
    cross_in, refs = refs[: 3 + extra], refs[3 + extra :]
    parts, refs = refs[:count], refs[count:]
    keep_out, send_out, keep_query, send_query, *cross_out = refs
    cross_body(spot, *cross_in, *cross_out)
    query = jnp.concatenate([kept_query[...], got[:, 2 * HEAD_DIM :]], axis=0)
    grad = jnp.concatenate([kept_grad[...], got_grad[...]], axis=0)
    queries = query.shape[0]

    def forward(state, block, index, start):
        top, weight_sum, weighted = state
        scores = dot_last(block[:, :HEAD_DIM], query) * score_scale
        raised = jnp.maximum(top, jnp.max(scores, axis=0, keepdims=True))
        rescale = jnp.exp(top - raised)
        weights = jnp.exp(scores - raised)
        weight_sum = weight_sum * rescale + jnp.sum(weights, axis=0, keepdims=True)
        values = block[:, HEAD_DIM:]
        weighted = weighted * rescale + dot_first(values, weights.astype(jnp.bfloat16))
        return raised, weight_sum, weighted

    top, weight_sum, weighted = over_rows(
        blocks,
        forward,
        (
            jnp.full((1, queries), -1e30, jnp.float32),
            jnp.zeros((1, queries), jnp.float32),
            jnp.zeros((HEAD_DIM, queries), jnp.float32),
        ),
    )
    attended = weighted / weight_sum
    delta = jnp.sum(attended * jnp.transpose(grad.astype(jnp.float32)), axis=0, keepdims=True)
    log_sum = top + jnp.log(weight_sum)

    def backward(state, block, index, start):
        keys, values = block[:, :HEAD_DIM], block[:, HEAD_DIM:]
        probs = jnp.exp(dot_last(keys, query) * score_scale - log_sum)
        grad_values = dot(probs.astype(jnp.bfloat16), grad)
        grad_scores = (probs * (dot_last(values, grad) - delta)).astype(jnp.bfloat16)
        grad_keys = dot(grad_scores, query) * score_scale
        rows = pl.ds(start if isinstance(start, int) else pl.multiple_of(start, 512), block.shape[0])
        parts[index][rows, :] = jnp.concatenate([grad_keys, grad_values], axis=1).astype(
            jnp.bfloat16
        )
        return state + dot_first(keys, grad_scores)

    flat = over_rows(blocks, backward, jnp.zeros((HEAD_DIM, queries), jnp.float32))
    for values, keep, send in (
        (attended, keep_out, send_out),
        (flat * score_scale, keep_query, send_query),
    ):
        turned_back = jnp.transpose(values).astype(jnp.bfloat16)
        keep[...] = turned_back[: queries // 2]
        send[...] = turned_back[queries // 2 :]


def key_sum_body(spot, sent_query, *refs):
    *parts, keep, send = refs
    both = parts_sum(parts).astype(jnp.bfloat16)
    half = keep.shape[0]
    keep[...] = both[:half]
    send[:, : 2 * HEAD_DIM] = both[half:]
    send[:, 2 * HEAD_DIM :] = sent_query[...]


def leading_sum(ref):
    summed = ref[0].astype(jnp.float32)
    for index in range(1, ref.shape[0]):
        summed += ref[index].astype(jnp.float32)
    return summed


def joined_grads(spot, kept_query, kept_pair, got, cross):
    odd = lax.rem(spot[0], 2) == 1
    parts = [got[:, i * HEAD_DIM : (i + 1) * HEAD_DIM] for i in range(3)]
    return [
        heads_joined(kept_query[...], parts[2], odd),
        heads_joined(kept_pair[:, :HEAD_DIM], parts[0], odd),
        heads_joined(kept_pair[:, HEAD_DIM:], parts[1], odd),
        cross[...],
    ]


def project_back_body(groups, spot, kq, kp, got, cross, center, inverse, kept, other, *refs):
    crossed, normed, maps, *refs = refs
    pieces, packs = refs[:groups], refs[groups : 2 * groups]
    *outs, out, frame = refs[2 * groups :]
    odd = lax.rem(spot[0], 2) == 1
    weights = Weights([maps], spot, groups)
    grads = joined_grads(spot, kq, kp, got, cross)
    area, span = cross.shape
    plain = dotted = 0.0
    for mask in range(groups):
        part = 0.0
        for position in range(4):
            part += dot_last(grads[position], weights.tap(mask, position))
        outs[mask][:area] = part.astype(jnp.bfloat16)
        eased = part * unpacked_rows(packs[mask], area)[0]
        unit = (pieces[mask][...].astype(jnp.float32) - center[...]) * inverse[...]
        plain += eased
        dotted += eased * unit
    ones = jnp.ones((8, plain.shape[1]), jnp.float32)
    sums = [
        lax.dot_general(
            ones,
            values,
            (((1,), (1,)), ((), ())),
            precision=highest,
            preferred_element_type=jnp.float32,
        )[0:1]
        for values in (plain, dotted)
    ]
    packed = packed_rows(jnp.concatenate(sums, axis=0))
    for part in outs:
        part[area:] = packed
    right = jnp.concatenate(grads, axis=1)
    out_right = jnp.concatenate([heads_joined(kept[...], other[...], odd), crossed[...]], axis=1)
    for mask in range(groups):
        frame[lax.bitwise_xor(spot[1], mask)] = packs[mask][:area]
    for chunk in range(groups):
        rows = slice(chunk * span, (chunk + 1) * span)
        out[rows, : 4 * span] = dot_first(normed[chunk], right).astype(jnp.bfloat16)
        out[rows, 4 * span :] = dot_first(frame[chunk], out_right).astype(jnp.bfloat16)


def weight_out_body(spot, sums, in_grad, self_grad, cross_grad):
    summed = sums[...].astype(jnp.float32)
    span = in_grad.shape[2]
    for position in range(4):
        in_grad[position] = summed[:, position * span : (position + 1) * span]
    self_grad[...] = jnp.transpose(summed[:, 4 * span : 5 * span])
    cross_grad[...] = jnp.transpose(summed[:, 5 * span :])


def norm_back_body(groups, width, spot, *refs):
    scaled, inverse, cotangent, gain, middle, low, near, far_row, terms = refs[groups:]
    area = scaled.shape[0]
    grad = plain = dotted = 0.0
    for ref in refs[:groups]:
        grad += ref[:area].astype(jnp.float32)
        sums = unpacked_rows(ref, area)
        plain, dotted = plain + sums[0], dotted + sums[1]
    same = lax.broadcasted_iota(jnp.int32, (area, area), 0) == lax.broadcasted_iota(
        jnp.int32, (area, area), 1
    )
    plain = jnp.sum(jnp.where(same, plain, 0.0), axis=1, keepdims=True) / C
    dotted = jnp.sum(jnp.where(same, dotted, 0.0), axis=1, keepdims=True) / C
    unit = scaled[...]
    terms[0:1, :] = jnp.sum(grad * unit, axis=0, keepdims=True)
    terms[1:2, :] = jnp.sum(grad, axis=0, keepdims=True)
    back = inverse[...] * (grad * gain[...] - plain - unit * dotted) + cotangent[...]
    middle[...] = back
    grad_low = (back * root_half).astype(jnp.bfloat16)
    low[...] = grad_low
    odd = lax.rem(spot[0], 2) == 1
    near[...] = jnp.where(odd, grad_low[:width], grad_low[-width:])
    far_row[...] = jnp.where(odd, grad_low[-width:], grad_low[:width])


def shards(
    pixels,
    text_states,
    text_length,
    timestep,
    conv_weights,
    film_time,
    film_text,
    group_gain,
    group_bias,
    layer_gain,
    layer_bias,
    attn_in,
    text_kv,
    out_self,
    out_cross,
    cotangent,
):
    map_count, row_count, col_count, width_own = pixels.shape
    token_count = row_count * col_count
    groups = lax.axis_size("tensor")
    pixel_count = token_count * lax.axis_size("wide")
    own_shape = (map_count, row_count, col_count, width_own)
    flat = (token_count, width_own)
    half = (token_count, HEAD_DIM)
    square = 2 * token_count * C * width_own
    edge = (col_count, width_own)
    spot = jnp.stack([lax.axis_index("wide"), lax.axis_index("tensor"), text_length[0]])
    spot = spot.astype(jnp.int32)
    own_pixels = pixels.reshape(flat)
    flat_cotangent = cotangent.reshape(flat)
    affine = [jnp.stack([group_gain[layer], group_bias[layer]]) for layer in range(2)]

    pack, sums = local_kernel(
        prepare_body,
        [bf16_like(token_count + 16, width_own), f32_like(2, width_own)],
        [spot, *far([own_pixels, flat_cotangent, layer_gain[None], layer_bias[None]])],
        [],
        8,
        0,
    )
    first_parts = part_totals(sums)
    kernel_one = gathered_blocks(conv_weights[0])
    maps = jnp.concatenate(
        [attn_in, jnp.transpose(jnp.stack([out_self, out_cross]), (0, 2, 1))], axis=0
    )
    maps = gathered_blocks(maps)[0]

    features = sinusoid(timestep).astype(jnp.bfloat16)
    present = jnp.arange(TEXT)[None, :] < text_length[:, None]
    pooled = jnp.einsum(
        "mtx,mt->mx", text_states, present.astype(jnp.bfloat16), preferred_element_type=jnp.float32
    )
    pooled = (pooled / text_length.astype(jnp.float32)[:, None]).astype(jnp.bfloat16)
    wide_index = lax.axis_index("wide")
    time_rows = film_time.shape[0]
    text_rows = film_text.shape[0]
    own_features = lax.dynamic_slice_in_dim(features, wide_index * time_rows, time_rows, 1)
    own_pooled = lax.dynamic_slice_in_dim(pooled, wide_index * text_rows, text_rows, 1)
    own_text = lax.dynamic_slice_in_dim(text_states, wide_index * text_rows, text_rows, 2)
    film_term = jnp.einsum(
        "mk,ksc->msc", own_features, film_time, preferred_element_type=jnp.float32
    ) + jnp.einsum("mk,ksc->msc", own_pooled, film_text, preferred_element_type=jnp.float32)
    text_term = jnp.einsum("mtx,pxd->pmtd", own_text, text_kv, preferred_element_type=jnp.float32)
    text_term = text_term.astype(jnp.bfloat16).reshape(2, TEXT, width_own)

    row_pair = f32_like(2, width_own)
    first, first_sums = local_kernel(
        functools.partial(first_norm_body, pixel_count),
        [bf16_like(*flat), row_pair],
        [spot, own_pixels, affine[0], *first_parts],
        [],
        8,
        0,
    )
    pieces = channel_pieces(first)
    edges = piece_edges(pieces, col_count)
    later = after(conv_weights, first)[1]
    if has_slots():
        kernel_two = over_chips(later)
        kernel_two += [flipped(part, "wide", 1) for part in kernel_two]
    else:
        kernel_two = gathered_blocks(later)
    packs = channel_pieces(after(pack, pieces))
    pieces[0] = after(pieces[0], film_term, packs, text_term)
    inner, sums, *first_sends = convolve(
        spot, pieces, edges, kernel_one, own_pixels, row_pair, [], row_count, col_count
    )
    sums = after(sums, kernel_two)
    inner_parts = part_totals(jnp.concatenate([film_term[0], sums]))
    second, film, inner_sums = local_kernel(
        functools.partial(second_norm_body, pixel_count),
        [bf16_like(*flat), row_pair, row_pair],
        [spot, inner, affine[1], *inner_parts],
        [],
        8,
        0,
    )
    text_all = lax.all_gather(after(text_term, second), "wide")
    pieces = channel_pieces(second)
    edges = piece_edges(pieces, col_count)
    middle, middle_low, *both_sends = convolve(
        spot,
        pieces,
        edges,
        kernel_two,
        own_pixels,
        bf16_like(*flat),
        first_sends,
        row_count,
        col_count,
    )

    middle_pieces = channel_pieces(middle_low)
    block_pair = [both_sends[0], flipped(both_sends[1], "wide", 1)] if has_slots() else []
    kept_grad, sent_grad, grad_crossed = local_kernel(
        functools.partial(out_grad_body, groups),
        [bf16_like(*half), bf16_like(*half), bf16_like(*flat)],
        [spot, *far([after(packs[0], middle_low)] + packs[1:]), *far([maps])],
        [],
        16,
        2 * square,
    )
    got_grad = flipped(sent_grad, "wide", 1)
    middle_pieces[0] = after(middle_pieces[0], got_grad, block_pair)
    column = f32_like(token_count, 1)
    triple = bf16_like(token_count, 3 * HEAD_DIM)
    kept_query, kept_pair, sent, cross_query, normed, scaled, center, inverse = local_kernel(
        functools.partial(project_body, groups),
        [
            bf16_like(*half),
            bf16_like(*flat),
            triple,
            bf16_like(*flat),
            far_like(bf16_like(groups, *flat)),
            far_like(f32_like(*flat)),
            far_like(column),
            far_like(column),
        ],
        [spot, *middle_pieces, *far(packs), middle, *far([maps])],
        [],
        24,
        4 * square,
    )
    got = flipped(sent, "wide", 1)
    blocks = spread_chips(jnp.concatenate([kept_pair, got[:, : 2 * HEAD_DIM]]))
    pair_shapes = [bf16_like(2, *block.shape[1:]) for block in block_pair[:1] * 3]
    attend_shapes = [bf16_like(*block.shape) for block in blocks] + [bf16_like(*half)] * 4
    cross_shapes = [bf16_like(*flat), bf16_like(*flat), bf16_like(2, TEXT, width_own)]
    outs = local_kernel(
        functools.partial(attend_body, len(blocks), len(block_pair)),
        [far_like(shape) for shape in attend_shapes + pair_shapes + cross_shapes],
        [
            spot,
            kept_query,
            got,
            *far([kept_grad, got_grad]),
            *blocks,
            cross_query,
            *far([grad_crossed, text_all]),
            *far(block_pair),
        ],
        [],
        48,
        14 * (2 * token_count) * HEAD_DIM * pixel_count,
    )
    key_parts, outs = outs[: len(blocks)], outs[len(blocks) :]
    kept_out, sent_out, kept_dq, sent_dq, *block_pairs = outs
    *block_pairs, crossed, grad_cross_query, text_grads = block_pairs
    text_sums = lax.all_gather(text_grads, "wide")
    key_sums = gathered_sums(key_parts)
    kept_dk, sent_all = local_kernel(
        key_sum_body,
        [bf16_like(*flat), bf16_like(token_count, 3 * HEAD_DIM)],
        [spot, *far([sent_dq, key_sums[0]]), *key_sums[1:]],
        [],
        16,
        0,
    )
    got_all = flipped(sent_all, "wide", 1)
    got_out = flipped(sent_out, "wide", 1)
    kept_dq, grad_cross_query = far([kept_dq, grad_cross_query])
    projected_grads = [kept_dq, kept_dk, got_all, grad_cross_query]
    *norm_parts, weight_parts = local_kernel(
        functools.partial(project_back_body, groups),
        [bf16_like(token_count + 16, width_own)] * groups + [far_like(bf16_like(C, 6 * width_own))],
        [
            spot,
            *projected_grads,
            *far([center, inverse, kept_out, got_out, crossed, normed, maps]),
            *far(middle_pieces),
            *far(packs),
        ],
        [pltpu.VMEM((groups, *flat), jnp.bfloat16)],
        32,
        10 * square,
    )
    weight_sums = lax.psum_scatter(weight_parts, "wide", scatter_dimension=0, tiled=True)
    received = sent_parts(norm_parts)
    if has_slots():
        close = [flipped(after(block_pairs[k], norm_parts[0]), "wide", 2 * k + 2) for k in range(2)]
        received[0] = after(received[0], close)
    grad_middle, grad_two, last, head, terms = local_kernel(
        functools.partial(norm_back_body, groups, col_count),
        [
            f32_like(*flat),
            bf16_like(*flat),
            bf16_like(*edge),
            bf16_like(*edge),
            f32_like(2, width_own),
        ],
        [
            spot,
            *received,
            scaled,
            inverse,
            flat_cotangent,
            layer_gain[None],
        ],
        [],
        16,
        0,
    )

    edges = edge_rows(last, head)
    mixed = local_kernel(
        functools.partial(mix_body, groups),
        [bf16_like(*flat)] * groups,
        [spot, after(kept_out, grad_two), got_out, *far([crossed, maps])],
        [],
        16,
        2 * square,
    )
    back_parts = convolve_back(
        spot, after(grad_two, mixed), edges, kernel_two, row_count, col_count
    )
    back_parts = sent_parts(back_parts)
    back, rows = local_kernel(
        functools.partial(second_back_body, groups, pixel_count),
        [f32_like(*flat), f32_like(8, width_own)],
        [spot, *back_parts, inner, inner_sums, film, affine[1], terms],
        [],
        16,
        0,
    )
    grad_one, last, head, film_rows, second_rows = local_kernel(
        functools.partial(second_input_body, pixel_count, col_count),
        [bf16_like(*flat), bf16_like(*edge), bf16_like(*edge), row_pair, f32_like(8, width_own)],
        [spot, back, inner, inner_sums, film, affine[1], *part_totals(rows)],
        [],
        16,
        0,
    )
    edges = edge_rows(last, head)
    both_grads = lax.all_gather(jnp.stack([grad_one, grad_two]), "wide", axis=1, tiled=True)
    back_parts = convolve_back(spot, grad_one, edges, kernel_one, row_count, col_count)
    if has_slots():
        block_pair += [*close, flipped(after(block_pairs[2], back_parts[0]), "wide", 6)]
    attn_in_grad, self_grad, cross_grad = local_kernel(
        weight_out_body,
        [f32_like(4, C // lax.axis_size("wide"), width_own)]
        + [f32_like(width_own, C // lax.axis_size("wide"))] * 2,
        [spot, after(weight_sums, back_parts[0])],
        [],
        16,
        0,
    )
    back_parts = sent_parts(back_parts)
    film_rows = after(film_rows, back_parts[1])
    time_grad, text_grad, kv_grad = local_kernel(
        text_out_body,
        [
            f32_like(time_rows, 2, width_own),
            f32_like(text_rows, 2, width_own),
            f32_like(2, text_rows, width_own),
        ],
        [spot, film_rows, own_features, own_pooled, own_text[0], *far([text_sums])],
        [],
        24,
        4 * TEXT * text_rows * width_own,
    )
    back_parts[0], attn_in_grad, time_grad = lax.optimization_barrier(
        (back_parts[0], attn_in_grad, time_grad)
    )
    mixed = sent_parts([after(part, *back_parts) for part in mixed])
    result = middle
    for part in mixed:
        result = result + part.astype(jnp.float32)
    back, rows = local_kernel(
        functools.partial(first_back_body, groups, pixel_count),
        [f32_like(*flat), f32_like(2, width_own)],
        [spot, *back_parts, own_pixels, first_sums, affine[0]],
        [],
        16,
        0,
    )
    row_parts = part_totals(rows)
    if has_slots():
        conv_grad = kernel_grad(spot, block_pair, both_grads, col_count)
    else:
        conv_grad = jnp.stack(
            [
                kernel_grad_whole(both_sends[0][:, k], both_grads[k], row_count, col_count)
                for k in range(2)
            ]
        )
    pixels_grad, gain_grad, bias_grad = local_kernel(
        functools.partial(first_input_body, pixel_count),
        [f32_like(*flat), row_pair, row_pair],
        [spot, back, own_pixels, first_sums, affine[0], grad_middle, second_rows, *row_parts],
        [],
        16,
        0,
    )
    return (
        result.reshape(own_shape),
        pixels_grad.reshape(own_shape),
        conv_grad,
        time_grad,
        text_grad,
        gain_grad,
        bias_grad,
        second_rows[3],
        second_rows[4],
        attn_in_grad,
        kv_grad,
        self_grad,
        cross_grad,
    )


def solution(mesh):
    placed = (
        P(None, "wide", None, "tensor"),
        P(),
        P(),
        P(),
        P(None, None, "wide", "tensor"),
        P("wide", None, "tensor"),
        P("wide", None, "tensor"),
        P(None, "tensor"),
        P(None, "tensor"),
        P("tensor"),
        P("tensor"),
        P(None, "wide", "tensor"),
        P(None, "wide", "tensor"),
        P("tensor", "wide"),
        P("tensor", "wide"),
        P(None, "wide", None, "tensor"),
    )
    return jax.shard_map(
        shards,
        mesh=mesh,
        in_specs=placed,
        out_specs=(
            P(None, "wide", None, "tensor"),
            P(None, "wide", None, "tensor"),
            P(None, None, "wide", "tensor"),
            P("wide", None, "tensor"),
            P("wide", None, "tensor"),
            P(None, "tensor"),
            P(None, "tensor"),
            P("tensor"),
            P("tensor"),
            P(None, "wide", "tensor"),
            P(None, "wide", "tensor"),
            P("tensor", "wide"),
            P("tensor", "wide"),
        ),
        check_vma=False,
    )
```

```python
import functools
import math

import jax
import jax.numpy as jnp
from jax import lax
from jax.experimental import pallas as pl
from jax.experimental.pallas import tpu as pltpu
from jax.sharding import PartitionSpec as P

C = 1024
GROUPS = 32
HEAD_DIM = 128
TEXT = 128
TEMB = 1024
MIB = 1 << 20
in_vmem = pl.BlockSpec(memory_space=pltpu.VMEM)
in_smem = pl.BlockSpec(memory_space=pltpu.SMEM)


def local_kernel(body, outs, operands, scratch, limit, flops, aliases=None, out_specs=None):
    size = sum(a.size * a.dtype.itemsize for a in operands)
    size += sum(math.prod(o.shape) * o.dtype.itemsize for o in outs)
    return pl.pallas_call(
        body,
        grid=(1,),
        out_shape=outs,
        in_specs=[in_smem] + [in_vmem] * (len(operands) - 1),
        out_specs=[in_vmem] * len(outs) if out_specs is None else out_specs,
        scratch_shapes=scratch,
        input_output_aliases={} if aliases is None else aliases,
        compiler_params=pltpu.CompilerParams(vmem_limit_bytes=limit * MIB),
        cost_estimate=pl.CostEstimate(flops=flops, bytes_accessed=size, transcendentals=0),
        name=getattr(body, "func", body).__name__,
    )(*operands)


def far(arrays):
    return [pltpu.with_memory_space_constraint(array, pltpu.HBM) for array in arrays]


def turned(values, width):
    rows = values.shape[0]
    wide = values.astype(jnp.float32)
    column = lax.rem(lax.broadcasted_iota(jnp.int32, values.shape, 0), width)
    before = jnp.where(column == 0, 0.0, pltpu.roll(wide, 1, 0))
    after = jnp.where(column == width - 1, 0.0, pltpu.roll(wide, rows - 1, 0))
    return before.astype(jnp.bfloat16), values, after.astype(jnp.bfloat16)


def halves_swapped(values, odd):
    half = values.shape[1] // 2
    other = jnp.concatenate([values[:, half:], values[:, :half]], axis=1)
    return jnp.where(odd, other, values)


class Weights:
    def __init__(self, refs, spot, groups):
        self.refs = refs
        self.paired = len(refs) > 1
        self.groups = groups
        self.spot = spot
        self.odd = lax.rem(spot[0], 2) == 1

    def block(self, chunk):
        return lax.bitwise_xor(lax.div(self.spot[0], 2) if self.paired else self.spot[1], chunk)

    def tap(self, chunk, position):
        if not self.paired:
            each = self.refs[0].shape[0] // self.groups
            start = self.block(chunk) * each
            parts = [self.refs[0][start + i, position] for i in range(each)]
            return jnp.concatenate(parts, axis=0)
        parts = [self.refs[chunk][position], self.refs[4 + chunk][position]]
        return jnp.concatenate(parts, axis=0)

    def ordered(self, values):
        return halves_swapped(values, self.odd) if self.paired else values


def conv_body(groups, parts, count, rows, width, spot, *refs):
    pieces = refs[:groups]
    near, far_row = refs[groups : groups + 2]
    weights = Weights(refs[groups + 2 : groups + 2 + parts], spot, groups)
    source, *rest = refs[groups + 2 + parts :]
    earlier, rest = rest[:count], rest[count:]
    first_out, second_out, *sends, frame = rest
    for send, held in zip(sends, earlier):
        send[:, 0] = held[...]
    if earlier:
        sends = [send.at[:, 1] for send in sends]
    span = pieces[0].shape[1]
    for mask in range(groups):
        block = lax.bitwise_xor(spot[1], mask)
        own = pieces[mask][...]
        lanes = slice(mask * span, (mask + 1) * span)
        framed = framed_rows(near[:, lanes], far_row[:, lanes], own, weights.odd)
        for column, values in enumerate(turned(weights.ordered(framed), width)):
            frame[block, column] = values
    total_sum = jnp.zeros(first_out.shape, jnp.float32)
    for chunk in range(groups):
        block = weights.block(chunk)
        for position in range(9):
            start = (position // 3) * width
            window = frame[block, position % 3, start : start + rows * width, :]
            total_sum += jnp.dot(
                window, weights.tap(chunk, position), preferred_element_type=jnp.float32
            )
        if len(sends) == 1:
            sends[0][chunk] = frame[chunk, 1, width : (rows + 1) * width, :]
        else:
            near = lax.bitwise_xor(lax.div(spot[0], 2), chunk)
            center = frame[near, 1, width : (rows + 1) * width, :]
            center = center if weights.paired else halves_swapped(center, weights.odd)
            sends[0][chunk] = center[:, : span // 2]
            sends[1][chunk] = center[:, span // 2 :]
    if second_out.shape[0] == 2:
        first_out[...] = total_sum
        second_out[...] = channel_sums(total_sum)
    else:
        middle = (source[...].astype(jnp.float32) + total_sum) * root_half
        first_out[...] = middle
        second_out[...] = middle.astype(jnp.bfloat16)


def back_body(groups, rows, width, spot, grad, near, far_row, *refs):
    frame, held = refs[-2:]
    outs = refs[-2 - groups : -2]
    weights = Weights(refs[: -2 - groups], spot, groups)
    framed = framed_rows(near[...], far_row[...], grad[...], weights.odd)
    for column, values in enumerate(turned(framed, width)):
        frame[column] = values
    for chunk in range(groups):
        total_sum = jnp.zeros(held.shape[1:], jnp.float32)
        for position in range(9):
            start = (2 - position // 3) * width
            total_sum += lax.dot_general(
                frame[2 - position % 3, start : start + rows * width, :],
                weights.tap(chunk, position),
                (((1,), (1,)), ((), ())),
                preferred_element_type=jnp.float32,
            )
        held[weights.block(chunk)] = weights.ordered(total_sum).astype(jnp.bfloat16)
    for mask in range(groups):
        outs[mask][...] = held[lax.bitwise_xor(spot[1], mask)]


def bf16_like(*shape):
    return jax.ShapeDtypeStruct(shape, jnp.bfloat16)


def far_like(shape):
    return pltpu.HBM(shape.shape, shape.dtype)


def f32_like(*shape):
    return jax.ShapeDtypeStruct(shape, jnp.float32)


def flipped(values, axis, mask):
    count = lax.axis_size(axis)
    return lax.ppermute(values, axis, [(i, i ^ mask) for i in range(count)])


def relayed_block(over_x, over_y):
    odd = lax.rem(lax.axis_index("wide"), 2) == 1
    far_pairs = [(i, i ^ (2 if i % 2 else 4)) for i in range(8)]
    return lax.ppermute(jnp.where(odd, over_y, over_x), "wide", far_pairs)


def over_chips(values):
    over_x, over_y = flipped(values, "wide", 2), flipped(values, "wide", 4)
    return [values, over_x, over_y, relayed_block(over_x, over_y)]


def has_slots():
    return lax.axis_size("wide") == 8


def after(value, *others):
    return lax.optimization_barrier((value, others))[0]


def gathered_blocks(blocks):
    return [lax.all_gather(blocks, "wide")]


def spread_chips(values):
    if has_slots():
        return over_chips(values)
    mask = 2
    while mask < lax.axis_size("wide"):
        values = jnp.concatenate([values, flipped(values, "wide", mask)])
        mask *= 2
    return [values]


def gathered_sums(parts):
    if has_slots():
        return [parts[0]] + [flipped(parts[k], "wide", 2 * k) for k in range(1, 4)]
    values = parts[0]
    mask = lax.axis_size("wide") // 2
    while mask > 1:
        half = values.shape[0] // 2
        values = values[:half] + flipped(values[half:], "wide", mask)
        mask //= 2
    return [values]


def channel_pieces(values):
    count = lax.axis_size("tensor")
    return [values] + [flipped(values, "tensor", mask) for mask in range(1, count)]


def edge_rows(near, far_row):
    count = lax.axis_size("wide")
    beyond = [(i, i + 1) for i in range(1, count - 1, 2)]
    beyond += [(i + 1, i) for i in range(1, count - 1, 2)]
    from_far = lax.ppermute(far_row, "wide", beyond)
    return flipped(after(near, far_row), "wide", 1), from_far


def framed_rows(near, far_row, own, odd):
    top = jnp.where(odd, near, far_row)
    bottom = jnp.where(odd, far_row, near)
    return jnp.concatenate([top, own, bottom], axis=0)


def convolve(spot, pieces, edges, kernel, source, second_shape, earlier, rows, width):
    groups, (area, span) = len(pieces), pieces[0].shape
    count, block = (2, span // 2) if has_slots() else (1, span)
    layers = (2,) if earlier else ()
    sends = [bf16_like(groups, *layers, area, block)] * count
    return local_kernel(
        functools.partial(conv_body, groups, len(kernel), len(earlier), rows, width),
        [f32_like(area, span), second_shape] + sends,
        [spot, *pieces, *edges, *far(kernel), source, *far(earlier)],
        [pltpu.VMEM((groups, 3, (rows + 2) * width, span), jnp.bfloat16)],
        32,
        2 * 9 * area * C * span,
    )


def piece_edges(pieces, width):
    odd = lax.rem(lax.axis_index("wide"), 2) == 1
    last = jnp.concatenate([piece[-width:] for piece in pieces], axis=1)
    first = jnp.concatenate([piece[:width] for piece in pieces], axis=1)
    return edge_rows(jnp.where(odd, first, last), jnp.where(odd, last, first))


def convolve_back(spot, grad, edges, kernel, rows, width):
    groups, (area, span) = lax.axis_size("tensor"), grad.shape
    return local_kernel(
        functools.partial(back_body, groups, rows, width),
        [bf16_like(area, span)] * groups,
        [spot, grad, *edges, *far(kernel)],
        [
            pltpu.VMEM((3, (rows + 2) * width, span), jnp.bfloat16),
            pltpu.VMEM((groups, area, span), jnp.bfloat16),
        ],
        32,
        2 * 9 * area * C * span,
    )


def sent_parts(parts):
    return [parts[0]] + [flipped(parts[mask], "tensor", mask) for mask in range(1, len(parts))]


def kernel_grad_body(width, spot, kept, got, *refs):
    *pairs, grads, out, turned_all = refs
    layer = pl.program_id(0)
    area, span = kept.shape[2:]
    depth = 8 * area
    turned_all[:, :width] = jnp.zeros((3 * span, width), jnp.bfloat16)
    turned_all[:, depth + width :] = jnp.zeros((3 * span, width), jnp.bfloat16)
    pieces = [kept[0, layer], got[0, layer]]
    pieces += [pair[core, layer] for pair in pairs for core in range(2)]
    lane = lax.broadcasted_iota(jnp.int32, (span, width), 1)
    for mask, piece in enumerate(pieces):
        start = pl.multiple_of(lax.bitwise_xor(spot[0], mask) * area, area)
        flat = jnp.transpose(piece.astype(jnp.float32))
        for row in range(area // width):
            center = flat[:, row * width : (row + 1) * width]
            before = jnp.where(lane == 0, 0.0, pltpu.roll(center, 1, 1))
            behind = jnp.where(lane == width - 1, 0.0, pltpu.roll(center, width - 1, 1))
            lanes = pl.ds(start + (row + 1) * width, width)
            for column, values in enumerate((before, center, behind)):
                turned_all[column * span : (column + 1) * span, lanes] = values.astype(jnp.bfloat16)
    for row in range(3):
        product = dot(turned_all[:, row * width : row * width + depth], grads[0])
        for column in range(3):
            out[0, 3 * row + column] = product[column * span : (column + 1) * span, :]


def kernel_grad(spot, pieces, grads, width):
    span = pieces[0].shape[3]
    depth, columns = grads.shape[1:]
    return pl.pallas_call(
        functools.partial(kernel_grad_body, width),
        out_shape=f32_like(2, 9, span, columns),
        grid=(2,),
        in_specs=[in_smem]
        + [in_vmem] * len(pieces)
        + [pl.BlockSpec((1, depth, columns), lambda i: (i, 0, 0))],
        out_specs=pl.BlockSpec((1, 9, span, columns), lambda i: (i, 0, 0, 0)),
        scratch_shapes=[pltpu.VMEM((3 * span, depth + 2 * width), jnp.bfloat16)],
        compiler_params=pltpu.CompilerParams(vmem_limit_bytes=24 * MIB),
        cost_estimate=pl.CostEstimate(
            flops=4 * 9 * depth * span * columns, bytes_accessed=6 * MIB, transcendentals=0
        ),
        name="kernel_grad_body",
    )(spot, *far(pieces), *far([grads]))


def kernel_grad_whole(send, grads, rows, width):
    natural = jnp.moveaxis(send, 0, 1).reshape(1, rows, width, C)
    swapped = lax.all_to_all(natural, "wide", split_axis=3, concat_axis=1, tiled=True)
    framed = jnp.pad(swapped, ((0, 0), (1, 1), (1, 1), (0, 0)))
    low = grads.reshape(1, -1, width, grads.shape[1])
    return jnp.stack(
        [
            jnp.einsum(
                "mrwc,mrwd->cd",
                framed[:, tap // 3 : tap // 3 + low.shape[1], tap % 3 : tap % 3 + width, :],
                low,
                preferred_element_type=jnp.float32,
            )
            for tap in range(9)
        ]
    )


root_half = 1.0 / math.sqrt(2.0)
highest = lax.Precision.HIGHEST


def sinusoid(steps):
    half_width = TEMB // 2
    frequency = jnp.exp(-math.log(10000.0) * jnp.arange(half_width, dtype=jnp.float32) / half_width)
    angles = steps.astype(jnp.float32)[:, None] * frequency[None, :]
    return jnp.concatenate([jnp.cos(angles), jnp.sin(angles)], axis=1)


def chip_parts(values):
    if has_slots():
        return [values] + [flipped(values, "wide", mask) for mask in (2, 4, 6)]
    mask = 2
    while mask < lax.axis_size("wide"):
        values = values + flipped(values, "wide", mask)
        mask *= 2
    return [values]


def part_totals(rows):
    return chip_parts(rows + flipped(rows, "wide", 1))


def sum_of_parts(refs):
    if len(refs) == 1:
        return refs[0][...]
    return (refs[0][...] + refs[1][...]) + (refs[2][...] + refs[3][...])


def total(values, axis, mask=1):
    while mask < lax.axis_size(axis):
        values = values + flipped(values, axis, mask)
        mask *= 2
    return values


def silu_slope(values):
    logistic = lax.logistic(values)
    return logistic * (1.0 + values * (1.0 - logistic))


def channel_sums(values):
    return jnp.concatenate(
        [
            jnp.sum(values, axis=0, keepdims=True),
            jnp.sum(values * values, axis=0, keepdims=True),
        ],
        axis=0,
    )


def group_means(first, second, pixel_count):
    channels = first.shape[1]
    per_group = C // GROUPS
    row = lax.div(lax.broadcasted_iota(jnp.int32, (channels, channels), 0), per_group)
    column = lax.div(lax.broadcasted_iota(jnp.int32, (channels, channels), 1), per_group)
    same = jnp.where(row == column, 1.0, 0.0)
    rows = jnp.concatenate([first, second, jnp.zeros((6, channels), jnp.float32)], axis=0)
    means = jnp.dot(rows, same, precision=highest, preferred_element_type=jnp.float32)
    means = means / (pixel_count * per_group)
    return means[0:1], means[1:2]


def group_scale(first, second, pixel_count):
    center, square = group_means(first, second, pixel_count)
    return center, lax.rsqrt(square - center * center + 1e-05)


def lifted_sums(sums, film, pixel_count):
    slope, shift = 1.0 + film[0:1], film[1:2]
    plain, square = sums[0:1], sums[1:2]
    return (
        slope * plain + pixel_count * shift,
        slope * slope * square + 2.0 * slope * shift * plain + pixel_count * shift * shift,
    )


def silu_low(values):
    return (values * lax.logistic(values)).astype(jnp.bfloat16)


def first_norm_body(pixel_count, spot, pixels, affine, *refs):
    *parts, out, sums = refs
    sums[...] = sum_of_parts(parts)
    center, inverse = group_scale(sums[0:1], sums[1:2], pixel_count)
    scaled = (pixels[...].astype(jnp.float32) - center) * inverse
    out[...] = silu_low(scaled * affine[0:1] + affine[1:2])


def second_norm_body(pixel_count, spot, inner, affine, *refs):
    *parts, out, film, sums = refs
    summed = sum_of_parts(parts)
    film[...], sums[...] = summed[:2], summed[2:]
    center, inverse = group_scale(*lifted_sums(sums[...], film[...], pixel_count), pixel_count)
    lifted = inner[...] * (1.0 + film[0:1]) + film[1:2]
    out[...] = silu_low((lifted - center) * inverse * affine[0:1] + affine[1:2])


def parts_sum(refs):
    summed = refs[0][...].astype(jnp.float32)
    for ref in refs[1:]:
        summed += ref[...].astype(jnp.float32)
    return summed


def stacked_rows(rows):
    return jnp.concatenate([jnp.sum(row, axis=0, keepdims=True) for row in rows], axis=0)


def second_back_body(groups, pixel_count, spot, *refs):
    inner, sums, film, affine, terms, out, rows = refs[groups:]
    center, inverse = group_scale(*lifted_sums(sums[...], film[...], pixel_count), pixel_count)
    own = inner[...]
    scaled = (own * (1.0 + film[0:1]) + film[1:2] - center) * inverse
    back = parts_sum(refs[:groups]) * silu_slope(scaled * affine[0:1] + affine[1:2])
    out[...] = back
    rows[0:3, :] = stacked_rows([back * scaled, back, back * own])
    rows[3:5, :] = terms[...]
    rows[5:8, :] = jnp.zeros((3, own.shape[1]), jnp.float32)


def second_input_body(pixel_count, width, spot, back, inner, sums, film, affine, *refs):
    *parts, low, near, far_row, film_rows, rows = refs
    rows[...] = sum_of_parts(parts)
    slope, shift, gain = 1.0 + film[0:1], film[1:2], affine[0:1]
    plain_sum, square_sum = sums[0:1], sums[1:2]
    lifted_sum, lifted_square = lifted_sums(sums[...], film[...], pixel_count)
    center, inverse = group_scale(lifted_sum, lifted_square, pixel_count)
    dotted, plain = group_means(gain * rows[0:1], gain * rows[1:2], pixel_count)
    scaled = (inner[...] * slope + shift - center) * inverse
    grad = inverse * (back[...] * gain - plain - scaled * dotted)
    grad_low = (grad * slope).astype(jnp.bfloat16)
    low[...] = grad_low
    odd = lax.rem(spot[0], 2) == 1
    near[...] = jnp.where(odd, grad_low[:width], grad_low[-width:])
    far_row[...] = jnp.where(odd, grad_low[-width:], grad_low[:width])
    scaled_sum = inverse * (lifted_sum - pixel_count * center)
    scaled_inner = inverse * (slope * square_sum + (shift - center) * plain_sum)
    film_rows[0:1, :] = inverse * (
        gain * rows[2:3] - plain * plain_sum - dotted * scaled_inner
    )
    film_rows[1:2, :] = inverse * (
        gain * rows[1:2] - pixel_count * plain - dotted * scaled_sum
    )


def first_back_body(groups, pixel_count, spot, *refs):
    pixels, sums, affine, out, rows = refs[groups:]
    center, inverse = group_scale(sums[0:1], sums[1:2], pixel_count)
    scaled = (pixels[...].astype(jnp.float32) - center) * inverse
    back = parts_sum(refs[:groups]) * silu_slope(scaled * affine[0:1] + affine[1:2])
    out[...] = back
    rows[...] = stacked_rows([back * scaled, back])


def first_input_body(pixel_count, spot, back, pixels, sums, affine, middle, second, *refs):
    *parts, out, gains, biases = refs
    rows = sum_of_parts(parts)
    gains[...] = jnp.concatenate([rows[0:1], second[0:1]], axis=0)
    biases[...] = jnp.concatenate([rows[1:2], second[1:2]], axis=0)
    gain = affine[0:1]
    center, inverse = group_scale(sums[0:1], sums[1:2], pixel_count)
    dotted, plain = group_means(gain * rows[0:1], gain * rows[1:2], pixel_count)
    scaled = (pixels[...].astype(jnp.float32) - center) * inverse
    out[...] = inverse * (back[...] * gain - plain - scaled * dotted) + middle[...] * root_half


def dot(left, right):
    return jnp.dot(left, right, preferred_element_type=jnp.float32)


def dot_last(left, right):
    return lax.dot_general(
        left, right, (((1,), (1,)), ((), ())), preferred_element_type=jnp.float32
    )


def flat_turn(values):
    return jnp.transpose(values.astype(jnp.float32)).astype(jnp.bfloat16)


def dot_first(left, right):
    return dot(flat_turn(left), right)


def head_choice(values, odd):
    first, second = values[:, :HEAD_DIM], values[:, HEAD_DIM:]
    return jnp.where(odd, second, first), jnp.where(odd, first, second)


def heads_joined(kept, received, odd):
    return jnp.where(
        odd,
        jnp.concatenate([received, kept], axis=1),
        jnp.concatenate([kept, received], axis=1),
    )


def packed_rows(values):
    rows = []
    for _ in range(3):
        rows.append(values.astype(jnp.bfloat16).astype(jnp.float32))
        values = values - rows[-1]
    rows.append(jnp.zeros((10, values.shape[1]), jnp.float32))
    return jnp.concatenate(rows, axis=0).astype(jnp.bfloat16)


def unpacked_rows(packed, area):
    rows = packed[area:, :].astype(jnp.float32)
    return rows[0:1] + rows[2:3] + rows[4:5], rows[1:2] + rows[3:4] + rows[5:6]


def prepare_body(spot, pixels, cotangent, gain, bias, pack, sums):
    area = cotangent.shape[0]
    pack[:area] = cotangent[...].astype(jnp.bfloat16)
    pack[area:] = packed_rows(jnp.concatenate([gain[...], bias[...]], axis=0))
    sums[...] = channel_sums(pixels[...].astype(jnp.float32))


def project_body(groups, spot, *refs):
    pieces, packs = refs[:groups], refs[groups : 2 * groups]
    own, maps, keep_query, keep, send, cross, normed, scaled, center, inverse = refs[2 * groups :]
    weights = Weights([maps], spot, groups)
    odd = lax.rem(spot[0], 2) == 1
    area = own.shape[0]
    token_sum = token_square = 0.0
    for piece in pieces:
        values = piece[...].astype(jnp.float32)
        token_sum += jnp.sum(values, axis=1, keepdims=True)
        token_square += jnp.sum(values * values, axis=1, keepdims=True)
    mean = token_sum / C
    scale = lax.rsqrt(token_square / C - mean * mean + 1e-05)
    lows = []
    for mask in range(groups):
        gain, bias = unpacked_rows(packs[mask], area)
        values = (pieces[mask][...].astype(jnp.float32) - mean) * scale
        lows.append((values * gain + bias).astype(jnp.bfloat16))
        normed[lax.bitwise_xor(spot[1], mask)] = lows[-1]
    center[...] = mean
    inverse[...] = scale
    scaled[...] = (own[...] - mean) * scale
    projected = []
    for position in range(4):
        total_sum = 0.0
        for mask in range(groups):
            total_sum += dot(lows[mask], weights.tap(mask, position))
        projected.append(total_sum.astype(jnp.bfloat16))
    cross[...] = projected[3]
    chosen = [head_choice(values, odd) for values in projected[:3]]
    chosen = chosen[1:] + chosen[:1]
    keep_query[...] = chosen[2][0]
    keep[...] = jnp.concatenate([pair[0] for pair in chosen[:2]], axis=1)
    send[...] = jnp.concatenate([pair[1] for pair in chosen], axis=1)


def out_grad_body(groups, spot, *refs):
    packs = refs[:groups]
    maps, keep, send, cross = refs[groups:]
    weights = Weights([maps], spot, groups)
    sums = []
    for position in (4, 5):
        total_sum = 0.0
        for mask in range(groups):
            total_sum += dot(packs[mask][: cross.shape[0]], weights.tap(mask, position))
        sums.append(total_sum.astype(jnp.bfloat16))
    kept, sent = head_choice(sums[0], lax.rem(spot[0], 2) == 1)
    keep[...] = kept
    send[...] = sent
    cross[...] = sums[1]


def text_out_body(spot, film, features, pooled, text, parts, time_grad, text_grad, kv_grad):
    for rows, out in ((features, time_grad), (pooled, text_grad)):
        column = jnp.transpose(jnp.broadcast_to(rows[...].astype(jnp.float32), (8, rows.shape[1])))
        for part in range(2):
            out[:, part, :] = column[:, 0:1] * film[part : part + 1, :]
    summed = leading_sum(parts)
    turned_text = flat_turn(text[...])
    for part in range(2):
        high = summed[part].astype(jnp.bfloat16)
        low = (summed[part] - high.astype(jnp.float32)).astype(jnp.bfloat16)
        kv_grad[part] = dot(turned_text, high) + dot(turned_text, low)


def mix_body(groups, spot, kept, other, crossed, maps, *outs):
    weights = Weights([maps], spot, groups)
    attended = heads_joined(kept[...], other[...], lax.rem(spot[0], 2) == 1)
    for mask in range(groups):
        total_sum = dot_last(attended, weights.tap(mask, 4))
        total_sum += dot_last(crossed[...], weights.tap(mask, 5))
        outs[mask][...] = total_sum.astype(jnp.bfloat16)


def over_rows(refs, step, state):
    for index, ref in enumerate(refs):
        rows = ref.shape[0]
        if rows <= 512:
            state = step(state, ref[...], index, 0)
        else:
            state = lax.fori_loop(
                0,
                rows // 512,
                lambda i, held: step(
                    held, ref[pl.ds(pl.multiple_of(i * 512, 512), 512), :], index, i * 512
                ),
                state,
            )
    return state


score_scale = HEAD_DIM ** (-0.5)


def cross_body(spot, query, grad, parts, *refs):
    *blocks, crossed, grad_query, text_grad = refs
    if blocks:
        kept_block, got_block, *pairs = blocks
        for index, pair in enumerate(pairs):
            pair[0] = kept_block[index + 1]
            pair[1] = got_block[index + 1]
    text = leading_sum(parts).astype(jnp.bfloat16)
    live = lax.broadcasted_iota(jnp.int32, (query.shape[0], text.shape[1]), 1) < spot[2]
    for head in range(query.shape[1] // HEAD_DIM):
        lanes = slice(head * HEAD_DIM, (head + 1) * HEAD_DIM)
        own, keys, values, back = query[:, lanes], text[0, :, lanes], text[1, :, lanes], grad[:, lanes]
        scores = jnp.where(live, dot_last(own, keys) * score_scale, -1e30)
        weights = jnp.exp(scores - jnp.max(scores, axis=1, keepdims=True))
        probs = weights / jnp.sum(weights, axis=1, keepdims=True)
        low = probs.astype(jnp.bfloat16)
        crossed[:, lanes] = dot(low, values).astype(jnp.bfloat16)
        grad_probs = dot_last(back, values)
        grad_scores = probs * (grad_probs - jnp.sum(probs * grad_probs, axis=1, keepdims=True))
        grad_low = grad_scores.astype(jnp.bfloat16)
        grad_query[:, lanes] = (dot(grad_low, keys) * score_scale).astype(jnp.bfloat16)
        text_grad[0, :, lanes] = (dot_first(grad_low, own) * score_scale).astype(jnp.bfloat16)
        text_grad[1, :, lanes] = dot_first(low, back).astype(jnp.bfloat16)


def attend_body(count, extra, spot, kept_query, got, kept_grad, got_grad, *refs):
    blocks, refs = refs[:count], refs[count:]
    cross_in, refs = refs[: 3 + extra], refs[3 + extra :]
    parts, refs = refs[:count], refs[count:]
    keep_out, send_out, keep_query, send_query, *cross_out = refs
    cross_body(spot, *cross_in, *cross_out)
    query = jnp.concatenate([kept_query[...], got[:, 2 * HEAD_DIM :]], axis=0)
    grad = jnp.concatenate([kept_grad[...], got_grad[...]], axis=0)
    queries = query.shape[0]

    def forward(state, block, index, start):
        top, weight_sum, weighted = state
        scores = dot_last(block[:, :HEAD_DIM], query) * score_scale
        raised = jnp.maximum(top, jnp.max(scores, axis=0, keepdims=True))
        rescale = jnp.exp(top - raised)
        weights = jnp.exp(scores - raised)
        weight_sum = weight_sum * rescale + jnp.sum(weights, axis=0, keepdims=True)
        values = block[:, HEAD_DIM:]
        weighted = weighted * rescale + dot_first(values, weights.astype(jnp.bfloat16))
        return raised, weight_sum, weighted

    top, weight_sum, weighted = over_rows(
        blocks,
        forward,
        (
            jnp.full((1, queries), -1e30, jnp.float32),
            jnp.zeros((1, queries), jnp.float32),
            jnp.zeros((HEAD_DIM, queries), jnp.float32),
        ),
    )
    attended = weighted / weight_sum
    delta = jnp.sum(attended * jnp.transpose(grad.astype(jnp.float32)), axis=0, keepdims=True)
    log_sum = top + jnp.log(weight_sum)

    def backward(state, block, index, start):
        keys, values = block[:, :HEAD_DIM], block[:, HEAD_DIM:]
        probs = jnp.exp(dot_last(keys, query) * score_scale - log_sum)
        grad_values = dot(probs.astype(jnp.bfloat16), grad)
        grad_scores = (probs * (dot_last(values, grad) - delta)).astype(jnp.bfloat16)
        grad_keys = dot(grad_scores, query) * score_scale
        rows = pl.ds(start if isinstance(start, int) else pl.multiple_of(start, 512), block.shape[0])
        parts[index][rows, :] = jnp.concatenate([grad_keys, grad_values], axis=1).astype(
            jnp.bfloat16
        )
        return state + dot_first(keys, grad_scores)

    flat = over_rows(blocks, backward, jnp.zeros((HEAD_DIM, queries), jnp.float32))
    for values, keep, send in (
        (attended, keep_out, send_out),
        (flat * score_scale, keep_query, send_query),
    ):
        turned_back = jnp.transpose(values).astype(jnp.bfloat16)
        keep[...] = turned_back[: queries // 2]
        send[...] = turned_back[queries // 2 :]


def key_sum_body(spot, sent_query, *refs):
    *parts, keep, send = refs
    both = parts_sum(parts).astype(jnp.bfloat16)
    half = keep.shape[0]
    keep[...] = both[:half]
    send[:, : 2 * HEAD_DIM] = both[half:]
    send[:, 2 * HEAD_DIM :] = sent_query[...]


def leading_sum(ref):
    summed = ref[0].astype(jnp.float32)
    for index in range(1, ref.shape[0]):
        summed += ref[index].astype(jnp.float32)
    return summed


def joined_grads(spot, kept_query, kept_pair, got, cross):
    odd = lax.rem(spot[0], 2) == 1
    parts = [got[:, i * HEAD_DIM : (i + 1) * HEAD_DIM] for i in range(3)]
    return [
        heads_joined(kept_query[...], parts[2], odd),
        heads_joined(kept_pair[:, :HEAD_DIM], parts[0], odd),
        heads_joined(kept_pair[:, HEAD_DIM:], parts[1], odd),
        cross[...],
    ]


def project_back_body(groups, spot, kq, kp, got, cross, center, inverse, kept, other, *refs):
    crossed, normed, maps, *refs = refs
    pieces, packs = refs[:groups], refs[groups : 2 * groups]
    *outs, out, frame = refs[2 * groups :]
    odd = lax.rem(spot[0], 2) == 1
    weights = Weights([maps], spot, groups)
    grads = joined_grads(spot, kq, kp, got, cross)
    area, span = cross.shape
    plain = dotted = 0.0
    for mask in range(groups):
        part = 0.0
        for position in range(4):
            part += dot_last(grads[position], weights.tap(mask, position))
        outs[mask][:area] = part.astype(jnp.bfloat16)
        eased = part * unpacked_rows(packs[mask], area)[0]
        unit = (pieces[mask][...].astype(jnp.float32) - center[...]) * inverse[...]
        plain += eased
        dotted += eased * unit
    ones = jnp.ones((8, plain.shape[1]), jnp.float32)
    sums = [
        lax.dot_general(
            ones,
            values,
            (((1,), (1,)), ((), ())),
            precision=highest,
            preferred_element_type=jnp.float32,
        )[0:1]
        for values in (plain, dotted)
    ]
    packed = packed_rows(jnp.concatenate(sums, axis=0))
    for part in outs:
        part[area:] = packed
    right = jnp.concatenate(grads, axis=1)
    out_right = jnp.concatenate([heads_joined(kept[...], other[...], odd), crossed[...]], axis=1)
    for mask in range(groups):
        frame[lax.bitwise_xor(spot[1], mask)] = packs[mask][:area]
    for chunk in range(groups):
        rows = slice(chunk * span, (chunk + 1) * span)
        out[rows, : 4 * span] = dot_first(normed[chunk], right).astype(jnp.bfloat16)
        out[rows, 4 * span :] = dot_first(frame[chunk], out_right).astype(jnp.bfloat16)


def weight_out_body(spot, sums, in_grad, self_grad, cross_grad):
    summed = sums[...].astype(jnp.float32)
    span = in_grad.shape[2]
    for position in range(4):
        in_grad[position] = summed[:, position * span : (position + 1) * span]
    self_grad[...] = jnp.transpose(summed[:, 4 * span : 5 * span])
    cross_grad[...] = jnp.transpose(summed[:, 5 * span :])


def norm_back_body(groups, width, spot, *refs):
    scaled, inverse, cotangent, gain, middle, low, near, far_row, terms = refs[groups:]
    area = scaled.shape[0]
    grad = plain = dotted = 0.0
    for ref in refs[:groups]:
        grad += ref[:area].astype(jnp.float32)
        sums = unpacked_rows(ref, area)
        plain, dotted = plain + sums[0], dotted + sums[1]
    same = lax.broadcasted_iota(jnp.int32, (area, area), 0) == lax.broadcasted_iota(
        jnp.int32, (area, area), 1
    )
    plain = jnp.sum(jnp.where(same, plain, 0.0), axis=1, keepdims=True) / C
    dotted = jnp.sum(jnp.where(same, dotted, 0.0), axis=1, keepdims=True) / C
    unit = scaled[...]
    terms[0:1, :] = jnp.sum(grad * unit, axis=0, keepdims=True)
    terms[1:2, :] = jnp.sum(grad, axis=0, keepdims=True)
    back = inverse[...] * (grad * gain[...] - plain - unit * dotted) + cotangent[...]
    middle[...] = back
    grad_low = (back * root_half).astype(jnp.bfloat16)
    low[...] = grad_low
    odd = lax.rem(spot[0], 2) == 1
    near[...] = jnp.where(odd, grad_low[:width], grad_low[-width:])
    far_row[...] = jnp.where(odd, grad_low[-width:], grad_low[:width])


def shards(
    pixels,
    text_states,
    text_length,
    timestep,
    conv_weights,
    film_time,
    film_text,
    group_gain,
    group_bias,
    layer_gain,
    layer_bias,
    attn_in,
    text_kv,
    out_self,
    out_cross,
    cotangent,
):
    map_count, row_count, col_count, width_own = pixels.shape
    token_count = row_count * col_count
    groups = lax.axis_size("tensor")
    pixel_count = token_count * lax.axis_size("wide")
    own_shape = (map_count, row_count, col_count, width_own)
    flat = (token_count, width_own)
    half = (token_count, HEAD_DIM)
    square = 2 * token_count * C * width_own
    edge = (col_count, width_own)
    spot = jnp.stack([lax.axis_index("wide"), lax.axis_index("tensor"), text_length[0]])
    spot = spot.astype(jnp.int32)
    own_pixels = pixels.reshape(flat)
    flat_cotangent = cotangent.reshape(flat)
    affine = [jnp.stack([group_gain[layer], group_bias[layer]]) for layer in range(2)]

    pack, sums = local_kernel(
        prepare_body,
        [bf16_like(token_count + 16, width_own), f32_like(2, width_own)],
        [spot, *far([own_pixels, flat_cotangent, layer_gain[None], layer_bias[None]])],
        [],
        8,
        0,
    )
    first_parts = part_totals(sums)
    kernel_one = gathered_blocks(conv_weights[0])
    features = sinusoid(timestep).astype(jnp.bfloat16)
    present = jnp.arange(TEXT)[None, :] < text_length[:, None]
    pooled = jnp.einsum(
        "mtx,mt->mx", text_states, present.astype(jnp.bfloat16), preferred_element_type=jnp.float32
    )
    pooled = (pooled / text_length.astype(jnp.float32)[:, None]).astype(jnp.bfloat16)
    wide_index = lax.axis_index("wide")
    time_rows = film_time.shape[0]
    text_rows = film_text.shape[0]
    own_features = lax.dynamic_slice_in_dim(features, wide_index * time_rows, time_rows, 1)
    own_pooled = lax.dynamic_slice_in_dim(pooled, wide_index * text_rows, text_rows, 1)
    own_text = lax.dynamic_slice_in_dim(text_states, wide_index * text_rows, text_rows, 2)
    film_term = jnp.einsum(
        "mk,ksc->msc", own_features, film_time, preferred_element_type=jnp.float32
    ) + jnp.einsum("mk,ksc->msc", own_pooled, film_text, preferred_element_type=jnp.float32)
    text_term = jnp.einsum("mtx,pxd->pmtd", own_text, text_kv, preferred_element_type=jnp.float32)
    text_term = text_term.astype(jnp.bfloat16).reshape(2, TEXT, width_own)

    row_pair = f32_like(2, width_own)
    first, first_sums = local_kernel(
        functools.partial(first_norm_body, pixel_count),
        [bf16_like(*flat), row_pair],
        [spot, own_pixels, affine[0], *first_parts],
        [],
        8,
        0,
    )
    maps = jnp.concatenate(
        [after(attn_in, first), jnp.transpose(after(jnp.stack([out_self, out_cross]), first), (0, 2, 1))], axis=0
    )
    maps = gathered_blocks(maps)[0]
    packs = channel_pieces(pack)
    pieces = channel_pieces(after(first, packs))
    edges = piece_edges(pieces, col_count)
    later = after(conv_weights, first)[1]
    if has_slots():
        kernel_two = over_chips(later)
        last = after(kernel_two[3], *edges)
        kernel_two += [flipped(part, "wide", 1) for part in [*kernel_two[:3], last]]
    else:
        kernel_two = gathered_blocks(later)
    pieces[0] = after(pieces[0], film_term, text_term)
    inner, sums, *first_sends = convolve(
        spot, pieces, edges, kernel_one, own_pixels, row_pair, [], row_count, col_count
    )
    sums = after(sums, kernel_two)
    inner_parts = part_totals(jnp.concatenate([film_term[0], sums]))
    second, film, inner_sums = local_kernel(
        functools.partial(second_norm_body, pixel_count),
        [bf16_like(*flat), row_pair, row_pair],
        [spot, inner, affine[1], *inner_parts],
        [],
        8,
        0,
    )
    text_all = lax.all_gather(after(text_term, second), "wide")
    pieces = channel_pieces(second)
    edges = piece_edges(pieces, col_count)
    middle, middle_low, *both_sends = convolve(
        spot,
        pieces,
        edges,
        kernel_two,
        own_pixels,
        bf16_like(*flat),
        first_sends,
        row_count,
        col_count,
    )

    middle_pieces = channel_pieces(middle_low)
    block_pair = [both_sends[0], flipped(both_sends[1], "wide", 1)] if has_slots() else []
    kept_grad, sent_grad, grad_crossed = local_kernel(
        functools.partial(out_grad_body, groups),
        [bf16_like(*half), bf16_like(*half), bf16_like(*flat)],
        [spot, *far([after(packs[0], middle_low)] + packs[1:]), *far([maps])],
        [],
        16,
        2 * square,
    )
    got_grad = flipped(sent_grad, "wide", 1)
    middle_pieces[0] = after(middle_pieces[0], got_grad, block_pair)
    column = f32_like(token_count, 1)
    triple = bf16_like(token_count, 3 * HEAD_DIM)
    kept_query, kept_pair, sent, cross_query, normed, scaled, center, inverse = local_kernel(
        functools.partial(project_body, groups),
        [
            bf16_like(*half),
            bf16_like(*flat),
            triple,
            bf16_like(*flat),
            far_like(bf16_like(groups, *flat)),
            far_like(f32_like(*flat)),
            far_like(column),
            far_like(column),
        ],
        [spot, *middle_pieces, *far(packs), middle, *far([maps])],
        [],
        24,
        4 * square,
    )
    got = flipped(sent, "wide", 1)
    blocks = spread_chips(jnp.concatenate([kept_pair, got[:, : 2 * HEAD_DIM]]))
    pair_shapes = [bf16_like(2, *block.shape[1:]) for block in block_pair[:1] * 3]
    attend_shapes = [bf16_like(*block.shape) for block in blocks] + [bf16_like(*half)] * 4
    cross_shapes = [bf16_like(*flat), bf16_like(*flat), bf16_like(2, TEXT, width_own)]
    outs = local_kernel(
        functools.partial(attend_body, len(blocks), len(block_pair)),
        [far_like(shape) for shape in attend_shapes + pair_shapes + cross_shapes],
        [
            spot,
            kept_query,
            got,
            *far([kept_grad, got_grad]),
            *blocks,
            cross_query,
            *far([grad_crossed, text_all]),
            *far(block_pair),
        ],
        [],
        48,
        14 * (2 * token_count) * HEAD_DIM * pixel_count,
    )
    key_parts, outs = outs[: len(blocks)], outs[len(blocks) :]
    kept_out, sent_out, kept_dq, sent_dq, *block_pairs = outs
    *block_pairs, crossed, grad_cross_query, text_grads = block_pairs
    text_sums = lax.all_gather(text_grads, "wide")
    key_sums = gathered_sums(key_parts)
    kept_dk, sent_all = local_kernel(
        key_sum_body,
        [bf16_like(*flat), bf16_like(token_count, 3 * HEAD_DIM)],
        [spot, *far([sent_dq, key_sums[0]]), *key_sums[1:]],
        [],
        16,
        0,
    )
    got_all = flipped(sent_all, "wide", 1)
    got_out = flipped(sent_out, "wide", 1)
    kept_dq, grad_cross_query = far([kept_dq, grad_cross_query])
    projected_grads = [kept_dq, kept_dk, got_all, grad_cross_query]
    *norm_parts, weight_parts = local_kernel(
        functools.partial(project_back_body, groups),
        [bf16_like(token_count + 16, width_own)] * groups + [far_like(bf16_like(C, 6 * width_own))],
        [
            spot,
            *projected_grads,
            *far([center, inverse, kept_out, got_out, crossed, normed, maps]),
            *far(middle_pieces),
            *far(packs),
        ],
        [pltpu.VMEM((groups, *flat), jnp.bfloat16)],
        32,
        10 * square,
    )
    weight_sums = lax.psum_scatter(weight_parts, "wide", scatter_dimension=0, tiled=True)
    received = sent_parts(norm_parts)
    if has_slots():
        close = [flipped(after(block_pairs[k], norm_parts[0]), "wide", 2 * k + 2) for k in range(2)]
        received[0] = after(received[0], close)
    grad_middle, grad_two, last, head, terms = local_kernel(
        functools.partial(norm_back_body, groups, col_count),
        [
            f32_like(*flat),
            bf16_like(*flat),
            bf16_like(*edge),
            bf16_like(*edge),
            f32_like(2, width_own),
        ],
        [
            spot,
            *received,
            scaled,
            inverse,
            flat_cotangent,
            layer_gain[None],
        ],
        [],
        16,
        0,
    )

    edges = edge_rows(last, head)
    mixed = local_kernel(
        functools.partial(mix_body, groups),
        [bf16_like(*flat)] * groups,
        [spot, after(kept_out, grad_two), got_out, *far([crossed, maps])],
        [],
        16,
        2 * square,
    )
    back_parts = convolve_back(
        spot, after(grad_two, mixed), edges, kernel_two, row_count, col_count
    )
    mixed = sent_parts([after(part, back_parts[0]) for part in mixed])
    result = middle
    for part in mixed:
        result = result + part.astype(jnp.float32)
    back_parts = sent_parts(back_parts)
    back, rows = local_kernel(
        functools.partial(second_back_body, groups, pixel_count),
        [f32_like(*flat), f32_like(8, width_own)],
        [spot, *back_parts, inner, inner_sums, film, affine[1], terms],
        [],
        16,
        0,
    )
    grad_one, last, head, film_rows, second_rows = local_kernel(
        functools.partial(second_input_body, pixel_count, col_count),
        [bf16_like(*flat), bf16_like(*edge), bf16_like(*edge), row_pair, f32_like(8, width_own)],
        [spot, after(back, mixed), inner, inner_sums, film, affine[1], *part_totals(rows)],
        [],
        16,
        0,
    )
    edges = edge_rows(last, head)
    both_grads = lax.all_gather(jnp.stack([grad_one, grad_two]), "wide", axis=1, tiled=True)
    back_parts = convolve_back(spot, grad_one, edges, kernel_one, row_count, col_count)
    if has_slots():
        block_pair += [*close, flipped(after(block_pairs[2], back_parts[0]), "wide", 6)]
    attn_in_grad, self_grad, cross_grad = local_kernel(
        weight_out_body,
        [f32_like(4, C // lax.axis_size("wide"), width_own)]
        + [f32_like(width_own, C // lax.axis_size("wide"))] * 2,
        [spot, after(weight_sums, back_parts[0])],
        [],
        16,
        0,
    )
    back_parts = sent_parts(back_parts)
    film_rows = after(film_rows, back_parts[1])
    time_grad, text_grad, kv_grad = local_kernel(
        text_out_body,
        [
            f32_like(time_rows, 2, width_own),
            f32_like(text_rows, 2, width_own),
            f32_like(2, text_rows, width_own),
        ],
        [spot, film_rows, own_features, own_pooled, own_text[0], *far([text_sums])],
        [],
        24,
        4 * TEXT * text_rows * width_own,
    )
    back_parts[0], attn_in_grad, time_grad = lax.optimization_barrier(
        (back_parts[0], attn_in_grad, time_grad)
    )
    back, rows = local_kernel(
        functools.partial(first_back_body, groups, pixel_count),
        [f32_like(*flat), f32_like(2, width_own)],
        [spot, *back_parts, own_pixels, first_sums, affine[0]],
        [],
        16,
        0,
    )
    row_parts = part_totals(rows)
    if has_slots():
        conv_grad = kernel_grad(spot, block_pair, both_grads, col_count)
    else:
        conv_grad = jnp.stack(
            [
                kernel_grad_whole(both_sends[0][:, k], both_grads[k], row_count, col_count)
                for k in range(2)
            ]
        )
    pixels_grad, gain_grad, bias_grad = local_kernel(
        functools.partial(first_input_body, pixel_count),
        [f32_like(*flat), row_pair, row_pair],
        [spot, back, own_pixels, first_sums, affine[0], grad_middle, second_rows, *row_parts],
        [],
        16,
        0,
    )
    return (
        result.reshape(own_shape),
        pixels_grad.reshape(own_shape),
        conv_grad,
        time_grad,
        text_grad,
        gain_grad,
        bias_grad,
        second_rows[3],
        second_rows[4],
        attn_in_grad,
        kv_grad,
        self_grad,
        cross_grad,
    )


def solution(mesh):
    placed = (
        P(None, "wide", None, "tensor"),
        P(),
        P(),
        P(),
        P(None, None, "wide", "tensor"),
        P("wide", None, "tensor"),
        P("wide", None, "tensor"),
        P(None, "tensor"),
        P(None, "tensor"),
        P("tensor"),
        P("tensor"),
        P(None, "wide", "tensor"),
        P(None, "wide", "tensor"),
        P("tensor", "wide"),
        P("tensor", "wide"),
        P(None, "wide", None, "tensor"),
    )
    return jax.shard_map(
        shards,
        mesh=mesh,
        in_specs=placed,
        out_specs=(
            P(None, "wide", None, "tensor"),
            P(None, "wide", None, "tensor"),
            P(None, None, "wide", "tensor"),
            P("wide", None, "tensor"),
            P("wide", None, "tensor"),
            P(None, "tensor"),
            P(None, "tensor"),
            P("tensor"),
            P("tensor"),
            P(None, "wide", "tensor"),
            P(None, "wide", "tensor"),
            P("tensor", "wide"),
            P("tensor", "wide"),
        ),
        check_vma=False,
    )
```

```python
import functools
import math

import jax
import jax.numpy as jnp
from jax import lax
from jax.experimental import pallas as pl
from jax.experimental.pallas import tpu as pltpu
from jax.sharding import PartitionSpec as P

C = 1024
GROUPS = 32
HEAD_DIM = 128
TEXT = 128
TEMB = 1024
MIB = 1 << 20
in_vmem = pl.BlockSpec(memory_space=pltpu.VMEM)
in_smem = pl.BlockSpec(memory_space=pltpu.SMEM)


def local_kernel(body, outs, operands, scratch, limit, flops, aliases=None, out_specs=None):
    size = sum(a.size * a.dtype.itemsize for a in operands)
    size += sum(math.prod(o.shape) * o.dtype.itemsize for o in outs)
    return pl.pallas_call(
        body,
        grid=(1,),
        out_shape=outs,
        in_specs=[in_smem] + [in_vmem] * (len(operands) - 1),
        out_specs=[in_vmem] * len(outs) if out_specs is None else out_specs,
        scratch_shapes=scratch,
        input_output_aliases={} if aliases is None else aliases,
        compiler_params=pltpu.CompilerParams(vmem_limit_bytes=limit * MIB),
        cost_estimate=pl.CostEstimate(flops=flops, bytes_accessed=size, transcendentals=0),
        name=getattr(body, "func", body).__name__,
    )(*operands)


def far(arrays):
    return [pltpu.with_memory_space_constraint(array, pltpu.HBM) for array in arrays]


def turned(values, width):
    rows = values.shape[0]
    wide = values.astype(jnp.float32)
    column = lax.rem(lax.broadcasted_iota(jnp.int32, values.shape, 0), width)
    before = jnp.where(column == 0, 0.0, pltpu.roll(wide, 1, 0))
    after = jnp.where(column == width - 1, 0.0, pltpu.roll(wide, rows - 1, 0))
    return before.astype(jnp.bfloat16), values, after.astype(jnp.bfloat16)


def halves_swapped(values, odd):
    half = values.shape[1] // 2
    other = jnp.concatenate([values[:, half:], values[:, :half]], axis=1)
    return jnp.where(odd, other, values)


class Weights:
    def __init__(self, refs, spot, groups):
        self.refs = refs
        self.paired = len(refs) > 1
        self.groups = groups
        self.spot = spot
        self.odd = lax.rem(spot[0], 2) == 1

    def block(self, chunk):
        return lax.bitwise_xor(lax.div(self.spot[0], 2) if self.paired else self.spot[1], chunk)

    def tap(self, chunk, position):
        if not self.paired:
            each = self.refs[0].shape[0] // self.groups
            start = self.block(chunk) * each
            parts = [self.refs[0][start + i, position] for i in range(each)]
            return jnp.concatenate(parts, axis=0)
        parts = [self.refs[chunk][position], self.refs[4 + chunk][position]]
        return jnp.concatenate(parts, axis=0)

    def ordered(self, values):
        return halves_swapped(values, self.odd) if self.paired else values


def conv_body(groups, parts, count, rows, width, spot, *refs):
    pieces = refs[:groups]
    near, far_row = refs[groups : groups + 2]
    weights = Weights(refs[groups + 2 : groups + 2 + parts], spot, groups)
    source, *rest = refs[groups + 2 + parts :]
    earlier, rest = rest[:count], rest[count:]
    first_out, second_out, *sends, frame = rest
    for send, held in zip(sends, earlier):
        send[:, 0] = held[...]
    if earlier:
        sends = [send.at[:, 1] for send in sends]
    span = pieces[0].shape[1]
    for mask in range(groups):
        block = lax.bitwise_xor(spot[1], mask)
        own = pieces[mask][...]
        lanes = slice(mask * span, (mask + 1) * span)
        framed = framed_rows(near[:, lanes], far_row[:, lanes], own, weights.odd)
        for column, values in enumerate(turned(weights.ordered(framed), width)):
            frame[block, column] = values
    total_sum = jnp.zeros(first_out.shape, jnp.float32)
    for chunk in range(groups):
        block = weights.block(chunk)
        for position in range(9):
            start = (position // 3) * width
            window = frame[block, position % 3, start : start + rows * width, :]
            total_sum += jnp.dot(
                window, weights.tap(chunk, position), preferred_element_type=jnp.float32
            )
        if len(sends) == 1:
            sends[0][chunk] = frame[chunk, 1, width : (rows + 1) * width, :]
        else:
            near = lax.bitwise_xor(lax.div(spot[0], 2), chunk)
            center = frame[near, 1, width : (rows + 1) * width, :]
            center = center if weights.paired else halves_swapped(center, weights.odd)
            sends[0][chunk] = center[:, : span // 2]
            sends[1][chunk] = center[:, span // 2 :]
    if second_out.shape[0] == 2:
        first_out[...] = total_sum
        second_out[...] = channel_sums(total_sum)
    else:
        middle = (source[...].astype(jnp.float32) + total_sum) * root_half
        first_out[...] = middle
        second_out[...] = middle.astype(jnp.bfloat16)


def back_body(groups, rows, width, spot, grad, near, far_row, *refs):
    frame, held = refs[-2:]
    outs = refs[-2 - groups : -2]
    weights = Weights(refs[: -2 - groups], spot, groups)
    framed = framed_rows(near[...], far_row[...], grad[...], weights.odd)
    for column, values in enumerate(turned(framed, width)):
        frame[column] = values
    for chunk in range(groups):
        total_sum = jnp.zeros(held.shape[1:], jnp.float32)
        for position in range(9):
            start = (2 - position // 3) * width
            total_sum += lax.dot_general(
                frame[2 - position % 3, start : start + rows * width, :],
                weights.tap(chunk, position),
                (((1,), (1,)), ((), ())),
                preferred_element_type=jnp.float32,
            )
        held[weights.block(chunk)] = weights.ordered(total_sum).astype(jnp.bfloat16)
    for mask in range(groups):
        outs[mask][...] = held[lax.bitwise_xor(spot[1], mask)]


def bf16_like(*shape):
    return jax.ShapeDtypeStruct(shape, jnp.bfloat16)


def far_like(shape):
    return pltpu.HBM(shape.shape, shape.dtype)


def f32_like(*shape):
    return jax.ShapeDtypeStruct(shape, jnp.float32)


def flipped(values, axis, mask):
    count = lax.axis_size(axis)
    return lax.ppermute(values, axis, [(i, i ^ mask) for i in range(count)])


def relayed_block(over_x, over_y):
    odd = lax.rem(lax.axis_index("wide"), 2) == 1
    far_pairs = [(i, i ^ (2 if i % 2 else 4)) for i in range(8)]
    return lax.ppermute(jnp.where(odd, over_y, over_x), "wide", far_pairs)


def over_chips(values):
    over_x, over_y = flipped(values, "wide", 2), flipped(values, "wide", 4)
    return [values, over_x, over_y, relayed_block(over_x, over_y)]


def has_slots():
    return lax.axis_size("wide") == 8


def after(value, *others):
    return lax.optimization_barrier((value, others))[0]


def gathered_blocks(blocks):
    return [lax.all_gather(blocks, "wide")]


def spread_chips(values):
    if has_slots():
        return over_chips(values)
    mask = 2
    while mask < lax.axis_size("wide"):
        values = jnp.concatenate([values, flipped(values, "wide", mask)])
        mask *= 2
    return [values]


def gathered_sums(parts):
    if has_slots():
        return [parts[0]] + [flipped(parts[k], "wide", 2 * k) for k in range(1, 4)]
    values = parts[0]
    mask = lax.axis_size("wide") // 2
    while mask > 1:
        half = values.shape[0] // 2
        values = values[:half] + flipped(values[half:], "wide", mask)
        mask //= 2
    return [values]


def channel_pieces(values):
    count = lax.axis_size("tensor")
    return [values] + [flipped(values, "tensor", mask) for mask in range(1, count)]


def edge_rows(near, far_row):
    count = lax.axis_size("wide")
    beyond = [(i, i + 1) for i in range(1, count - 1, 2)]
    beyond += [(i + 1, i) for i in range(1, count - 1, 2)]
    from_far = lax.ppermute(far_row, "wide", beyond)
    return flipped(after(near, far_row), "wide", 1), from_far


def framed_rows(near, far_row, own, odd):
    top = jnp.where(odd, near, far_row)
    bottom = jnp.where(odd, far_row, near)
    return jnp.concatenate([top, own, bottom], axis=0)


def convolve(spot, pieces, edges, kernel, source, second_shape, earlier, rows, width):
    groups, (area, span) = len(pieces), pieces[0].shape
    count, block = (2, span // 2) if has_slots() else (1, span)
    layers = (2,) if earlier else ()
    sends = [bf16_like(groups, *layers, area, block)] * count
    return local_kernel(
        functools.partial(conv_body, groups, len(kernel), len(earlier), rows, width),
        [f32_like(area, span), second_shape]
        + [far_like(shape) if earlier else shape for shape in sends],
        [spot, *pieces, *edges, *far(kernel), source, *far(earlier)],
        [pltpu.VMEM((groups, 3, (rows + 2) * width, span), jnp.bfloat16)],
        32,
        2 * 9 * area * C * span,
    )


def piece_edges(pieces, width):
    odd = lax.rem(lax.axis_index("wide"), 2) == 1
    last = jnp.concatenate([piece[-width:] for piece in pieces], axis=1)
    first = jnp.concatenate([piece[:width] for piece in pieces], axis=1)
    return edge_rows(jnp.where(odd, first, last), jnp.where(odd, last, first))


def convolve_back(spot, grad, edges, kernel, rows, width):
    groups, (area, span) = lax.axis_size("tensor"), grad.shape
    return local_kernel(
        functools.partial(back_body, groups, rows, width),
        [bf16_like(area, span)] * groups,
        [spot, grad, *edges, *far(kernel)],
        [
            pltpu.VMEM((3, (rows + 2) * width, span), jnp.bfloat16),
            pltpu.VMEM((groups, area, span), jnp.bfloat16),
        ],
        32,
        2 * 9 * area * C * span,
    )


def sent_parts(parts):
    return [parts[0]] + [flipped(parts[mask], "tensor", mask) for mask in range(1, len(parts))]


def kernel_grad_body(width, spot, kept, got, *refs):
    *pairs, grads, out, turned_all = refs
    layer = pl.program_id(0)
    area, span = kept.shape[2:]
    depth = 8 * area
    turned_all[:, :width] = jnp.zeros((3 * span, width), jnp.bfloat16)
    turned_all[:, depth + width :] = jnp.zeros((3 * span, width), jnp.bfloat16)
    pieces = [kept[0, layer], got[0, layer]]
    pieces += [pair[core, layer] for pair in pairs for core in range(2)]
    lane = lax.broadcasted_iota(jnp.int32, (span, width), 1)
    for mask, piece in enumerate(pieces):
        start = pl.multiple_of(lax.bitwise_xor(spot[0], mask) * area, area)
        flat = jnp.transpose(piece.astype(jnp.float32))
        for row in range(area // width):
            center = flat[:, row * width : (row + 1) * width]
            before = jnp.where(lane == 0, 0.0, pltpu.roll(center, 1, 1))
            behind = jnp.where(lane == width - 1, 0.0, pltpu.roll(center, width - 1, 1))
            lanes = pl.ds(start + (row + 1) * width, width)
            for column, values in enumerate((before, center, behind)):
                turned_all[column * span : (column + 1) * span, lanes] = values.astype(jnp.bfloat16)
    for row in range(3):
        product = dot(turned_all[:, row * width : row * width + depth], grads[0])
        for column in range(3):
            out[0, 3 * row + column] = product[column * span : (column + 1) * span, :]


def kernel_grad(spot, pieces, grads, width):
    span = pieces[0].shape[3]
    depth, columns = grads.shape[1:]
    return pl.pallas_call(
        functools.partial(kernel_grad_body, width),
        out_shape=f32_like(2, 9, span, columns),
        grid=(2,),
        in_specs=[in_smem]
        + [in_vmem] * len(pieces)
        + [pl.BlockSpec((1, depth, columns), lambda i: (i, 0, 0))],
        out_specs=pl.BlockSpec((1, 9, span, columns), lambda i: (i, 0, 0, 0)),
        scratch_shapes=[pltpu.VMEM((3 * span, depth + 2 * width), jnp.bfloat16)],
        compiler_params=pltpu.CompilerParams(vmem_limit_bytes=24 * MIB),
        cost_estimate=pl.CostEstimate(
            flops=4 * 9 * depth * span * columns, bytes_accessed=6 * MIB, transcendentals=0
        ),
        name="kernel_grad_body",
    )(spot, *far(pieces), *far([grads]))


def kernel_grad_whole(send, grads, rows, width):
    natural = jnp.moveaxis(send, 0, 1).reshape(1, rows, width, C)
    swapped = lax.all_to_all(natural, "wide", split_axis=3, concat_axis=1, tiled=True)
    framed = jnp.pad(swapped, ((0, 0), (1, 1), (1, 1), (0, 0)))
    low = grads.reshape(1, -1, width, grads.shape[1])
    return jnp.stack(
        [
            jnp.einsum(
                "mrwc,mrwd->cd",
                framed[:, tap // 3 : tap // 3 + low.shape[1], tap % 3 : tap % 3 + width, :],
                low,
                preferred_element_type=jnp.float32,
            )
            for tap in range(9)
        ]
    )


root_half = 1.0 / math.sqrt(2.0)
highest = lax.Precision.HIGHEST


def sinusoid(steps):
    half_width = TEMB // 2
    frequency = jnp.exp(-math.log(10000.0) * jnp.arange(half_width, dtype=jnp.float32) / half_width)
    angles = steps.astype(jnp.float32)[:, None] * frequency[None, :]
    return jnp.concatenate([jnp.cos(angles), jnp.sin(angles)], axis=1)


def chip_parts(values):
    if has_slots():
        return [values] + [flipped(values, "wide", mask) for mask in (2, 4, 6)]
    mask = 2
    while mask < lax.axis_size("wide"):
        values = values + flipped(values, "wide", mask)
        mask *= 2
    return [values]


def part_totals(rows):
    return chip_parts(rows + flipped(rows, "wide", 1))


def sum_of_parts(refs):
    if len(refs) == 1:
        return refs[0][...]
    return (refs[0][...] + refs[1][...]) + (refs[2][...] + refs[3][...])


def total(values, axis, mask=1):
    while mask < lax.axis_size(axis):
        values = values + flipped(values, axis, mask)
        mask *= 2
    return values


def silu_slope(values):
    logistic = lax.logistic(values)
    return logistic * (1.0 + values * (1.0 - logistic))


def channel_sums(values):
    return jnp.concatenate(
        [
            jnp.sum(values, axis=0, keepdims=True),
            jnp.sum(values * values, axis=0, keepdims=True),
        ],
        axis=0,
    )


def group_means(first, second, pixel_count):
    channels = first.shape[1]
    per_group = C // GROUPS
    row = lax.div(lax.broadcasted_iota(jnp.int32, (channels, channels), 0), per_group)
    column = lax.div(lax.broadcasted_iota(jnp.int32, (channels, channels), 1), per_group)
    same = jnp.where(row == column, 1.0, 0.0)
    rows = jnp.concatenate([first, second, jnp.zeros((6, channels), jnp.float32)], axis=0)
    means = jnp.dot(rows, same, precision=highest, preferred_element_type=jnp.float32)
    means = means / (pixel_count * per_group)
    return means[0:1], means[1:2]


def group_scale(first, second, pixel_count):
    center, square = group_means(first, second, pixel_count)
    return center, lax.rsqrt(square - center * center + 1e-05)


def lifted_sums(sums, film, pixel_count):
    slope, shift = 1.0 + film[0:1], film[1:2]
    plain, square = sums[0:1], sums[1:2]
    return (
        slope * plain + pixel_count * shift,
        slope * slope * square + 2.0 * slope * shift * plain + pixel_count * shift * shift,
    )


def silu_low(values):
    return (values * lax.logistic(values)).astype(jnp.bfloat16)


def first_norm_body(pixel_count, spot, pixels, affine, *refs):
    *parts, out, sums = refs
    sums[...] = sum_of_parts(parts)
    center, inverse = group_scale(sums[0:1], sums[1:2], pixel_count)
    scaled = (pixels[...].astype(jnp.float32) - center) * inverse
    out[...] = silu_low(scaled * affine[0:1] + affine[1:2])


def second_norm_body(pixel_count, spot, inner, affine, *refs):
    *parts, out, film, sums = refs
    summed = sum_of_parts(parts)
    film[...], sums[...] = summed[:2], summed[2:]
    center, inverse = group_scale(*lifted_sums(sums[...], film[...], pixel_count), pixel_count)
    lifted = inner[...] * (1.0 + film[0:1]) + film[1:2]
    out[...] = silu_low((lifted - center) * inverse * affine[0:1] + affine[1:2])


def parts_sum(refs):
    summed = refs[0][...].astype(jnp.float32)
    for ref in refs[1:]:
        summed += ref[...].astype(jnp.float32)
    return summed


def stacked_rows(rows):
    return jnp.concatenate([jnp.sum(row, axis=0, keepdims=True) for row in rows], axis=0)


def second_back_body(groups, pixel_count, spot, *refs):
    inner, sums, film, affine, terms, out, rows = refs[groups:]
    center, inverse = group_scale(*lifted_sums(sums[...], film[...], pixel_count), pixel_count)
    own = inner[...]
    scaled = (own * (1.0 + film[0:1]) + film[1:2] - center) * inverse
    back = parts_sum(refs[:groups]) * silu_slope(scaled * affine[0:1] + affine[1:2])
    out[...] = back
    rows[0:3, :] = stacked_rows([back * scaled, back, back * own])
    rows[3:5, :] = terms[...]
    rows[5:8, :] = jnp.zeros((3, own.shape[1]), jnp.float32)


def second_input_body(pixel_count, width, spot, back, inner, sums, film, affine, *refs):
    *parts, low, near, far_row, film_rows, rows = refs
    rows[...] = sum_of_parts(parts)
    slope, shift, gain = 1.0 + film[0:1], film[1:2], affine[0:1]
    plain_sum, square_sum = sums[0:1], sums[1:2]
    lifted_sum, lifted_square = lifted_sums(sums[...], film[...], pixel_count)
    center, inverse = group_scale(lifted_sum, lifted_square, pixel_count)
    dotted, plain = group_means(gain * rows[0:1], gain * rows[1:2], pixel_count)
    scaled = (inner[...] * slope + shift - center) * inverse
    grad = inverse * (back[...] * gain - plain - scaled * dotted)
    grad_low = (grad * slope).astype(jnp.bfloat16)
    low[...] = grad_low
    odd = lax.rem(spot[0], 2) == 1
    near[...] = jnp.where(odd, grad_low[:width], grad_low[-width:])
    far_row[...] = jnp.where(odd, grad_low[-width:], grad_low[:width])
    scaled_sum = inverse * (lifted_sum - pixel_count * center)
    scaled_inner = inverse * (slope * square_sum + (shift - center) * plain_sum)
    film_rows[0:1, :] = inverse * (
        gain * rows[2:3] - plain * plain_sum - dotted * scaled_inner
    )
    film_rows[1:2, :] = inverse * (
        gain * rows[1:2] - pixel_count * plain - dotted * scaled_sum
    )


def first_back_body(groups, pixel_count, spot, *refs):
    pixels, sums, affine, out, rows = refs[groups:]
    center, inverse = group_scale(sums[0:1], sums[1:2], pixel_count)
    scaled = (pixels[...].astype(jnp.float32) - center) * inverse
    back = parts_sum(refs[:groups]) * silu_slope(scaled * affine[0:1] + affine[1:2])
    out[...] = back
    rows[...] = stacked_rows([back * scaled, back])


def first_input_body(pixel_count, spot, back, pixels, sums, affine, middle, second, *refs):
    *parts, out, gains, biases = refs
    rows = sum_of_parts(parts)
    gains[...] = jnp.concatenate([rows[0:1], second[0:1]], axis=0)
    biases[...] = jnp.concatenate([rows[1:2], second[1:2]], axis=0)
    gain = affine[0:1]
    center, inverse = group_scale(sums[0:1], sums[1:2], pixel_count)
    dotted, plain = group_means(gain * rows[0:1], gain * rows[1:2], pixel_count)
    scaled = (pixels[...].astype(jnp.float32) - center) * inverse
    out[...] = inverse * (back[...] * gain - plain - scaled * dotted) + middle[...] * root_half


def dot(left, right):
    return jnp.dot(left, right, preferred_element_type=jnp.float32)


def dot_last(left, right):
    return lax.dot_general(
        left, right, (((1,), (1,)), ((), ())), preferred_element_type=jnp.float32
    )


def flat_turn(values):
    return jnp.transpose(values.astype(jnp.float32)).astype(jnp.bfloat16)


def dot_first(left, right):
    return dot(flat_turn(left), right)


def head_choice(values, odd):
    first, second = values[:, :HEAD_DIM], values[:, HEAD_DIM:]
    return jnp.where(odd, second, first), jnp.where(odd, first, second)


def heads_joined(kept, received, odd):
    return jnp.where(
        odd,
        jnp.concatenate([received, kept], axis=1),
        jnp.concatenate([kept, received], axis=1),
    )


def packed_rows(values):
    rows = []
    for _ in range(3):
        rows.append(values.astype(jnp.bfloat16).astype(jnp.float32))
        values = values - rows[-1]
    rows.append(jnp.zeros((10, values.shape[1]), jnp.float32))
    return jnp.concatenate(rows, axis=0).astype(jnp.bfloat16)


def unpacked_rows(packed, area):
    rows = packed[area:, :].astype(jnp.float32)
    return rows[0:1] + rows[2:3] + rows[4:5], rows[1:2] + rows[3:4] + rows[5:6]


def prepare_body(spot, pixels, cotangent, gain, bias, pack, sums):
    area = cotangent.shape[0]
    pack[:area] = cotangent[...].astype(jnp.bfloat16)
    pack[area:] = packed_rows(jnp.concatenate([gain[...], bias[...]], axis=0))
    sums[...] = channel_sums(pixels[...].astype(jnp.float32))


def project_body(groups, spot, *refs):
    pieces, packs = refs[:groups], refs[groups : 2 * groups]
    own, maps, keep_query, keep, send, *rest = refs[2 * groups :]
    cross, normed, scaled, center, inverse = rest
    weights = Weights([maps], spot, groups)
    odd = lax.rem(spot[0], 2) == 1
    area = own.shape[0]
    token_sum = token_square = 0.0
    for piece in pieces:
        values = piece[...].astype(jnp.float32)
        token_sum += jnp.sum(values, axis=1, keepdims=True)
        token_square += jnp.sum(values * values, axis=1, keepdims=True)
    mean = token_sum / C
    scale = lax.rsqrt(token_square / C - mean * mean + 1e-05)
    lows = []
    for mask in range(groups):
        gain, bias = unpacked_rows(packs[mask], area)
        values = (pieces[mask][...].astype(jnp.float32) - mean) * scale
        lows.append((values * gain + bias).astype(jnp.bfloat16))
        normed[lax.bitwise_xor(spot[1], mask)] = lows[-1]
    center[...] = mean
    inverse[...] = scale
    scaled[...] = (own[...] - mean) * scale
    projected = []
    for position in range(4):
        total_sum = 0.0
        for mask in range(groups):
            total_sum += dot(lows[mask], weights.tap(mask, position))
        projected.append(total_sum.astype(jnp.bfloat16))
    cross[...] = projected[3]
    chosen = [head_choice(values, odd) for values in projected[:3]]
    chosen = chosen[1:] + chosen[:1]
    keep_query[...] = chosen[2][0]
    keep[...] = jnp.concatenate([pair[0] for pair in chosen[:2]], axis=1)
    send[...] = jnp.concatenate([pair[1] for pair in chosen], axis=1)


def out_grad_body(groups, spot, *refs):
    packs = refs[:groups]
    maps, keep, send, cross = refs[groups:]
    weights = Weights([maps], spot, groups)
    sums = []
    for position in (4, 5):
        total_sum = 0.0
        for mask in range(groups):
            total_sum += dot(packs[mask][: cross.shape[0]], weights.tap(mask, position))
        sums.append(total_sum.astype(jnp.bfloat16))
    kept, sent = head_choice(sums[0], lax.rem(spot[0], 2) == 1)
    keep[...] = kept
    send[...] = sent
    cross[...] = sums[1]


def text_out_body(spot, film, features, pooled, text, parts, time_grad, text_grad, kv_grad):
    for rows, out in ((features, time_grad), (pooled, text_grad)):
        column = jnp.transpose(jnp.broadcast_to(rows[...].astype(jnp.float32), (8, rows.shape[1])))
        for part in range(2):
            out[:, part, :] = column[:, 0:1] * film[part : part + 1, :]
    summed = leading_sum(parts)
    turned_text = flat_turn(text[...])
    for part in range(2):
        high = summed[part].astype(jnp.bfloat16)
        low = (summed[part] - high.astype(jnp.float32)).astype(jnp.bfloat16)
        kv_grad[part] = dot(turned_text, high) + dot(turned_text, low)


def mix_body(groups, spot, kept, other, crossed, maps, *outs):
    weights = Weights([maps], spot, groups)
    attended = heads_joined(kept[...], other[:, :HEAD_DIM], lax.rem(spot[0], 2) == 1)
    for mask in range(groups):
        total_sum = dot_last(attended, weights.tap(mask, 4))
        total_sum += dot_last(crossed[...], weights.tap(mask, 5))
        outs[mask][...] = total_sum.astype(jnp.bfloat16)


def over_rows(refs, step, state):
    for index, ref in enumerate(refs):
        rows = ref.shape[0]
        if rows <= 512:
            state = step(state, ref[...], index, 0)
        else:
            state = lax.fori_loop(
                0,
                rows // 512,
                lambda i, held: step(
                    held, ref[pl.ds(pl.multiple_of(i * 512, 512), 512), :], index, i * 512
                ),
                state,
            )
    return state


score_scale = HEAD_DIM ** (-0.5)


def cross_body(spot, query, grad, parts, *refs):
    *blocks, crossed, grad_query, text_grad = refs
    if blocks:
        kept_block, got_block, *pairs = blocks
        for index, pair in enumerate(pairs):
            pair[0] = kept_block[index + 1]
            pair[1] = got_block[index + 1]
    text = leading_sum(parts).astype(jnp.bfloat16)
    live = lax.broadcasted_iota(jnp.int32, (query.shape[0], text.shape[1]), 1) < spot[2]
    for head in range(query.shape[1] // HEAD_DIM):
        lanes = slice(head * HEAD_DIM, (head + 1) * HEAD_DIM)
        own, keys, values, back = query[:, lanes], text[0, :, lanes], text[1, :, lanes], grad[:, lanes]
        scores = jnp.where(live, dot_last(own, keys) * score_scale, -1e30)
        weights = jnp.exp(scores - jnp.max(scores, axis=1, keepdims=True))
        probs = weights / jnp.sum(weights, axis=1, keepdims=True)
        low = probs.astype(jnp.bfloat16)
        crossed[:, lanes] = dot(low, values).astype(jnp.bfloat16)
        grad_probs = dot_last(back, values)
        grad_scores = probs * (grad_probs - jnp.sum(probs * grad_probs, axis=1, keepdims=True))
        grad_low = grad_scores.astype(jnp.bfloat16)
        grad_query[:, lanes] = (dot(grad_low, keys) * score_scale).astype(jnp.bfloat16)
        text_grad[0, :, lanes] = (dot_first(grad_low, own) * score_scale).astype(jnp.bfloat16)
        text_grad[1, :, lanes] = dot_first(low, back).astype(jnp.bfloat16)


def attend_body(count, extra, halves, spot, kept_query, got, kept_grad, got_grad, *refs):
    blocks, refs = refs[:count], refs[count:]
    cross_in, refs = refs[: 3 + extra], refs[3 + extra :]
    parts, refs = refs[: count * halves], refs[count * halves :]
    keep_out, keep_query, send, *cross_out = refs
    cross_body(spot, *cross_in, *cross_out)
    query = jnp.concatenate([kept_query[...], got[:, 2 * HEAD_DIM :]], axis=0)
    grad = jnp.concatenate([kept_grad[...], got_grad[...]], axis=0)
    queries = query.shape[0]

    def forward(state, block, index, start):
        top, weight_sum, weighted = state
        scores = dot_last(block[:, :HEAD_DIM], query) * score_scale
        raised = jnp.maximum(top, jnp.max(scores, axis=0, keepdims=True))
        rescale = jnp.exp(top - raised)
        weights = jnp.exp(scores - raised)
        weight_sum = weight_sum * rescale + jnp.sum(weights, axis=0, keepdims=True)
        values = block[:, HEAD_DIM : 2 * HEAD_DIM]
        weighted = weighted * rescale + dot_first(values, weights.astype(jnp.bfloat16))
        return raised, weight_sum, weighted

    top, weight_sum, weighted = over_rows(
        blocks,
        forward,
        (
            jnp.full((1, queries), -1e30, jnp.float32),
            jnp.zeros((1, queries), jnp.float32),
            jnp.zeros((HEAD_DIM, queries), jnp.float32),
        ),
    )
    attended = weighted / weight_sum
    delta = jnp.sum(attended * jnp.transpose(grad.astype(jnp.float32)), axis=0, keepdims=True)
    log_sum = top + jnp.log(weight_sum)

    def backward(state, block, index, start):
        keys, values = block[:, :HEAD_DIM], block[:, HEAD_DIM : 2 * HEAD_DIM]
        probs = jnp.exp(dot_last(keys, query) * score_scale - log_sum)
        grad_values = dot(probs.astype(jnp.bfloat16), grad)
        grad_scores = (probs * (dot_last(values, grad) - delta)).astype(jnp.bfloat16)
        grad_keys = dot(grad_scores, query) * score_scale
        both = jnp.concatenate([grad_keys, grad_values], axis=1).astype(jnp.bfloat16)
        rows = block.shape[0] // halves
        first = start if isinstance(start, int) else pl.multiple_of(start, 512)
        for half in range(halves):
            parts[halves * index + half][pl.ds(first, rows), :] = both[half * rows : (half + 1) * rows]
        return state + dot_first(keys, grad_scores)

    flat = over_rows(blocks, backward, jnp.zeros((HEAD_DIM, queries), jnp.float32))
    for index, (values, keep) in enumerate(((attended, keep_out), (flat * score_scale, keep_query))):
        turned_back = jnp.transpose(values).astype(jnp.bfloat16)
        keep[...] = turned_back[: queries // 2]
        send[:, index * HEAD_DIM : (index + 1) * HEAD_DIM] = turned_back[queries // 2 :]


def leading_sum(ref):
    summed = ref[0].astype(jnp.float32)
    for index in range(1, ref.shape[0]):
        summed += ref[index].astype(jnp.float32)
    return summed


def joined_grads(spot, kept_query, got, cross, kept_pairs, got_pairs):
    odd = lax.rem(spot[0], 2) == 1
    own, other = [parts_sum(pairs).astype(jnp.bfloat16) for pairs in (kept_pairs, got_pairs)]
    return [
        heads_joined(kept_query[...], got[:, HEAD_DIM:], odd),
        heads_joined(own[:, :HEAD_DIM], other[:, :HEAD_DIM], odd),
        heads_joined(own[:, HEAD_DIM:], other[:, HEAD_DIM:], odd),
        cross[...],
    ]


def project_back_body(groups, count, spot, kq, got, cross, center, inverse, kept, *refs):
    crossed, normed, maps, *refs = refs
    kept_pairs, got_pairs, refs = refs[:count], refs[count : 2 * count], refs[2 * count :]
    pieces, packs = refs[:groups], refs[groups : 2 * groups]
    *outs, out, frame = refs[2 * groups :]
    odd = lax.rem(spot[0], 2) == 1
    weights = Weights([maps], spot, groups)
    grads = joined_grads(spot, kq, got, cross, kept_pairs, got_pairs)
    area, span = cross.shape
    plain = dotted = 0.0
    for mask in range(groups):
        part = 0.0
        for position in range(4):
            part += dot_last(grads[position], weights.tap(mask, position))
        outs[mask][:area] = part.astype(jnp.bfloat16)
        eased = part * unpacked_rows(packs[mask], area)[0]
        unit = (pieces[mask][...].astype(jnp.float32) - center[...]) * inverse[...]
        plain += eased
        dotted += eased * unit
    ones = jnp.ones((8, plain.shape[1]), jnp.float32)
    sums = [
        lax.dot_general(
            ones,
            values,
            (((1,), (1,)), ((), ())),
            precision=highest,
            preferred_element_type=jnp.float32,
        )[0:1]
        for values in (plain, dotted)
    ]
    packed = packed_rows(jnp.concatenate(sums, axis=0))
    for part in outs:
        part[area:] = packed
    right = jnp.concatenate(grads, axis=1)
    attended = heads_joined(kept[...], got[:, :HEAD_DIM], odd)
    out_right = jnp.concatenate([attended, crossed[...]], axis=1)
    for mask in range(groups):
        frame[lax.bitwise_xor(spot[1], mask)] = packs[mask][:area]
    for chunk in range(groups):
        rows = slice(chunk * span, (chunk + 1) * span)
        out[rows, : 4 * span] = dot_first(normed[chunk], right).astype(jnp.bfloat16)
        out[rows, 4 * span :] = dot_first(frame[chunk], out_right).astype(jnp.bfloat16)


def weight_out_body(spot, sums, in_grad, self_grad, cross_grad):
    summed = sums[...].astype(jnp.float32)
    span = in_grad.shape[2]
    for position in range(4):
        in_grad[position] = summed[:, position * span : (position + 1) * span]
    self_grad[...] = jnp.transpose(summed[:, 4 * span : 5 * span])
    cross_grad[...] = jnp.transpose(summed[:, 5 * span :])


def norm_back_body(groups, width, spot, *refs):
    scaled, inverse, cotangent, gain, middle, low, near, far_row, terms = refs[groups:]
    area = scaled.shape[0]
    grad = plain = dotted = 0.0
    for ref in refs[:groups]:
        grad += ref[:area].astype(jnp.float32)
        sums = unpacked_rows(ref, area)
        plain, dotted = plain + sums[0], dotted + sums[1]
    same = lax.broadcasted_iota(jnp.int32, (area, area), 0) == lax.broadcasted_iota(
        jnp.int32, (area, area), 1
    )
    plain = jnp.sum(jnp.where(same, plain, 0.0), axis=1, keepdims=True) / C
    dotted = jnp.sum(jnp.where(same, dotted, 0.0), axis=1, keepdims=True) / C
    unit = scaled[...]
    terms[0:1, :] = jnp.sum(grad * unit, axis=0, keepdims=True)
    terms[1:2, :] = jnp.sum(grad, axis=0, keepdims=True)
    back = inverse[...] * (grad * gain[...] - plain - unit * dotted) + cotangent[...]
    middle[...] = back
    grad_low = (back * root_half).astype(jnp.bfloat16)
    low[...] = grad_low
    odd = lax.rem(spot[0], 2) == 1
    near[...] = jnp.where(odd, grad_low[:width], grad_low[-width:])
    far_row[...] = jnp.where(odd, grad_low[-width:], grad_low[:width])


def shards(
    pixels,
    text_states,
    text_length,
    timestep,
    conv_weights,
    film_time,
    film_text,
    group_gain,
    group_bias,
    layer_gain,
    layer_bias,
    attn_in,
    text_kv,
    out_self,
    out_cross,
    cotangent,
):
    map_count, row_count, col_count, width_own = pixels.shape
    token_count = row_count * col_count
    groups = lax.axis_size("tensor")
    pixel_count = token_count * lax.axis_size("wide")
    own_shape = (map_count, row_count, col_count, width_own)
    flat = (token_count, width_own)
    half = (token_count, HEAD_DIM)
    square = 2 * token_count * C * width_own
    edge = (col_count, width_own)
    spot = jnp.stack([lax.axis_index("wide"), lax.axis_index("tensor"), text_length[0]])
    spot = spot.astype(jnp.int32)
    own_pixels = pixels.reshape(flat)
    flat_cotangent = cotangent.reshape(flat)
    affine = [jnp.stack([group_gain[layer], group_bias[layer]]) for layer in range(2)]

    pack, sums = local_kernel(
        prepare_body,
        [bf16_like(token_count + 16, width_own), f32_like(2, width_own)],
        [spot, *far([own_pixels, flat_cotangent, layer_gain[None], layer_bias[None]])],
        [],
        8,
        0,
    )
    first_parts = part_totals(sums)
    kernel_one = gathered_blocks(conv_weights[0])
    features = sinusoid(timestep).astype(jnp.bfloat16)
    present = jnp.arange(TEXT)[None, :] < text_length[:, None]
    pooled = jnp.einsum(
        "mtx,mt->mx", text_states, present.astype(jnp.bfloat16), preferred_element_type=jnp.float32
    )
    pooled = (pooled / text_length.astype(jnp.float32)[:, None]).astype(jnp.bfloat16)
    wide_index = lax.axis_index("wide")
    time_rows = film_time.shape[0]
    text_rows = film_text.shape[0]
    own_features = lax.dynamic_slice_in_dim(features, wide_index * time_rows, time_rows, 1)
    own_pooled = lax.dynamic_slice_in_dim(pooled, wide_index * text_rows, text_rows, 1)
    own_text = lax.dynamic_slice_in_dim(text_states, wide_index * text_rows, text_rows, 2)
    film_term = jnp.einsum(
        "mk,ksc->msc", own_features, film_time, preferred_element_type=jnp.float32
    ) + jnp.einsum("mk,ksc->msc", own_pooled, film_text, preferred_element_type=jnp.float32)
    text_term = jnp.einsum("mtx,pxd->pmtd", own_text, text_kv, preferred_element_type=jnp.float32)
    text_term = text_term.astype(jnp.bfloat16).reshape(2, TEXT, width_own)

    row_pair = f32_like(2, width_own)
    first, first_sums = local_kernel(
        functools.partial(first_norm_body, pixel_count),
        [bf16_like(*flat), row_pair],
        [spot, own_pixels, affine[0], *first_parts],
        [],
        8,
        0,
    )
    maps = jnp.concatenate(
        [after(attn_in, first), jnp.transpose(after(jnp.stack([out_self, out_cross]), first), (0, 2, 1))], axis=0
    )
    maps = gathered_blocks(maps)[0]
    packs = channel_pieces(pack)
    pieces = channel_pieces(after(first, packs))
    edges = piece_edges(pieces, col_count)
    later = after(conv_weights, first)[1]
    if has_slots():
        kernel_two = over_chips(later)
        last = after(kernel_two[3], *edges)
        kernel_two += [flipped(part, "wide", 1) for part in [*kernel_two[:3], last]]
    else:
        kernel_two = gathered_blocks(later)
    pieces[0] = after(pieces[0], film_term, text_term)
    inner, sums, *first_sends = convolve(
        spot, pieces, edges, kernel_one, own_pixels, row_pair, [], row_count, col_count
    )
    sums = after(sums, kernel_two)
    inner_parts = part_totals(jnp.concatenate([film_term[0], sums]))
    second, film, inner_sums = local_kernel(
        functools.partial(second_norm_body, pixel_count),
        [bf16_like(*flat), row_pair, row_pair],
        [spot, inner, affine[1], *inner_parts],
        [],
        8,
        0,
    )
    text_all = lax.all_gather(after(text_term, second), "wide")
    pieces = channel_pieces(second)
    edges = piece_edges(pieces, col_count)
    middle, middle_low, *both_sends = convolve(
        spot,
        pieces,
        edges,
        kernel_two,
        own_pixels,
        bf16_like(*flat),
        first_sends,
        row_count,
        col_count,
    )

    middle_pieces = channel_pieces(middle_low)
    block_pair = [both_sends[0], flipped(both_sends[1], "wide", 1)] if has_slots() else []
    kept_grad, sent_grad, grad_crossed = local_kernel(
        functools.partial(out_grad_body, groups),
        [far_like(bf16_like(*half)), bf16_like(*half), far_like(bf16_like(*flat))],
        [spot, *far([after(packs[0], middle_low)] + packs[1:]), *far([maps])],
        [],
        16,
        2 * square,
    )
    got_grad = flipped(sent_grad, "wide", 1)
    middle_pieces[0] = after(middle_pieces[0], got_grad, block_pair)
    column = f32_like(token_count, 1)
    triple = bf16_like(token_count, 3 * HEAD_DIM)
    kept_query, kept_pair, sent, *outs = local_kernel(
        functools.partial(project_body, groups),
        [
            bf16_like(*half),
            bf16_like(*flat),
            triple,
            bf16_like(*flat),
            far_like(bf16_like(groups, *flat)),
            far_like(f32_like(*flat)),
            far_like(column),
            far_like(column),
        ],
        [spot, *middle_pieces, *far(packs), middle, *far([maps])],
        [],
        24,
        4 * square,
    )
    cross_query, normed, scaled, center, inverse = outs
    got = flipped(sent, "wide", 1)
    blocks = spread_chips(jnp.concatenate([kept_pair, got[:, : 2 * HEAD_DIM]]))
    pair_shapes = [bf16_like(2, *block.shape[1:]) for block in block_pair[:1] * 3]
    halves = 2 if has_slots() else 1
    attend_shapes = [bf16_like(block.shape[0] // halves, 2 * HEAD_DIM) for block in blocks * halves]
    attend_shapes += [bf16_like(*half), bf16_like(*half), bf16_like(*flat)]
    cross_shapes = [bf16_like(*flat), bf16_like(*flat), bf16_like(2, TEXT, width_own)]
    outs = local_kernel(
        functools.partial(attend_body, len(blocks), len(block_pair), halves),
        [far_like(shape) for shape in attend_shapes + pair_shapes + cross_shapes],
        [
            spot,
            kept_query,
            got,
            *far([kept_grad, got_grad]),
            *blocks,
            cross_query,
            *far([grad_crossed, text_all]),
            *far(block_pair),
        ],
        [],
        48,
        14 * (2 * token_count) * HEAD_DIM * pixel_count,
    )
    key_parts, outs = outs[: len(blocks) * halves], outs[len(blocks) * halves :]
    kept_out, kept_dq, sent_both, *block_pairs = outs
    *block_pairs, crossed, grad_cross_query, text_grads = block_pairs
    text_sums = lax.all_gather(text_grads, "wide")
    if has_slots():
        key_parts = [key_parts[0]] + [flipped(key_parts[mask], "wide", mask) for mask in range(1, 8)]
        kept_pairs, got_pairs = key_parts[0::2], key_parts[1::2]
        kept_pairs[0] = far(kept_pairs[:1])[0]
    else:
        (summed,) = gathered_sums(key_parts)
        kept_pairs = [summed[:token_count]]
        got_pairs = [flipped(summed[token_count:], "wide", 1)]
    got_both = flipped(sent_both, "wide", 1)
    *norm_parts, weight_parts = local_kernel(
        functools.partial(project_back_body, groups, len(kept_pairs)),
        [bf16_like(token_count + 16, width_own)] * groups + [far_like(bf16_like(C, 6 * width_own))],
        [
            spot,
            *far([kept_dq]),
            got_both,
            *far([grad_cross_query, center, inverse, kept_out, crossed, normed, maps]),
            *kept_pairs,
            *got_pairs,
            *far(middle_pieces),
            *far(packs),
        ],
        [pltpu.VMEM((groups, *flat), jnp.bfloat16)],
        32,
        10 * square,
    )
    weight_sums = lax.psum_scatter(weight_parts, "wide", scatter_dimension=0, tiled=True)
    received = sent_parts(norm_parts)
    if has_slots():
        close = [flipped(after(block_pairs[k], norm_parts[0]), "wide", 2 * k + 2) for k in range(2)]
        received[0] = after(received[0], close)
    grad_middle, grad_two, last, head, terms = local_kernel(
        functools.partial(norm_back_body, groups, col_count),
        [
            f32_like(*flat),
            bf16_like(*flat),
            bf16_like(*edge),
            bf16_like(*edge),
            f32_like(2, width_own),
        ],
        [
            spot,
            *received,
            scaled,
            inverse,
            flat_cotangent,
            layer_gain[None],
        ],
        [],
        16,
        0,
    )

    edges = edge_rows(last, head)
    mixed = local_kernel(
        functools.partial(mix_body, groups),
        [bf16_like(*flat)] * groups,
        [spot, after(kept_out, grad_two), got_both, *far([crossed, maps])],
        [],
        16,
        2 * square,
    )
    back_parts = convolve_back(
        spot, after(grad_two, mixed), edges, kernel_two, row_count, col_count
    )
    mixed = sent_parts([after(part, back_parts[0]) for part in mixed])
    result = middle
    for part in mixed:
        result = result + part.astype(jnp.float32)
    back_parts = sent_parts(back_parts)
    back, rows = local_kernel(
        functools.partial(second_back_body, groups, pixel_count),
        [f32_like(*flat), f32_like(8, width_own)],
        [spot, *back_parts, inner, inner_sums, film, affine[1], terms],
        [],
        16,
        0,
    )
    grad_one, last, head, film_rows, second_rows = local_kernel(
        functools.partial(second_input_body, pixel_count, col_count),
        [bf16_like(*flat), bf16_like(*edge), bf16_like(*edge), row_pair, f32_like(8, width_own)],
        [spot, after(back, mixed), inner, inner_sums, film, affine[1], *part_totals(rows)],
        [],
        16,
        0,
    )
    edges = edge_rows(last, head)
    both_grads = lax.all_gather(jnp.stack([grad_one, grad_two]), "wide", axis=1, tiled=True)
    back_parts = convolve_back(spot, grad_one, edges, kernel_one, row_count, col_count)
    if has_slots():
        block_pair += [*close, flipped(after(block_pairs[2], back_parts[0]), "wide", 6)]
    attn_in_grad, self_grad, cross_grad = local_kernel(
        weight_out_body,
        [f32_like(4, C // lax.axis_size("wide"), width_own)]
        + [f32_like(width_own, C // lax.axis_size("wide"))] * 2,
        [spot, *far([after(weight_sums, back_parts[0])])],
        [],
        16,
        0,
    )
    back_parts = sent_parts(back_parts)
    film_rows = after(film_rows, back_parts[1])
    time_grad, text_grad, kv_grad = local_kernel(
        text_out_body,
        [
            f32_like(time_rows, 2, width_own),
            f32_like(text_rows, 2, width_own),
            f32_like(2, text_rows, width_own),
        ],
        [spot, film_rows, own_features, own_pooled, own_text[0], *far([text_sums])],
        [],
        24,
        4 * TEXT * text_rows * width_own,
    )
    back_parts[0], attn_in_grad, time_grad = lax.optimization_barrier(
        (back_parts[0], attn_in_grad, time_grad)
    )
    back, rows = local_kernel(
        functools.partial(first_back_body, groups, pixel_count),
        [f32_like(*flat), f32_like(2, width_own)],
        [spot, *back_parts, own_pixels, first_sums, affine[0]],
        [],
        16,
        0,
    )
    row_parts = part_totals(rows)
    if has_slots():
        conv_grad = kernel_grad(spot, block_pair, both_grads, col_count)
    else:
        conv_grad = jnp.stack(
            [
                kernel_grad_whole(both_sends[0][:, k], both_grads[k], row_count, col_count)
                for k in range(2)
            ]
        )
    pixels_grad, gain_grad, bias_grad = local_kernel(
        functools.partial(first_input_body, pixel_count),
        [f32_like(*flat), row_pair, row_pair],
        [spot, back, own_pixels, first_sums, affine[0], grad_middle, second_rows, *row_parts],
        [],
        16,
        0,
    )
    return (
        result.reshape(own_shape),
        pixels_grad.reshape(own_shape),
        conv_grad,
        time_grad,
        text_grad,
        gain_grad,
        bias_grad,
        second_rows[3],
        second_rows[4],
        attn_in_grad,
        kv_grad,
        self_grad,
        cross_grad,
    )


def solution(mesh):
    placed = (
        P(None, "wide", None, "tensor"),
        P(),
        P(),
        P(),
        P(None, None, "wide", "tensor"),
        P("wide", None, "tensor"),
        P("wide", None, "tensor"),
        P(None, "tensor"),
        P(None, "tensor"),
        P("tensor"),
        P("tensor"),
        P(None, "wide", "tensor"),
        P(None, "wide", "tensor"),
        P("tensor", "wide"),
        P("tensor", "wide"),
        P(None, "wide", None, "tensor"),
    )
    return jax.shard_map(
        shards,
        mesh=mesh,
        in_specs=placed,
        out_specs=(
            P(None, "wide", None, "tensor"),
            P(None, "wide", None, "tensor"),
            P(None, None, "wide", "tensor"),
            P("wide", None, "tensor"),
            P("wide", None, "tensor"),
            P(None, "tensor"),
            P(None, "tensor"),
            P("tensor"),
            P("tensor"),
            P(None, "wide", "tensor"),
            P(None, "wide", "tensor"),
            P("tensor", "wide"),
            P("tensor", "wide"),
        ),
        check_vma=False,
    )
```

```python
import functools
import math

import jax
import jax.numpy as jnp
from jax import lax
from jax.experimental import pallas as pl
from jax.experimental.pallas import tpu as pltpu
from jax.sharding import PartitionSpec as P

C = 1024
GROUPS = 32
HEAD_DIM = 128
TEXT = 128
TEMB = 1024
MIB = 1 << 20
in_vmem = pl.BlockSpec(memory_space=pltpu.VMEM)
in_smem = pl.BlockSpec(memory_space=pltpu.SMEM)


def local_kernel(body, outs, operands, scratch, limit, flops, aliases=None, out_specs=None):
    size = sum(a.size * a.dtype.itemsize for a in operands)
    size += sum(math.prod(o.shape) * o.dtype.itemsize for o in outs)
    return pl.pallas_call(
        body,
        grid=(1,),
        out_shape=outs,
        in_specs=[in_smem] + [in_vmem] * (len(operands) - 1),
        out_specs=[in_vmem] * len(outs) if out_specs is None else out_specs,
        scratch_shapes=scratch,
        input_output_aliases={} if aliases is None else aliases,
        compiler_params=pltpu.CompilerParams(vmem_limit_bytes=limit * MIB),
        cost_estimate=pl.CostEstimate(flops=flops, bytes_accessed=size, transcendentals=0),
        name=getattr(body, "func", body).__name__,
    )(*operands)


def far(arrays):
    return [pltpu.with_memory_space_constraint(array, pltpu.HBM) for array in arrays]


def turned(values, width):
    rows = values.shape[0]
    wide = values.astype(jnp.float32)
    column = lax.rem(lax.broadcasted_iota(jnp.int32, values.shape, 0), width)
    before = jnp.where(column == 0, 0.0, pltpu.roll(wide, 1, 0))
    after = jnp.where(column == width - 1, 0.0, pltpu.roll(wide, rows - 1, 0))
    return before.astype(jnp.bfloat16), values, after.astype(jnp.bfloat16)


def halves_swapped(values, odd):
    half = values.shape[1] // 2
    other = jnp.concatenate([values[:, half:], values[:, :half]], axis=1)
    return jnp.where(odd, other, values)


class Weights:
    def __init__(self, refs, spot, groups):
        self.refs = refs
        self.paired = len(refs) > 1
        self.groups = groups
        self.spot = spot
        self.odd = lax.rem(spot[0], 2) == 1

    def block(self, chunk):
        return lax.bitwise_xor(lax.div(self.spot[0], 2) if self.paired else self.spot[1], chunk)

    def tap(self, chunk, position):
        if not self.paired:
            each = self.refs[0].shape[0] // self.groups
            start = self.block(chunk) * each
            parts = [self.refs[0][start + i, position] for i in range(each)]
            return jnp.concatenate(parts, axis=0)
        parts = [self.refs[chunk][position], self.refs[4 + chunk][position]]
        return jnp.concatenate(parts, axis=0)

    def ordered(self, values):
        return halves_swapped(values, self.odd) if self.paired else values


def conv_body(groups, parts, count, rows, width, spot, *refs):
    pieces = refs[:groups]
    near, far_row = refs[groups : groups + 2]
    weights = Weights(refs[groups + 2 : groups + 2 + parts], spot, groups)
    source, *rest = refs[groups + 2 + parts :]
    earlier, rest = rest[:count], rest[count:]
    first_out, second_out, *sends, frame = rest
    for send, held in zip(sends, earlier):
        send[:, 0] = held[...]
    if earlier:
        sends = [send.at[:, 1] for send in sends]
    span = pieces[0].shape[1]
    for mask in range(groups):
        block = lax.bitwise_xor(spot[1], mask)
        own = pieces[mask][...]
        lanes = slice(mask * span, (mask + 1) * span)
        framed = framed_rows(near[:, lanes], far_row[:, lanes], own, weights.odd)
        for column, values in enumerate(turned(weights.ordered(framed), width)):
            frame[block, column] = values
    total_sum = jnp.zeros(first_out.shape, jnp.float32)
    for chunk in range(groups):
        block = weights.block(chunk)
        for position in range(9):
            start = (position // 3) * width
            window = frame[block, position % 3, start : start + rows * width, :]
            total_sum += jnp.dot(
                window, weights.tap(chunk, position), preferred_element_type=jnp.float32
            )
        if len(sends) == 1:
            sends[0][chunk] = frame[chunk, 1, width : (rows + 1) * width, :]
        else:
            near = lax.bitwise_xor(lax.div(spot[0], 2), chunk)
            center = frame[near, 1, width : (rows + 1) * width, :]
            center = center if weights.paired else halves_swapped(center, weights.odd)
            sends[0][chunk] = center[:, : span // 2]
            sends[1][chunk] = center[:, span // 2 :]
    if second_out.shape[0] == 2:
        first_out[...] = total_sum
        second_out[...] = channel_sums(total_sum)
    else:
        middle = (source[...].astype(jnp.float32) + total_sum) * root_half
        first_out[...] = middle
        second_out[...] = middle.astype(jnp.bfloat16)


def back_body(groups, rows, width, spot, grad, near, far_row, *refs):
    frame, held = refs[-2:]
    outs = refs[-2 - groups : -2]
    weights = Weights(refs[: -2 - groups], spot, groups)
    framed = framed_rows(near[...], far_row[...], grad[...], weights.odd)
    for column, values in enumerate(turned(framed, width)):
        frame[column] = values
    for chunk in range(groups):
        total_sum = jnp.zeros(held.shape[1:], jnp.float32)
        for position in range(9):
            start = (2 - position // 3) * width
            total_sum += lax.dot_general(
                frame[2 - position % 3, start : start + rows * width, :],
                weights.tap(chunk, position),
                (((1,), (1,)), ((), ())),
                preferred_element_type=jnp.float32,
            )
        held[weights.block(chunk)] = weights.ordered(total_sum).astype(jnp.bfloat16)
    for mask in range(groups):
        outs[mask][...] = held[lax.bitwise_xor(spot[1], mask)]


def bf16_like(*shape):
    return jax.ShapeDtypeStruct(shape, jnp.bfloat16)


def far_like(shape):
    return pltpu.HBM(shape.shape, shape.dtype)


def f32_like(*shape):
    return jax.ShapeDtypeStruct(shape, jnp.float32)


def flipped(values, axis, mask):
    count = lax.axis_size(axis)
    return lax.ppermute(values, axis, [(i, i ^ mask) for i in range(count)])


def relayed_block(over_x, over_y):
    odd = lax.rem(lax.axis_index("wide"), 2) == 1
    far_pairs = [(i, i ^ (2 if i % 2 else 4)) for i in range(8)]
    return lax.ppermute(jnp.where(odd, over_y, over_x), "wide", far_pairs)


def over_chips(values):
    over_x, over_y = flipped(values, "wide", 2), flipped(values, "wide", 4)
    return [values, over_x, over_y, relayed_block(over_x, over_y)]


def has_slots():
    return lax.axis_size("wide") == 8


def after(value, *others):
    return lax.optimization_barrier((value, others))[0]


def gathered_blocks(blocks):
    return [lax.all_gather(blocks, "wide")]


def spread_chips(values):
    if has_slots():
        return over_chips(values)
    mask = 2
    while mask < lax.axis_size("wide"):
        values = jnp.concatenate([values, flipped(values, "wide", mask)])
        mask *= 2
    return [values]


def gathered_sums(parts):
    if has_slots():
        return [parts[0]] + [flipped(parts[k], "wide", 2 * k) for k in range(1, 4)]
    values = parts[0]
    mask = lax.axis_size("wide") // 2
    while mask > 1:
        half = values.shape[0] // 2
        values = values[:half] + flipped(values[half:], "wide", mask)
        mask //= 2
    return [values]


def channel_pieces(values):
    count = lax.axis_size("tensor")
    return [values] + [flipped(values, "tensor", mask) for mask in range(1, count)]


def edge_rows(near, far_row):
    count = lax.axis_size("wide")
    beyond = [(i, i + 1) for i in range(1, count - 1, 2)]
    beyond += [(i + 1, i) for i in range(1, count - 1, 2)]
    from_far = lax.ppermute(far_row, "wide", beyond)
    return flipped(after(near, far_row), "wide", 1), from_far


def framed_rows(near, far_row, own, odd):
    top = jnp.where(odd, near, far_row)
    bottom = jnp.where(odd, far_row, near)
    return jnp.concatenate([top, own, bottom], axis=0)


def convolve(spot, pieces, edges, kernel, source, second_shape, earlier, rows, width):
    groups, (area, span) = len(pieces), pieces[0].shape
    count, block = (2, span // 2) if has_slots() else (1, span)
    layers = (2,) if earlier else ()
    sends = [bf16_like(groups, *layers, area, block)] * count
    return local_kernel(
        functools.partial(conv_body, groups, len(kernel), len(earlier), rows, width),
        [f32_like(area, span), second_shape]
        + [far_like(shape) if earlier else shape for shape in sends],
        [spot, *pieces, *edges, *far(kernel), source, *far(earlier)],
        [pltpu.VMEM((groups, 3, (rows + 2) * width, span), jnp.bfloat16)],
        32,
        2 * 9 * area * C * span,
    )


def piece_edges(pieces, width):
    odd = lax.rem(lax.axis_index("wide"), 2) == 1
    last = jnp.concatenate([piece[-width:] for piece in pieces], axis=1)
    first = jnp.concatenate([piece[:width] for piece in pieces], axis=1)
    return edge_rows(jnp.where(odd, first, last), jnp.where(odd, last, first))


def convolve_back(spot, grad, edges, kernel, rows, width):
    groups, (area, span) = lax.axis_size("tensor"), grad.shape
    return local_kernel(
        functools.partial(back_body, groups, rows, width),
        [bf16_like(area, span)] * groups,
        [spot, grad, *edges, *far(kernel)],
        [
            pltpu.VMEM((3, (rows + 2) * width, span), jnp.bfloat16),
            pltpu.VMEM((groups, area, span), jnp.bfloat16),
        ],
        32,
        2 * 9 * area * C * span,
    )


def sent_parts(parts):
    return [parts[0]] + [flipped(parts[mask], "tensor", mask) for mask in range(1, len(parts))]


def kernel_grad_body(width, spot, kept, got, *refs):
    *pairs, grads, out, turned_all = refs
    layer = pl.program_id(0)
    area, span = kept.shape[2:]
    depth = 8 * area
    turned_all[:, :width] = jnp.zeros((3 * span, width), jnp.bfloat16)
    turned_all[:, depth + width :] = jnp.zeros((3 * span, width), jnp.bfloat16)
    pieces = [kept[0, layer], got[0, layer]]
    pieces += [pair[core, layer] for pair in pairs for core in range(2)]
    lane = lax.broadcasted_iota(jnp.int32, (span, width), 1)
    for mask, piece in enumerate(pieces):
        start = pl.multiple_of(lax.bitwise_xor(spot[0], mask) * area, area)
        flat = jnp.transpose(piece.astype(jnp.float32))
        for row in range(area // width):
            center = flat[:, row * width : (row + 1) * width]
            before = jnp.where(lane == 0, 0.0, pltpu.roll(center, 1, 1))
            behind = jnp.where(lane == width - 1, 0.0, pltpu.roll(center, width - 1, 1))
            lanes = pl.ds(start + (row + 1) * width, width)
            for column, values in enumerate((before, center, behind)):
                turned_all[column * span : (column + 1) * span, lanes] = values.astype(jnp.bfloat16)
    for row in range(3):
        product = dot(turned_all[:, row * width : row * width + depth], grads[0])
        for column in range(3):
            out[0, 3 * row + column] = product[column * span : (column + 1) * span, :]


def kernel_grad(spot, pieces, grads, width):
    span = pieces[0].shape[3]
    depth, columns = grads.shape[1:]
    return pl.pallas_call(
        functools.partial(kernel_grad_body, width),
        out_shape=f32_like(2, 9, span, columns),
        grid=(2,),
        in_specs=[in_smem]
        + [in_vmem] * len(pieces)
        + [pl.BlockSpec((1, depth, columns), lambda i: (i, 0, 0))],
        out_specs=pl.BlockSpec((1, 9, span, columns), lambda i: (i, 0, 0, 0)),
        scratch_shapes=[pltpu.VMEM((3 * span, depth + 2 * width), jnp.bfloat16)],
        compiler_params=pltpu.CompilerParams(vmem_limit_bytes=24 * MIB),
        cost_estimate=pl.CostEstimate(
            flops=4 * 9 * depth * span * columns, bytes_accessed=6 * MIB, transcendentals=0
        ),
        name="kernel_grad_body",
    )(spot, *far(pieces), *far([grads]))


def kernel_grad_whole(send, grads, rows, width):
    natural = jnp.moveaxis(send, 0, 1).reshape(1, rows, width, C)
    swapped = lax.all_to_all(natural, "wide", split_axis=3, concat_axis=1, tiled=True)
    framed = jnp.pad(swapped, ((0, 0), (1, 1), (1, 1), (0, 0)))
    low = grads.reshape(1, -1, width, grads.shape[1])
    return jnp.stack(
        [
            jnp.einsum(
                "mrwc,mrwd->cd",
                framed[:, tap // 3 : tap // 3 + low.shape[1], tap % 3 : tap % 3 + width, :],
                low,
                preferred_element_type=jnp.float32,
            )
            for tap in range(9)
        ]
    )


root_half = 1.0 / math.sqrt(2.0)
highest = lax.Precision.HIGHEST


def sinusoid(steps):
    half_width = TEMB // 2
    frequency = jnp.exp(-math.log(10000.0) * jnp.arange(half_width, dtype=jnp.float32) / half_width)
    angles = steps.astype(jnp.float32)[:, None] * frequency[None, :]
    return jnp.concatenate([jnp.cos(angles), jnp.sin(angles)], axis=1)


def chip_parts(values):
    if has_slots():
        return [values] + [flipped(values, "wide", mask) for mask in (2, 4, 6)]
    mask = 2
    while mask < lax.axis_size("wide"):
        values = values + flipped(values, "wide", mask)
        mask *= 2
    return [values]


def part_totals(rows):
    return chip_parts(rows + flipped(rows, "wide", 1))


def sum_of_parts(refs):
    if len(refs) == 1:
        return refs[0][...]
    return (refs[0][...] + refs[1][...]) + (refs[2][...] + refs[3][...])


def total(values, axis, mask=1):
    while mask < lax.axis_size(axis):
        values = values + flipped(values, axis, mask)
        mask *= 2
    return values


def silu_slope(values):
    logistic = lax.logistic(values)
    return logistic * (1.0 + values * (1.0 - logistic))


def channel_sums(values):
    return jnp.concatenate(
        [
            jnp.sum(values, axis=0, keepdims=True),
            jnp.sum(values * values, axis=0, keepdims=True),
        ],
        axis=0,
    )


def group_means(first, second, pixel_count):
    channels = first.shape[1]
    per_group = C // GROUPS
    row = lax.div(lax.broadcasted_iota(jnp.int32, (channels, channels), 0), per_group)
    column = lax.div(lax.broadcasted_iota(jnp.int32, (channels, channels), 1), per_group)
    same = jnp.where(row == column, 1.0, 0.0)
    rows = jnp.concatenate([first, second, jnp.zeros((6, channels), jnp.float32)], axis=0)
    means = jnp.dot(rows, same, precision=highest, preferred_element_type=jnp.float32)
    means = means / (pixel_count * per_group)
    return means[0:1], means[1:2]


def group_scale(first, second, pixel_count):
    center, square = group_means(first, second, pixel_count)
    return center, lax.rsqrt(square - center * center + 1e-05)


def lifted_sums(sums, film, pixel_count):
    slope, shift = 1.0 + film[0:1], film[1:2]
    plain, square = sums[0:1], sums[1:2]
    return (
        slope * plain + pixel_count * shift,
        slope * slope * square + 2.0 * slope * shift * plain + pixel_count * shift * shift,
    )


def silu_low(values):
    return (values * lax.logistic(values)).astype(jnp.bfloat16)


def first_norm_body(pixel_count, spot, pixels, affine, *refs):
    *parts, out, sums = refs
    sums[...] = sum_of_parts(parts)
    center, inverse = group_scale(sums[0:1], sums[1:2], pixel_count)
    scaled = (pixels[...].astype(jnp.float32) - center) * inverse
    out[...] = silu_low(scaled * affine[0:1] + affine[1:2])


def second_norm_body(pixel_count, spot, inner, affine, *refs):
    *parts, out, film, sums = refs
    summed = sum_of_parts(parts)
    film[...], sums[...] = summed[:2], summed[2:]
    center, inverse = group_scale(*lifted_sums(sums[...], film[...], pixel_count), pixel_count)
    lifted = inner[...] * (1.0 + film[0:1]) + film[1:2]
    out[...] = silu_low((lifted - center) * inverse * affine[0:1] + affine[1:2])


def parts_sum(refs):
    summed = refs[0][...].astype(jnp.float32)
    for ref in refs[1:]:
        summed += ref[...].astype(jnp.float32)
    return summed


def stacked_rows(rows):
    return jnp.concatenate([jnp.sum(row, axis=0, keepdims=True) for row in rows], axis=0)


def second_back_body(groups, pixel_count, spot, *refs):
    inner, sums, film, affine, terms, out, rows = refs[groups:]
    center, inverse = group_scale(*lifted_sums(sums[...], film[...], pixel_count), pixel_count)
    own = inner[...]
    scaled = (own * (1.0 + film[0:1]) + film[1:2] - center) * inverse
    back = parts_sum(refs[:groups]) * silu_slope(scaled * affine[0:1] + affine[1:2])
    out[...] = back
    rows[0:3, :] = stacked_rows([back * scaled, back, back * own])
    rows[3:5, :] = terms[...]
    rows[5:8, :] = jnp.zeros((3, own.shape[1]), jnp.float32)


def second_input_body(pixel_count, width, spot, back, inner, sums, film, affine, other, *refs):
    *parts, low, both, near, far_row, film_rows, rows = refs
    rows[...] = sum_of_parts(parts)
    slope, shift, gain = 1.0 + film[0:1], film[1:2], affine[0:1]
    plain_sum, square_sum = sums[0:1], sums[1:2]
    lifted_sum, lifted_square = lifted_sums(sums[...], film[...], pixel_count)
    center, inverse = group_scale(lifted_sum, lifted_square, pixel_count)
    dotted, plain = group_means(gain * rows[0:1], gain * rows[1:2], pixel_count)
    scaled = (inner[...] * slope + shift - center) * inverse
    grad = inverse * (back[...] * gain - plain - scaled * dotted)
    grad_low = (grad * slope).astype(jnp.bfloat16)
    low[...] = grad_low
    both[0] = grad_low
    both[1] = other[...]
    odd = lax.rem(spot[0], 2) == 1
    near[...] = jnp.where(odd, grad_low[:width], grad_low[-width:])
    far_row[...] = jnp.where(odd, grad_low[-width:], grad_low[:width])
    scaled_sum = inverse * (lifted_sum - pixel_count * center)
    scaled_inner = inverse * (slope * square_sum + (shift - center) * plain_sum)
    film_rows[0:1, :] = inverse * (
        gain * rows[2:3] - plain * plain_sum - dotted * scaled_inner
    )
    film_rows[1:2, :] = inverse * (
        gain * rows[1:2] - pixel_count * plain - dotted * scaled_sum
    )


def first_back_body(groups, pixel_count, spot, *refs):
    pixels, sums, affine, out, rows = refs[groups:]
    center, inverse = group_scale(sums[0:1], sums[1:2], pixel_count)
    scaled = (pixels[...].astype(jnp.float32) - center) * inverse
    back = parts_sum(refs[:groups]) * silu_slope(scaled * affine[0:1] + affine[1:2])
    out[...] = back
    rows[...] = stacked_rows([back * scaled, back])


def first_input_body(pixel_count, spot, back, pixels, sums, affine, middle, second, *refs):
    *parts, out, gains, biases = refs
    rows = sum_of_parts(parts)
    gains[...] = jnp.concatenate([rows[0:1], second[0:1]], axis=0)
    biases[...] = jnp.concatenate([rows[1:2], second[1:2]], axis=0)
    gain = affine[0:1]
    center, inverse = group_scale(sums[0:1], sums[1:2], pixel_count)
    dotted, plain = group_means(gain * rows[0:1], gain * rows[1:2], pixel_count)
    scaled = (pixels[...].astype(jnp.float32) - center) * inverse
    out[...] = inverse * (back[...] * gain - plain - scaled * dotted) + middle[...] * root_half


def dot(left, right):
    return jnp.dot(left, right, preferred_element_type=jnp.float32)


def dot_last(left, right):
    return lax.dot_general(
        left, right, (((1,), (1,)), ((), ())), preferred_element_type=jnp.float32
    )


def flat_turn(values):
    return jnp.transpose(values.astype(jnp.float32)).astype(jnp.bfloat16)


def dot_first(left, right):
    return dot(flat_turn(left), right)


def head_choice(values, odd):
    first, second = values[:, :HEAD_DIM], values[:, HEAD_DIM:]
    return jnp.where(odd, second, first), jnp.where(odd, first, second)


def heads_joined(kept, received, odd):
    return jnp.where(
        odd,
        jnp.concatenate([received, kept], axis=1),
        jnp.concatenate([kept, received], axis=1),
    )


def packed_rows(values):
    rows = []
    for _ in range(3):
        rows.append(values.astype(jnp.bfloat16).astype(jnp.float32))
        values = values - rows[-1]
    rows.append(jnp.zeros((10, values.shape[1]), jnp.float32))
    return jnp.concatenate(rows, axis=0).astype(jnp.bfloat16)


def unpacked_rows(packed, area):
    rows = packed[area:, :].astype(jnp.float32)
    return rows[0:1] + rows[2:3] + rows[4:5], rows[1:2] + rows[3:4] + rows[5:6]


def prepare_body(spot, pixels, cotangent, gain, bias, pack, sums):
    area = cotangent.shape[0]
    pack[:area] = cotangent[...].astype(jnp.bfloat16)
    pack[area:] = packed_rows(jnp.concatenate([gain[...], bias[...]], axis=0))
    sums[...] = channel_sums(pixels[...].astype(jnp.float32))


def project_body(groups, spot, *refs):
    pieces, packs = refs[:groups], refs[groups : 2 * groups]
    own, maps, keep_query, keep, send, *rest = refs[2 * groups :]
    cross, normed, scaled, center, inverse = rest
    weights = Weights([maps], spot, groups)
    odd = lax.rem(spot[0], 2) == 1
    area = own.shape[0]
    token_sum = token_square = 0.0
    for piece in pieces:
        values = piece[...].astype(jnp.float32)
        token_sum += jnp.sum(values, axis=1, keepdims=True)
        token_square += jnp.sum(values * values, axis=1, keepdims=True)
    mean = token_sum / C
    scale = lax.rsqrt(token_square / C - mean * mean + 1e-05)
    lows = []
    for mask in range(groups):
        gain, bias = unpacked_rows(packs[mask], area)
        values = (pieces[mask][...].astype(jnp.float32) - mean) * scale
        lows.append((values * gain + bias).astype(jnp.bfloat16))
        normed[lax.bitwise_xor(spot[1], mask)] = lows[-1]
    center[...] = mean
    inverse[...] = scale
    scaled[...] = (own[...] - mean) * scale
    projected = []
    for position in range(4):
        total_sum = 0.0
        for mask in range(groups):
            total_sum += dot(lows[mask], weights.tap(mask, position))
        projected.append(total_sum.astype(jnp.bfloat16))
    cross[...] = projected[3]
    chosen = [head_choice(values, odd) for values in projected[:3]]
    chosen = chosen[1:] + chosen[:1]
    keep_query[...] = chosen[2][0]
    keep[...] = jnp.concatenate([pair[0] for pair in chosen[:2]], axis=1)
    send[...] = jnp.concatenate([pair[1] for pair in chosen], axis=1)


def out_grad_body(groups, spot, *refs):
    packs = refs[:groups]
    maps, keep, send, cross = refs[groups:]
    weights = Weights([maps], spot, groups)
    sums = []
    for position in (4, 5):
        total_sum = 0.0
        for mask in range(groups):
            total_sum += dot(packs[mask][: cross.shape[0]], weights.tap(mask, position))
        sums.append(total_sum.astype(jnp.bfloat16))
    kept, sent = head_choice(sums[0], lax.rem(spot[0], 2) == 1)
    keep[...] = kept
    send[...] = sent
    cross[...] = sums[1]


def text_out_body(spot, film, features, pooled, text, parts, time_grad, text_grad, kv_grad):
    for rows, out in ((features, time_grad), (pooled, text_grad)):
        column = jnp.transpose(jnp.broadcast_to(rows[...].astype(jnp.float32), (8, rows.shape[1])))
        for part in range(2):
            out[:, part, :] = column[:, 0:1] * film[part : part + 1, :]
    summed = leading_sum(parts)
    turned_text = flat_turn(text[...])
    for part in range(2):
        high = summed[part].astype(jnp.bfloat16)
        low = (summed[part] - high.astype(jnp.float32)).astype(jnp.bfloat16)
        kv_grad[part] = dot(turned_text, high) + dot(turned_text, low)


def mix_body(groups, spot, kept, other, crossed, maps, *outs):
    weights = Weights([maps], spot, groups)
    attended = heads_joined(kept[...], other[:, :HEAD_DIM], lax.rem(spot[0], 2) == 1)
    for mask in range(groups):
        total_sum = dot_last(attended, weights.tap(mask, 4))
        total_sum += dot_last(crossed[...], weights.tap(mask, 5))
        outs[mask][...] = total_sum.astype(jnp.bfloat16)


def over_rows(refs, step, state):
    for index, ref in enumerate(refs):
        rows = ref.shape[0]
        if rows <= 512:
            state = step(state, ref[...], index, 0)
        else:
            state = lax.fori_loop(
                0,
                rows // 512,
                lambda i, held: step(
                    held, ref[pl.ds(pl.multiple_of(i * 512, 512), 512), :], index, i * 512
                ),
                state,
            )
    return state


score_scale = HEAD_DIM ** (-0.5)


def cross_body(spot, query, grad, parts, *refs):
    *blocks, crossed, grad_query, text_grad = refs
    if blocks:
        kept_block, got_block, *pairs = blocks
        for index, pair in enumerate(pairs):
            pair[0] = kept_block[index + 1]
            pair[1] = got_block[index + 1]
    text = leading_sum(parts).astype(jnp.bfloat16)
    live = lax.broadcasted_iota(jnp.int32, (query.shape[0], text.shape[1]), 1) < spot[2]
    for head in range(query.shape[1] // HEAD_DIM):
        lanes = slice(head * HEAD_DIM, (head + 1) * HEAD_DIM)
        own, keys, values, back = query[:, lanes], text[0, :, lanes], text[1, :, lanes], grad[:, lanes]
        scores = jnp.where(live, dot_last(own, keys) * score_scale, -1e30)
        weights = jnp.exp(scores - jnp.max(scores, axis=1, keepdims=True))
        probs = weights / jnp.sum(weights, axis=1, keepdims=True)
        low = probs.astype(jnp.bfloat16)
        crossed[:, lanes] = dot(low, values).astype(jnp.bfloat16)
        grad_probs = dot_last(back, values)
        grad_scores = probs * (grad_probs - jnp.sum(probs * grad_probs, axis=1, keepdims=True))
        grad_low = grad_scores.astype(jnp.bfloat16)
        grad_query[:, lanes] = (dot(grad_low, keys) * score_scale).astype(jnp.bfloat16)
        text_grad[0, :, lanes] = (dot_first(grad_low, own) * score_scale).astype(jnp.bfloat16)
        text_grad[1, :, lanes] = dot_first(low, back).astype(jnp.bfloat16)


def attend_body(count, extra, halves, spot, kept_query, got, kept_grad, got_grad, *refs):
    blocks, refs = refs[:count], refs[count:]
    cross_in, refs = refs[: 3 + extra], refs[3 + extra :]
    parts, refs = refs[: count * halves], refs[count * halves :]
    keep_out, keep_query, send, *cross_out = refs
    cross_body(spot, *cross_in, *cross_out)
    query = jnp.concatenate([kept_query[...], got[:, 2 * HEAD_DIM :]], axis=0)
    grad = jnp.concatenate([kept_grad[...], got_grad[...]], axis=0)
    queries = query.shape[0]

    def forward(state, block, index, start):
        top, weight_sum, weighted = state
        scores = dot_last(block[:, :HEAD_DIM], query) * score_scale
        raised = jnp.maximum(top, jnp.max(scores, axis=0, keepdims=True))
        rescale = jnp.exp(top - raised)
        weights = jnp.exp(scores - raised)
        weight_sum = weight_sum * rescale + jnp.sum(weights, axis=0, keepdims=True)
        values = block[:, HEAD_DIM : 2 * HEAD_DIM]
        weighted = weighted * rescale + dot_first(values, weights.astype(jnp.bfloat16))
        return raised, weight_sum, weighted

    top, weight_sum, weighted = over_rows(
        blocks,
        forward,
        (
            jnp.full((1, queries), -1e30, jnp.float32),
            jnp.zeros((1, queries), jnp.float32),
            jnp.zeros((HEAD_DIM, queries), jnp.float32),
        ),
    )
    attended = weighted / weight_sum
    delta = jnp.sum(attended * jnp.transpose(grad.astype(jnp.float32)), axis=0, keepdims=True)
    log_sum = top + jnp.log(weight_sum)

    def backward(state, block, index, start):
        keys, values = block[:, :HEAD_DIM], block[:, HEAD_DIM : 2 * HEAD_DIM]
        probs = jnp.exp(dot_last(keys, query) * score_scale - log_sum)
        grad_values = dot(probs.astype(jnp.bfloat16), grad)
        grad_scores = (probs * (dot_last(values, grad) - delta)).astype(jnp.bfloat16)
        grad_keys = dot(grad_scores, query) * score_scale
        both = jnp.concatenate([grad_keys, grad_values], axis=1).astype(jnp.bfloat16)
        rows = block.shape[0] // halves
        first = start if isinstance(start, int) else pl.multiple_of(start, 512)
        for half in range(halves):
            parts[halves * index + half][pl.ds(first, rows), :] = both[half * rows : (half + 1) * rows]
        return state + dot_first(keys, grad_scores)

    flat = over_rows(blocks, backward, jnp.zeros((HEAD_DIM, queries), jnp.float32))
    for index, (values, keep) in enumerate(((attended, keep_out), (flat * score_scale, keep_query))):
        turned_back = jnp.transpose(values).astype(jnp.bfloat16)
        keep[...] = turned_back[: queries // 2]
        send[:, index * HEAD_DIM : (index + 1) * HEAD_DIM] = turned_back[queries // 2 :]


def leading_sum(ref):
    summed = ref[0].astype(jnp.float32)
    for index in range(1, ref.shape[0]):
        summed += ref[index].astype(jnp.float32)
    return summed


def joined_grads(spot, kept_query, got, cross, kept_pairs, got_pairs):
    odd = lax.rem(spot[0], 2) == 1
    own, other = [parts_sum(pairs).astype(jnp.bfloat16) for pairs in (kept_pairs, got_pairs)]
    return [
        heads_joined(kept_query[...], got[:, HEAD_DIM:], odd),
        heads_joined(own[:, :HEAD_DIM], other[:, :HEAD_DIM], odd),
        heads_joined(own[:, HEAD_DIM:], other[:, HEAD_DIM:], odd),
        cross[...],
    ]


def project_back_body(groups, count, spot, kq, got, cross, center, inverse, kept, *refs):
    crossed, normed, maps, *refs = refs
    kept_pairs, got_pairs, refs = refs[:count], refs[count : 2 * count], refs[2 * count :]
    pieces, packs = refs[:groups], refs[groups : 2 * groups]
    *outs, out, frame = refs[2 * groups :]
    odd = lax.rem(spot[0], 2) == 1
    weights = Weights([maps], spot, groups)
    grads = joined_grads(spot, kq, got, cross, kept_pairs, got_pairs)
    area, span = cross.shape
    plain = dotted = 0.0
    for mask in range(groups):
        part = 0.0
        for position in range(4):
            part += dot_last(grads[position], weights.tap(mask, position))
        outs[mask][:area] = part.astype(jnp.bfloat16)
        eased = part * unpacked_rows(packs[mask], area)[0]
        unit = (pieces[mask][...].astype(jnp.float32) - center[...]) * inverse[...]
        plain += eased
        dotted += eased * unit
    ones = jnp.ones((8, plain.shape[1]), jnp.float32)
    sums = [
        lax.dot_general(
            ones,
            values,
            (((1,), (1,)), ((), ())),
            precision=highest,
            preferred_element_type=jnp.float32,
        )[0:1]
        for values in (plain, dotted)
    ]
    packed = packed_rows(jnp.concatenate(sums, axis=0))
    for part in outs:
        part[area:] = packed
    right = jnp.concatenate(grads, axis=1)
    attended = heads_joined(kept[...], got[:, :HEAD_DIM], odd)
    out_right = jnp.concatenate([attended, crossed[...]], axis=1)
    for mask in range(groups):
        frame[lax.bitwise_xor(spot[1], mask)] = packs[mask][:area]
    for chunk in range(groups):
        rows = slice(chunk * span, (chunk + 1) * span)
        out[rows, : 4 * span] = dot_first(normed[chunk], right).astype(jnp.bfloat16)
        out[rows, 4 * span :] = dot_first(frame[chunk], out_right).astype(jnp.bfloat16)


def weight_out_body(spot, sums, in_grad, self_grad, cross_grad):
    summed = sums[...].astype(jnp.float32)
    span = in_grad.shape[2]
    for position in range(4):
        in_grad[position] = summed[:, position * span : (position + 1) * span]
    self_grad[...] = jnp.transpose(summed[:, 4 * span : 5 * span])
    cross_grad[...] = jnp.transpose(summed[:, 5 * span :])


def norm_back_body(groups, width, spot, *refs):
    scaled, inverse, cotangent, gain, middle, low, near, far_row, terms = refs[groups:]
    area = scaled.shape[0]
    grad = plain = dotted = 0.0
    for ref in refs[:groups]:
        grad += ref[:area].astype(jnp.float32)
        sums = unpacked_rows(ref, area)
        plain, dotted = plain + sums[0], dotted + sums[1]
    same = lax.broadcasted_iota(jnp.int32, (area, area), 0) == lax.broadcasted_iota(
        jnp.int32, (area, area), 1
    )
    plain = jnp.sum(jnp.where(same, plain, 0.0), axis=1, keepdims=True) / C
    dotted = jnp.sum(jnp.where(same, dotted, 0.0), axis=1, keepdims=True) / C
    unit = scaled[...]
    terms[0:1, :] = jnp.sum(grad * unit, axis=0, keepdims=True)
    terms[1:2, :] = jnp.sum(grad, axis=0, keepdims=True)
    back = inverse[...] * (grad * gain[...] - plain - unit * dotted) + cotangent[...]
    middle[...] = back
    grad_low = (back * root_half).astype(jnp.bfloat16)
    low[...] = grad_low
    odd = lax.rem(spot[0], 2) == 1
    near[...] = jnp.where(odd, grad_low[:width], grad_low[-width:])
    far_row[...] = jnp.where(odd, grad_low[-width:], grad_low[:width])


def shards(
    pixels,
    text_states,
    text_length,
    timestep,
    conv_weights,
    film_time,
    film_text,
    group_gain,
    group_bias,
    layer_gain,
    layer_bias,
    attn_in,
    text_kv,
    out_self,
    out_cross,
    cotangent,
):
    map_count, row_count, col_count, width_own = pixels.shape
    token_count = row_count * col_count
    groups = lax.axis_size("tensor")
    pixel_count = token_count * lax.axis_size("wide")
    own_shape = (map_count, row_count, col_count, width_own)
    flat = (token_count, width_own)
    half = (token_count, HEAD_DIM)
    square = 2 * token_count * C * width_own
    edge = (col_count, width_own)
    spot = jnp.stack([lax.axis_index("wide"), lax.axis_index("tensor"), text_length[0]])
    spot = spot.astype(jnp.int32)
    own_pixels = pixels.reshape(flat)
    flat_cotangent = cotangent.reshape(flat)
    affine = [jnp.stack([group_gain[layer], group_bias[layer]]) for layer in range(2)]

    pack, sums = local_kernel(
        prepare_body,
        [bf16_like(token_count + 16, width_own), f32_like(2, width_own)],
        [spot, *far([own_pixels, flat_cotangent, layer_gain[None], layer_bias[None]])],
        [],
        8,
        0,
    )
    first_parts = part_totals(sums)
    kernel_one = gathered_blocks(conv_weights[0])
    features = sinusoid(timestep).astype(jnp.bfloat16)
    present = jnp.arange(TEXT)[None, :] < text_length[:, None]
    pooled = jnp.einsum(
        "mtx,mt->mx", text_states, present.astype(jnp.bfloat16), preferred_element_type=jnp.float32
    )
    pooled = (pooled / text_length.astype(jnp.float32)[:, None]).astype(jnp.bfloat16)
    wide_index = lax.axis_index("wide")
    time_rows = film_time.shape[0]
    text_rows = film_text.shape[0]
    own_features = lax.dynamic_slice_in_dim(features, wide_index * time_rows, time_rows, 1)
    own_pooled = lax.dynamic_slice_in_dim(pooled, wide_index * text_rows, text_rows, 1)
    own_text = lax.dynamic_slice_in_dim(text_states, wide_index * text_rows, text_rows, 2)
    film_term = jnp.einsum(
        "mk,ksc->msc", own_features, film_time, preferred_element_type=jnp.float32
    ) + jnp.einsum("mk,ksc->msc", own_pooled, film_text, preferred_element_type=jnp.float32)
    text_term = jnp.einsum("mtx,pxd->pmtd", own_text, text_kv, preferred_element_type=jnp.float32)
    text_term = text_term.astype(jnp.bfloat16).reshape(2, TEXT, width_own)

    row_pair = f32_like(2, width_own)
    first, first_sums = local_kernel(
        functools.partial(first_norm_body, pixel_count),
        [bf16_like(*flat), row_pair],
        [spot, own_pixels, affine[0], *first_parts],
        [],
        8,
        0,
    )
    maps = jnp.concatenate(
        [after(attn_in, first), jnp.transpose(after(jnp.stack([out_self, out_cross]), first), (0, 2, 1))], axis=0
    )
    maps = gathered_blocks(maps)[0]
    packs = channel_pieces(pack)
    pieces = channel_pieces(after(first, packs))
    edges = piece_edges(pieces, col_count)
    later = after(conv_weights, first)[1]
    if has_slots():
        kernel_two = over_chips(later)
        last = after(kernel_two[3], *edges)
        kernel_two += [flipped(part, "wide", 1) for part in [*kernel_two[:3], last]]
    else:
        kernel_two = gathered_blocks(later)
    pieces[0] = after(pieces[0], film_term, text_term)
    inner, sums, *first_sends = convolve(
        spot, pieces, edges, kernel_one, own_pixels, row_pair, [], row_count, col_count
    )
    sums = after(sums, kernel_two)
    inner_parts = part_totals(jnp.concatenate([film_term[0], sums]))
    second, film, inner_sums = local_kernel(
        functools.partial(second_norm_body, pixel_count),
        [bf16_like(*flat), row_pair, row_pair],
        [spot, inner, affine[1], *inner_parts],
        [],
        8,
        0,
    )
    text_all = lax.all_gather(after(text_term, second), "wide")
    pieces = channel_pieces(second)
    edges = piece_edges(pieces, col_count)
    middle, middle_low, *both_sends = convolve(
        spot,
        pieces,
        edges,
        kernel_two,
        own_pixels,
        bf16_like(*flat),
        first_sends,
        row_count,
        col_count,
    )

    middle_pieces = channel_pieces(middle_low)
    block_pair = [both_sends[0], flipped(both_sends[1], "wide", 1)] if has_slots() else []
    kept_grad, sent_grad, grad_crossed = local_kernel(
        functools.partial(out_grad_body, groups),
        [far_like(bf16_like(*half)), bf16_like(*half), far_like(bf16_like(*flat))],
        [spot, *far([after(packs[0], middle_low)] + packs[1:]), *far([maps])],
        [],
        16,
        2 * square,
    )
    got_grad = flipped(sent_grad, "wide", 1)
    middle_pieces[0] = after(middle_pieces[0], got_grad, block_pair)
    column = f32_like(token_count, 1)
    triple = bf16_like(token_count, 3 * HEAD_DIM)
    kept_query, kept_pair, sent, *outs = local_kernel(
        functools.partial(project_body, groups),
        [
            bf16_like(*half),
            bf16_like(*flat),
            triple,
            bf16_like(*flat),
            far_like(bf16_like(groups, *flat)),
            far_like(f32_like(*flat)),
            far_like(column),
            far_like(column),
        ],
        [spot, *middle_pieces, *far(packs), middle, *far([maps])],
        [],
        24,
        4 * square,
    )
    cross_query, normed, scaled, center, inverse = outs
    got = flipped(sent, "wide", 1)
    blocks = spread_chips(jnp.concatenate([kept_pair, got[:, : 2 * HEAD_DIM]]))
    pair_shapes = [bf16_like(2, *block.shape[1:]) for block in block_pair[:1] * 3]
    halves = 2 if has_slots() else 1
    attend_shapes = [bf16_like(block.shape[0] // halves, 2 * HEAD_DIM) for block in blocks * halves]
    attend_shapes += [bf16_like(*half), bf16_like(*half), bf16_like(*flat)]
    cross_shapes = [bf16_like(*flat), bf16_like(*flat), bf16_like(2, TEXT, width_own)]
    outs = local_kernel(
        functools.partial(attend_body, len(blocks), len(block_pair), halves),
        [far_like(shape) for shape in attend_shapes + pair_shapes + cross_shapes],
        [
            spot,
            kept_query,
            got,
            *far([kept_grad, got_grad]),
            *blocks,
            cross_query,
            *far([grad_crossed, text_all]),
            *far(block_pair),
        ],
        [],
        48,
        14 * (2 * token_count) * HEAD_DIM * pixel_count,
    )
    key_parts, outs = outs[: len(blocks) * halves], outs[len(blocks) * halves :]
    kept_out, kept_dq, sent_both, *block_pairs = outs
    *block_pairs, crossed, grad_cross_query, text_grads = block_pairs
    text_sums = lax.all_gather(text_grads, "wide")
    if has_slots():
        key_parts = [key_parts[0]] + [flipped(key_parts[mask], "wide", mask) for mask in range(1, 8)]
        kept_pairs, got_pairs = key_parts[0::2], key_parts[1::2]
        kept_pairs[0] = far(kept_pairs[:1])[0]
    else:
        (summed,) = gathered_sums(key_parts)
        kept_pairs = [summed[:token_count]]
        got_pairs = [flipped(summed[token_count:], "wide", 1)]
    got_both = flipped(sent_both, "wide", 1)
    *norm_parts, weight_parts = local_kernel(
        functools.partial(project_back_body, groups, len(kept_pairs)),
        [bf16_like(token_count + 16, width_own)] * groups + [far_like(bf16_like(C, 6 * width_own))],
        [
            spot,
            *far([kept_dq]),
            got_both,
            *far([grad_cross_query, center, inverse, kept_out, crossed, normed, maps]),
            *kept_pairs,
            *got_pairs,
            *far(middle_pieces),
            *far(packs),
        ],
        [pltpu.VMEM((groups, *flat), jnp.bfloat16)],
        32,
        10 * square,
    )
    weight_sums = lax.psum_scatter(weight_parts, "wide", scatter_dimension=0, tiled=True)
    received = sent_parts(norm_parts)
    if has_slots():
        close = [flipped(after(block_pairs[k], norm_parts[0]), "wide", 2 * k + 2) for k in range(2)]
        received[0] = after(received[0], close)
    grad_middle, grad_two, last, head, terms = local_kernel(
        functools.partial(norm_back_body, groups, col_count),
        [
            f32_like(*flat),
            bf16_like(*flat),
            bf16_like(*edge),
            bf16_like(*edge),
            f32_like(2, width_own),
        ],
        [
            spot,
            *received,
            scaled,
            inverse,
            flat_cotangent,
            layer_gain[None],
        ],
        [],
        16,
        0,
    )

    edges = edge_rows(last, head)
    mixed = local_kernel(
        functools.partial(mix_body, groups),
        [bf16_like(*flat)] * groups,
        [spot, after(kept_out, grad_two), got_both, *far([crossed, maps])],
        [],
        16,
        2 * square,
    )
    back_parts = convolve_back(
        spot, after(grad_two, mixed), edges, kernel_two, row_count, col_count
    )
    mixed = sent_parts([after(part, back_parts[0]) for part in mixed])
    result = middle
    for part in mixed:
        result = result + part.astype(jnp.float32)
    back_parts = sent_parts(back_parts)
    back, rows = local_kernel(
        functools.partial(second_back_body, groups, pixel_count),
        [f32_like(*flat), f32_like(8, width_own)],
        [spot, *back_parts, inner, inner_sums, film, affine[1], terms],
        [],
        16,
        0,
    )
    grad_one, both_low, last, head, film_rows, second_rows = local_kernel(
        functools.partial(second_input_body, pixel_count, col_count),
        [
            bf16_like(*flat),
            far_like(bf16_like(2, *flat)),
            bf16_like(*edge), bf16_like(*edge), row_pair, f32_like(8, width_own)],
        [spot, after(back, mixed), inner, inner_sums, film, affine[1], *far([grad_two]), *part_totals(rows)],
        [],
        16,
        0,
    )
    edges = edge_rows(last, head)
    both_grads = lax.all_gather(both_low, "wide", axis=1, tiled=True)
    back_parts = convolve_back(spot, grad_one, edges, kernel_one, row_count, col_count)
    if has_slots():
        block_pair += [*close, flipped(after(block_pairs[2], back_parts[0]), "wide", 6)]
    attn_in_grad, self_grad, cross_grad = local_kernel(
        weight_out_body,
        [f32_like(4, C // lax.axis_size("wide"), width_own)]
        + [f32_like(width_own, C // lax.axis_size("wide"))] * 2,
        [spot, *far([after(weight_sums, back_parts[0])])],
        [],
        16,
        0,
    )
    back_parts = sent_parts(back_parts)
    film_rows = after(film_rows, back_parts[1])
    time_grad, text_grad, kv_grad = local_kernel(
        text_out_body,
        [
            f32_like(time_rows, 2, width_own),
            f32_like(text_rows, 2, width_own),
            f32_like(2, text_rows, width_own),
        ],
        [spot, film_rows, own_features, own_pooled, own_text[0], *far([text_sums])],
        [],
        24,
        4 * TEXT * text_rows * width_own,
    )
    back_parts[0], attn_in_grad, time_grad = lax.optimization_barrier(
        (back_parts[0], attn_in_grad, time_grad)
    )
    back, rows = local_kernel(
        functools.partial(first_back_body, groups, pixel_count),
        [f32_like(*flat), f32_like(2, width_own)],
        [spot, *back_parts, own_pixels, first_sums, affine[0]],
        [],
        16,
        0,
    )
    row_parts = part_totals(rows)
    if has_slots():
        conv_grad = kernel_grad(spot, block_pair, both_grads, col_count)
    else:
        conv_grad = jnp.stack(
            [
                kernel_grad_whole(both_sends[0][:, k], both_grads[k], row_count, col_count)
                for k in range(2)
            ]
        )
    pixels_grad, gain_grad, bias_grad = local_kernel(
        functools.partial(first_input_body, pixel_count),
        [f32_like(*flat), row_pair, row_pair],
        [spot, back, own_pixels, first_sums, affine[0], grad_middle, second_rows, *row_parts],
        [],
        16,
        0,
    )
    return (
        result.reshape(own_shape),
        pixels_grad.reshape(own_shape),
        conv_grad,
        time_grad,
        text_grad,
        gain_grad,
        bias_grad,
        second_rows[3],
        second_rows[4],
        attn_in_grad,
        kv_grad,
        self_grad,
        cross_grad,
    )


def solution(mesh):
    placed = (
        P(None, "wide", None, "tensor"),
        P(),
        P(),
        P(),
        P(None, None, "wide", "tensor"),
        P("wide", None, "tensor"),
        P("wide", None, "tensor"),
        P(None, "tensor"),
        P(None, "tensor"),
        P("tensor"),
        P("tensor"),
        P(None, "wide", "tensor"),
        P(None, "wide", "tensor"),
        P("tensor", "wide"),
        P("tensor", "wide"),
        P(None, "wide", None, "tensor"),
    )
    return jax.shard_map(
        shards,
        mesh=mesh,
        in_specs=placed,
        out_specs=(
            P(None, "wide", None, "tensor"),
            P(None, "wide", None, "tensor"),
            P(None, None, "wide", "tensor"),
            P("wide", None, "tensor"),
            P("wide", None, "tensor"),
            P(None, "tensor"),
            P(None, "tensor"),
            P("tensor"),
            P("tensor"),
            P(None, "wide", "tensor"),
            P(None, "wide", "tensor"),
            P("tensor", "wide"),
            P("tensor", "wide"),
        ),
        check_vma=False,
    )
```
